512 devices in a mesh: gx: 8 (over y, z_hi), gy: 8 (over z_lo), gz: 8 (over x, core).
Axes of the slice: x: 4, y: 4, z: 16 (z_hi: 2, z_lo: 8; z = z_hi * 8 + z_lo), core: 2. Of those that a mesh axis runs over, the one named last changes fastest.
Arguments:
- right_side: float32 [4, 64, 64, 1024], P(None, 'gx', 'gy', 'gz'), may hold values from -5 to 5.2
- affinity: float32 [3, 64, 64, 1024], P(None, 'gx', 'gy', 'gz'), may hold values from 0.05 to 1
Outputs:
- correction: float32 [4, 64, 64, 1024], P(None, 'gx', 'gy', 'gz')
The draws below stay inside these ranges and needn't reach their ends.
All inputs are finite; a program needn't handle non-finite values.
Results may differ from the reference program's by a relative error of at most 0.0001.
Values sent between devices are 32-bit elements; how exact they have to be, the bound alone decides.
A program may use at most 128 MiB of HBM per device.

```python
import jax
import jax.numpy as jnp
from jax import lax

VECS = 4
DEGREE = 3
COARSE_DEGREE = 8
NX = 64
NY = 64
NZ = 1024


def draw_right_side(key, part):
    key = jax.random.fold_in(key, 7)
    noise_key = jax.random.fold_in(key, 1)
    base = jnp.clip(jax.random.normal(noise_key, (VECS, NX, NY, NZ), jnp.float32), -5.0, 5.0)
    return base


def draw_affinity(key, part):
    key = jax.random.fold_in(key, 11)
    unit = jax.random.uniform(key, (3, NX, NY, NZ), jnp.float32, 0.0, 1.0)
    lower = jnp.array([0.05, 0.05, 0.5], jnp.float32).reshape(3, 1, 1, 1)
    upper = jnp.array([0.12, 0.12, 1.0], jnp.float32).reshape(3, 1, 1, 1)
    return lower + (upper - lower) * unit


def setup_inputs(seed: int = 0) -> dict:
    key_of = jax.random.split(jax.random.key(seed), 3)
    right_side = draw_right_side(jax.random.fold_in(key_of[2], 71), 0)
    affinity = draw_affinity(jax.random.fold_in(key_of[2], 71), 0)
    return {"right_side": right_side, "affinity": affinity}


SPECTRAL_SHIFT = 0.02
SMOOTH_LOWER = 0.5
SMOOTH_UPPER = 2.0 + SPECTRAL_SHIFT

def zero_rim(values):
    widths = [(0, 0)] * (values.ndim - 3) + [(1, 1)] * 3
    return jnp.pad(values, widths)

def across(padded, axis, offset):
    cells = padded.shape[-3:]
    lead = padded.ndim - 3
    starts = [0] * lead + [1, 1, 1]
    limits = list(padded.shape[:lead]) + [cells[0] - 1, cells[1] - 1, cells[2] - 1]
    starts[lead + axis] = offset
    limits[lead + axis] = cells[axis] - 2 + offset
    return lax.slice(padded, starts, limits)

def make_operator(faces, rim_fn):
    scale = lax.rsqrt(faces[0] + faces[1] + faces[2] + faces[3] + faces[4] + faces[5])

    def apply(values):
        padded = rim_fn(scale * values)
        beside_all = faces[0] * across(padded, 0, 0) + faces[1] * across(padded, 0, 2)
        beside_all = beside_all + faces[2] * across(padded, 1, 0) + faces[3] * across(padded, 1, 2)
        beside_all = beside_all + faces[4] * across(padded, 2, 0) + faces[5] * across(padded, 2, 2)
        return (1.0 + SPECTRAL_SHIFT) * values - scale * beside_all
    return apply

def chebyshev(apply, guess, target, lower_end, upper_end, degree):
    theta = 0.5 * (upper_end + lower_end)
    delta = 0.5 * (upper_end - lower_end)
    sigma = theta / delta
    ratio = 1.0 / sigma
    if guess is None:
        residual = target
    else:
        residual = target - apply(guess)
    update = residual / theta
    result = update if guess is None else guess + update
    for turn in range(degree - 1):
        residual = residual - apply(update)
        ratio_next = 1.0 / (2.0 * sigma - ratio)
        update = ratio_next * ratio * update + 2.0 * ratio_next / delta * residual
        ratio = ratio_next
        result = result + update
    return result

def restrict(values):
    lead = values.shape[:-3]
    cells = values.shape[-3:]
    depth = len(lead)
    grouped = values.reshape(lead + (cells[0] // 2, 2, cells[1] // 2, 2, cells[2] // 2, 2))
    return 0.125 * lax.optimization_barrier(jnp.sum(grouped, axis=(depth + 1, depth + 3, depth + 5)))

def prolong(values):
    lead = values.shape[:-3]
    cells = values.shape[-3:]
    expanded = values.reshape(lead + (cells[0], 1, cells[1], 1, cells[2], 1))
    expanded = jnp.broadcast_to(expanded, lead + (cells[0], 2, cells[1], 2, cells[2], 2))
    return expanded.reshape(lead + (2 * cells[0], 2 * cells[1], 2 * cells[2]))

def coarsen_faces(faces):
    cells = faces.shape[1:]
    halves = [cells[0] // 2, cells[1] // 2, cells[2] // 2]
    pieces = []
    for index in range(6):
        axis = index // 2
        picked = lax.slice_in_dim(faces[index], index % 2, cells[axis], stride=2, axis=axis)
        shape = [halves[0], 2, halves[1], 2, halves[2], 2]
        shape[2 * axis + 1] = 1
        pieces.append(0.25 * lax.optimization_barrier(jnp.sum(picked.reshape(shape), axis=(1, 3, 5))))
    return jnp.stack(pieces)

def fine_faces(affinity):
    padded = zero_rim(affinity)
    cells = affinity.shape[1:]
    pieces = []
    for axis in range(3):
        channel = affinity[axis]
        position = lax.broadcasted_iota(jnp.int32, cells, axis)
        below = across(padded[axis], axis, 0)
        above = across(padded[axis], axis, 2)
        pieces.append(jnp.where(position > 0, 0.5 * (below + channel), 0.0))
        pieces.append(jnp.where(position < cells[axis] - 1, 0.5 * (above + channel), 0.0))
    return jnp.stack(pieces)

def reference(right_side, affinity):
    faces = [fine_faces(affinity)]
    for level in range(4):
        faces.append(coarsen_faces(faces[-1]))
    operators = [make_operator(entry, zero_rim) for entry in faces]

    def cycle(target, level):
        apply = operators[level]
        if level == 4:
            return chebyshev(apply, None, target, SPECTRAL_SHIFT, SMOOTH_UPPER, COARSE_DEGREE)
        result = chebyshev(apply, None, target, SMOOTH_LOWER, SMOOTH_UPPER, DEGREE)
        coarse_target = restrict(target - apply(result))
        result = result + prolong(cycle(coarse_target, level + 1))
        return chebyshev(apply, result, target, SMOOTH_LOWER, SMOOTH_UPPER, DEGREE)

    def single(target):
        return cycle(target, 0)
    return lax.map(single, right_side)
```

```python
import functools

import jax
import jax.numpy as jnp
from jax import lax
from jax.experimental import pallas as pl
from jax.experimental.pallas import tpu as pltpu
from jax.sharding import PartitionSpec as P

MESH = pl.DeviceIdType.MESH
HIGHEST = lax.Precision.HIGHEST
F32 = jnp.float32

DEGREE = 3
COARSE_DEGREE = 8
SHIFT = 0.02
SMOOTH_LOWER = 0.5
UPPER = 2.0 + SHIFT


def cheb_coefs(a, b, m):
    theta, delta = 0.5 * (b + a), 0.5 * (b - a)
    sigma = theta / delta
    rho = 1.0 / sigma
    steps = []
    for _ in range(m - 1):
        nxt = 1.0 / (2.0 * sigma - rho)
        steps.append((nxt * rho, 2.0 * nxt / delta))
        rho = nxt
    return 1.0 / theta, steps


SMOOTH = cheb_coefs(SMOOTH_LOWER, UPPER, DEGREE)
SOLVE = cheb_coefs(SHIFT, UPPER, COARSE_DEGREE)


def iota(dim, shape=(1, 8, 128)):
    return lax.broadcasted_iota(jnp.int32, shape, dim)


def roll(x, shift, axis):
    shift = shift % x.shape[axis]
    return x if shift == 0 else pltpu.roll(x, shift, axis)


def both(x, k, axis):
    bit = (iota(axis, (1,) + x.shape[1:]) // k) % 2
    return x + jnp.where(bit == 0, roll(x, -k, axis), roll(x, k, axis))


def pick(x, k, axis, upper):
    bit = (iota(axis, (1,) + x.shape[1:]) // k) % 2
    if upper:
        return jnp.where(bit == 1, x, roll(x, -k, axis))
    return jnp.where(bit == 0, x, roll(x, k, axis))


def slots(ref, start, count, rows=16):
    if not isinstance(start, int):
        start = pl.multiple_of(start * rows, rows)
    else:
        start = start * rows
    return ref[pl.ds(start, count * rows), :].reshape(count, rows, 128)


def put(ref, start, value):
    count, rows = value.shape[:2]
    if not isinstance(start, int):
        start = pl.multiple_of(start * rows, rows)
    else:
        start = start * rows
    ref[pl.ds(start, count * rows), :] = value.reshape(count * rows, 128)


def loop(count, body):
    def run(i, carry):
        body(i)
        return carry

    lax.fori_loop(0, count, run, 0)


class Level:
    def __init__(self, z, rows, sy, sx, mode, refs):
        self.z, self.rows, self.sy, self.sx, self.mode = z, rows, sy, sx, mode
        self.ch = 128 // rows
        self.turns = z // self.ch
        (self.coef, self.scale, self.f, self.r, self.d, self.x, self.wa, self.wb, self.up, self.low) = refs

    def get(self, ref, i, offset=0):
        return slots(ref, i * self.ch + offset, self.ch, self.rows)

    def put(self, ref, i, value, offset=0):
        put(ref, i * self.ch + offset, value)


LEVELS = ((72, 16, 1, 1, 0), (72, 16, 1, 1, 0), (48, 16, 1, 2, 0), (32, 8, 1, 4, 1), (32, 8, 2, 8, 2))


def level_shapes(z, rows):
    n = z * rows
    pad = (z + 2) * rows
    return [pltpu.VMEM((6 * n, 128), F32)] + [pltpu.VMEM((n, 128), F32)] * 5 + [pltpu.VMEM((pad, 128), F32)] * 2 + [
        pltpu.VMEM((n, 128), F32)] * 2


def neighbours(lv, w_ref, i):
    w, before, after = lv.get(w_ref, i, 1), lv.get(w_ref, i, 0), lv.get(w_ref, i, 2)
    xd, xu = roll(w, lv.sx, 2), roll(w, -lv.sx, 2)
    yd, yu = roll(w, lv.sy, 1), roll(w, -lv.sy, 1)
    if lv.mode == 0:
        zd, zu = before, after
    else:
        s = lv.mode
        t = iota(2) % 4
        zu = jnp.where(t < 4 - s, roll(w, -s, 2), roll(after, 4 - s, 2))
        zd = jnp.where(t >= s, roll(w, s, 2), roll(before, s - 4, 2))
    return w, xd, xu, yd, yu, zd, zu


def apply_at(lv, w_ref, i):
    _, *near = neighbours(lv, w_ref, i)
    total = None
    for k, value in enumerate(near):
        term = slots(lv.coef, k * lv.z + i * lv.ch, lv.ch, lv.rows) * value
        total = term if total is None else total + term
    return total


def init_down(lv, over_theta):
    def body(i):
        f = lv.get(lv.f, i)
        d = f * over_theta
        lv.put(lv.r, i, f)
        lv.put(lv.d, i, d)
        lv.put(lv.x, i, d)
        lv.put(lv.wa, i, lv.get(lv.scale, i) * d, 1)

    loop(lv.turns, body)


def init_up(lv, coarse_at):
    def body(i):
        d = coarse_at(i)
        lv.put(lv.d, i, d)
        lv.put(lv.x, i, lv.get(lv.x, i) + d)
        lv.put(lv.wa, i, lv.get(lv.scale, i) * d, 1)

    loop(lv.turns, body)


def step(lv, w_ref, w_next, alpha=None, beta=None, last=False):
    def body(i):
        d = lv.get(lv.d, i)
        r = lv.get(lv.r, i) - ((1.0 + SHIFT) * d - apply_at(lv, w_ref, i))
        if not last:
            lv.put(lv.r, i, r)
        if beta is None:
            return
        d = beta * r if alpha is None else alpha * d + beta * r
        lv.put(lv.x, i, lv.get(lv.x, i) + d)
        if not last:
            lv.put(lv.d, i, d)
            lv.put(w_next, i, lv.get(lv.scale, i) * d, 1)

    loop(lv.turns, body)


def make_coefs(lv, group):
    g = (iota(2, (1, lv.rows, 128)) // group) % 4

    def spread(value, k):
        out = value
        for to in range(4):
            if to != k:
                out = jnp.where(g == to, roll(value, group * (to - k), 2), out)
        return out

    def body(i):
        low, up = lv.get(lv.low, i), lv.get(lv.up, i)
        faces = []
        for k in range(3):
            faces += [spread(low, k), spread(up, k)]
        total = faces[0] + faces[1] + faces[2] + faces[3] + faces[4] + faces[5]
        scale = jnp.where(total > 0.0, lax.rsqrt(total), 0.0)
        lv.put(lv.scale, i, scale)
        for k in range(6):
            put(lv.coef, k * lv.z + i * lv.ch, scale * faces[k])

    loop(lv.turns, body)


def own_pairs(ref, i):
    v = slots(ref, 4 + 32 * i, 32)[:, :8].reshape(16, 2, 8, 128)
    return v[:, 0], v[:, 1]


def coarse_faces(first, second, group, upper, ky, kx):
    g = (iota(2) // group) % 4
    v = jnp.where(g == 2, second if upper else first, first + second)
    v = jnp.where(g == 1, pick(v, ky, 1, upper), both(v, ky, 1))
    if kx is not None:
        v = jnp.where(g == 0, pick(v, kx, 2, upper), both(v, kx, 2))
    return v


def kernel(nx, ny, nz, f_hbm, a_hbm, out_ref, *scratch):
    refs = list(scratch)

    def take(count):
        got = refs[:count]
        del refs[:count]
        return got

    levels = [Level(*shape, take(10)) for shape in LEVELS]
    (fext, aext, ys, yr, zs, zr, tb, tmp, xg1, xgf, rxs, rxr, pz1, pzf, yg1, ygf, eb2, eb1, eb0) = take(19)
    (local_sem, strip_send, strip_recv, ex_send, ex_recv, xg_send, xg_recv, rx_send, rx_recv,
     pz_send, pz_recv, yg_send, yg_recv, zg_send, zg_recv) = take(15)
    l0, l1, l2, l3, l4 = levels

    b, j, k = lax.axis_index("gx"), lax.axis_index("gy"), lax.axis_index("gz")
    sub, lane, lane16 = iota(1), iota(2), iota(2, (1, 16, 128))
    lane2 = lax.broadcasted_iota(jnp.int32, (1, 128), 1)

    def remote(src, dst, send, recv, **to):
        return pltpu.make_async_remote_copy(
            src_ref=src, dst_ref=dst, send_sem=send, recv_sem=recv, device_id=to, device_id_type=MESH)

    own_f = pltpu.make_async_copy(f_hbm, fext.at[:, pl.ds(4, 8)], local_sem.at[0])
    own_a = pltpu.make_async_copy(a_hbm, aext.at[pl.ds(0, 3), pl.ds(4, 8)], local_sem.at[1])
    own_a.start()
    own_f.start()
    zr[...] = jnp.zeros_like(zr)

    barrier = pltpu.get_barrier_semaphore()
    partners = [{"gx": lax.rem(b + t, 8)} for t in (1, 2, 4, 6, 7)]
    partners += [{"gy": lax.rem(j + t, 8)} for t in range(1, 8)]
    partners += [{"gz": lax.rem(k + t, 8)} for t in range(1, 8)]
    partners += [{"gy": lax.rem(j + t, 8), "gz": lax.rem(k + u, 8)} for t in (1, 7) for u in (1, 7)]
    for to in partners:
        pl.semaphore_signal(barrier, inc=1, device_id=to, device_id_type=MESH)

    fext[:, 0] = jnp.zeros((4, 8, 128), F32)
    fext[:, 15] = jnp.zeros((4, 8, 128), F32)
    aext[3] = jnp.zeros((16, 8, 128), F32)
    for ref in (l0.f, l0.wa, l1.f, l1.up, l1.low, eb1):
        ref[...] = jnp.zeros_like(ref)
    for lv in levels:
        for w in (lv.wa, lv.wb):
            w[pl.ds(0, lv.rows), :] = jnp.zeros((lv.rows, 128), F32)
            w[pl.ds((lv.z + 1) * lv.rows, lv.rows), :] = jnp.zeros((lv.rows, 128), F32)
    pl.semaphore_wait(barrier, len(partners))

    b_up, b_down = lax.rem(b + 1, 8), lax.rem(b + 7, 8)
    strips = [
        remote(a_hbm.at[:, pl.ds(4, 4)], aext.at[pl.ds(0, 3), pl.ds(0, 4)],
               strip_send.at[0], strip_recv.at[0], gx=b_up),
        remote(a_hbm.at[:, pl.ds(0, 4)], aext.at[pl.ds(0, 3), pl.ds(12, 4)],
               strip_send.at[1], strip_recv.at[1], gx=b_down),
        remote(f_hbm.at[:, pl.ds(5, 3)], fext.at[:, pl.ds(1, 3)],
               strip_send.at[2], strip_recv.at[2], gx=b_up),
        remote(f_hbm.at[:, pl.ds(0, 3)], fext.at[:, pl.ds(12, 3)],
               strip_send.at[3], strip_recv.at[3], gx=b_down),
    ]
    for copy in strips:
        copy.start()

    class Wide:
        def __init__(self, n, block, ref, base, h):
            self.n, self.block, self.ref, self.base, self.h = n, block, ref, base, h
            rows, part = pl.ds(0, h), pl.ds(0, h * 8)
            j_up, j_down = jnp.minimum(j + 1, 7), jnp.maximum(j - 1, 0)
            k_to = (lax.rem(k + 1, 8), lax.rem(k + 7, 8))

            def make(src, dst, index, **to):
                return remote(src, dst, ex_send.at[n, index], ex_recv.at[n, index], **to)

            self.up = [make(ys.at[n, 0, rows], yr.at[n, 0, rows], 0, gy=j_up)]
            self.down = [make(ys.at[n, 1, rows], yr.at[n, 1, rows], 1, gy=j_down)]
            self.flat = []
            for dz in range(2):
                self.flat.append(make(zs.at[n, dz, part], zr.at[n, dz, 0, part], 2 + dz, gz=k_to[dz]))
                self.up.append(make(zs.at[n, dz, part], zr.at[n, dz, 1, part], 4 + dz, gy=j_up, gz=k_to[dz]))
                self.down.append(make(zs.at[n, dz, part], zr.at[n, dz, 2, part], 6 + dz, gy=j_down, gz=k_to[dz]))

        def start(self):
            n, block, ref, base, h = self.n, self.block, self.ref, self.base, self.h
            for i in range(h):
                ys[n, 0, i] = ref[pl.ds((base + 4) * 16 + block - h + i, 64, stride=16), :]
                ys[n, 1, i] = ref[pl.ds((base + 4) * 16 + i, 64, stride=16), :]
                zs[n, 0, pl.ds(i * 8, 8), :] = ref[pl.ds((base + 68 - h + i) * 16, 8), :]
                zs[n, 1, pl.ds(i * 8, 8), :] = ref[pl.ds((base + 4 + i) * 16, 8), :]

            @pl.when(j < 7)
            def _():
                for copy in self.up:
                    copy.start()

            @pl.when(j > 0)
            def _():
                for copy in self.down:
                    copy.start()

            for copy in self.flat:
                copy.start()

        def finish(self):
            n, block, ref, base, h = self.n, self.block, self.ref, self.base, self.h

            @pl.when(j > 0)
            def _():
                for copy in self.up:
                    copy.wait_recv()
                for i in range(h):
                    ref[pl.ds((base + 4) * 16 + 16 - h + i, 64, stride=16), :] = yr[n, 0, i]

            @pl.when(j < 7)
            def _():
                for copy in self.down:
                    copy.wait_recv()
                for i in range(h):
                    ref[pl.ds((base + 4) * 16 + block + i, 64, stride=16), :] = yr[n, 1, i]

            for copy in self.flat:
                copy.wait_recv()
            for dz in range(2):
                here, low, high = (zr[n, dz, m, pl.ds(0, h * 8), :].reshape(h, 8, 128) for m in range(3))
                if block == 8:
                    pair = [here, jnp.where(sub < 4, high, low)]
                else:
                    pair = [jnp.where(sub < 4, here, roll(high, 4, 1)), roll(low, 4, 1)]
                v = jnp.concatenate(pair, axis=1)
                if block == 8:
                    if dz == 0:
                        v = roll(jnp.where(lane16 < 64, slots(ref, base + 68 - h, h), v), 64, 2)
                    else:
                        v = roll(jnp.where(lane16 < 64, v, slots(ref, base + 4, h)), 64, 2)
                put(ref, base + (4 - h if dz == 0 else 68), v)

            @pl.when(j < 7)
            def _():
                for copy in self.up:
                    copy.wait_send()

            @pl.when(j > 0)
            def _():
                for copy in self.down:
                    copy.wait_send()

            for copy in self.flat:
                copy.wait_send()

    half_lane = lax.broadcasted_iota(jnp.int32, (64, 128), 1) < 64

    def to_tiles(src, dst, base):
        for y in range(0, 8, 2):
            rows = [src[pl.ds(y + d, 64, stride=8), :] for d in range(2)]
            turned = jnp.concatenate(rows, axis=0).T
            low, high = turned[:64], turned[64:]
            first = (base + 4) * 16 + y
            dst[pl.ds(first, 64, stride=16), :] = jnp.where(half_lane, low, pltpu.roll(high, 64, 1))
            dst[pl.ds(first + 1, 64, stride=16), :] = jnp.where(half_lane, pltpu.roll(low, 64, 1), high)

    fext_rows, aext_rows = fext.reshape(512, 128), aext.reshape(512, 128)

    def x_gather(xg, n):
        first = remote(xg.at[b], xg.at[b], xg_send.at[n, 0], xg_recv.at[n, 0], gx=b + 1 - 2 * lax.rem(b, 2))
        pair = pl.ds((b // 2) * 2, 2)
        second = [remote(xg.at[pair], xg.at[pair], xg_send.at[n, t], xg_recv.at[n, t], gx=lax.rem(b + 2 * t, 8))
                  for t in range(1, 4)]
        return first, second

    def x_pack(weight, xg, first, upper=None):
        source = lax.broadcasted_iota(jnp.int32, (128, 256), 0)
        target = lax.broadcasted_iota(jnp.int32, (128, 256), 1)
        slot, inner = source % 16, (target % 128) % 32
        hit = (source // 64 == target // 128) & ((source % 64) // 16 == (target % 128) // 32) & (inner < 4)
        pair = (slot // 2 == inner + 2) & hit
        if upper is not None:
            pair = pair & (((source % 64) // 16 != 0) | (slot % 2 == (1 if upper else 0)))
        matrix = jnp.where(pair, weight, 0.0).astype(F32)
        moved = jnp.dot(tb[...], matrix, precision=HIGHEST, preferred_element_type=F32)
        parts = [moved[:, :128].reshape(32, 8, 128), moved[:, 128:].reshape(32, 8, 128)]
        total = None
        for g in range(8):
            part = roll(parts[g // 4][(g % 4) * 8:(g % 4) * 8 + 8], 4 * g, 2)
            total = part if total is None else total + part
        packed = jnp.where(sub % 2 == 0, total[:4], total[4:])
        xg[b, pl.ds(first * 8, 32), :] = packed.reshape(32, 128)

    def x_unpack(xg, first, dst):
        g = (lane // 4) % 8
        for q in range(4):
            for odd in range(2):
                v = []
                for n in range(8):
                    tile = xg[n, pl.ds((first + q) * 8, 8), :].reshape(1, 8, 128)
                    v.append(jnp.where(sub % 2 == 1, tile, roll(tile, -1, 1)) if odd
                             else jnp.where(sub % 2 == 0, tile, roll(tile, 1, 1)))
                for s in (1, 2, 4):
                    high = (g // s) % 2 == 1
                    for n in range(8):
                        if n & s == 0:
                            lo, hi = v[n], v[n + s]
                            v[n] = jnp.where(high, roll(hi, 4 * s, 2), lo)
                            v[n + s] = jnp.where(high, hi, roll(lo, -4 * s, 2))
                for n in range(8):
                    put(tmp, n * 8 + 4 * odd + q, v[n])
        for i in range(4):
            dst[pl.ds(64 + i, 64, stride=16), :] = tmp[pl.ds(2 * i, 64, stride=8), :]

    own_a.wait()
    strips[0].wait_recv()
    strips[1].wait_recv()
    to_tiles(aext_rows, l0.wa, 1)
    edges = Wide(0, 8, l0.wa, 1, 4)
    edges.start()
    edges.finish()
    group0 = (lane16 // 16) % 4
    row16 = iota(1, (1, 16, 128))
    x_at = 8 * b + lane16 % 16 - 4
    y_at = 8 * j + jnp.where(row16 < 12, row16, row16 - 16)

    def face_body(i):
        a, xd, xu, yd, yu, zd, zu = neighbours(l0, l0.wa, i)
        z_at = 128 * k + 64 * (iota(2, a.shape) // 64) + i * l0.ch - 4 + iota(0, a.shape)
        side_up = jnp.where(group0 == 0, xu, jnp.where(group0 == 1, yu, zu))
        side_low = jnp.where(group0 == 0, xd, jnp.where(group0 == 1, yd, zd))
        where = jnp.where(group0 == 0, x_at, jnp.where(group0 == 1, y_at, z_at))
        end = jnp.where(group0 == 0, nx - 1, jnp.where(group0 == 1, ny - 1, nz - 1))
        l0.put(l0.up, i, jnp.where(where == end, 0.0, 0.5 * (a + side_up)))
        l0.put(l0.low, i, jnp.where(where == 0, 0.0, 0.5 * (a + side_low)))

    loop(l0.turns, face_body)

    for upper, ref in ((True, l0.up), (False, l0.low)):
        def body(i, ref=ref, upper=upper):
            put(tb, i * 16, coarse_faces(*own_pairs(ref, i), 16, upper, 1, None))

        loop(2, body)
        x_pack(0.25, xgf, 0 if upper else 4, upper)
    faces_first, faces_second = x_gather(xgf, 1)
    faces_first.start()
    make_coefs(l0, 16)

    own_f.wait()
    strips[2].wait_recv()
    strips[3].wait_recv()
    to_tiles(fext_rows, l0.f, 0)
    edges = Wide(1, 8, l0.f, 0, 3)
    edges.start()
    faces_first.wait_recv()
    for copy in faces_second:
        copy.start()
    edges.finish()

    over_theta, ((a1, b1), (a2, b2)) = SMOOTH

    def downward(lv):
        init_down(lv, over_theta)
        step(lv, lv.wa, lv.wb, a1, b1)
        step(lv, lv.wb, lv.wa, a2, b2)
        step(lv, lv.wa, None)

    def upward(lv, coarse_at):
        init_up(lv, coarse_at)
        step(lv, lv.wa, lv.wb, None, over_theta)
        step(lv, lv.wb, lv.wa, a1, b1)
        step(lv, lv.wa, None, a2, b2, last=True)

    downward(l0)

    def body(i):
        first, second = own_pairs(l0.r, i)
        put(tb, i * 16, both(first + second, 1, 1))

    loop(2, body)
    x_pack(0.125, xg1, 0)
    right_first, right_second = x_gather(xg1, 0)
    right_first.start()

    slot = lane % 16
    for side, first in ((0, 10), (1, 4)):
        packed = jnp.zeros((8, 8, 128), F32)
        for g in range(8):
            v = slots(l0.r, 4 + 8 * g, 8)[:, :8]
            packed = jnp.where(slot // 2 == g, roll(v, 2 * g - first, 2), packed)
        rxs[side] = packed.reshape(64, 128)
    rx = [remote(rxs.at[0], rxr.at[0], rx_send.at[0], rx_recv.at[0], gx=b_up),
          remote(rxs.at[1], rxr.at[1], rx_send.at[1], rx_recv.at[1], gx=b_down)]
    for copy in rx:
        copy.start()

    for copy in faces_second:
        copy.wait_recv()
    x_unpack(xgf, 0, l1.up)
    x_unpack(xgf, 4, l1.low)
    edges_up, edges_low = Wide(2, 4, l1.up, 0, 3), Wide(3, 4, l1.low, 0, 3)
    edges_up.start()
    edges_low.start()

    def second_pack(pz, first):
        v = jnp.where(lane2 % 2 == 0, tb[pl.ds(0, 32, stride=8), :], tb[pl.ds(2, 32, stride=8), :])
        pz[pl.ds(first + 8, 32), :] = v

    def second_edges(pz, first, n):
        up, down = pl.ds(first + 32, 8), pl.ds(first + 8, 8)
        return [remote(pz.at[up], pz.at[pl.ds(first, 8)], pz_send.at[n, 0], pz_recv.at[n, 0], gz=lax.rem(k + 1, 8)),
                remote(pz.at[down], pz.at[pl.ds(first + 40, 8)], pz_send.at[n, 1], pz_recv.at[n, 1],
                       gz=lax.rem(k + 7, 8))]

    def y_gather(pz, yg, n):
        return [remote(pz, yg.at[j], yg_send.at[n, t], yg_recv.at[n, t], gy=lax.rem(j + t, 8)) for t in range(1, 8)]

    def second_unpack(yg, first, dst):
        for n in range(8):
            v = yg[n, pl.ds(first, 48), :]
            dst[pl.ds(2 * n, 48, stride=16), :] = jnp.where(lane2 % 2 == 0, v, roll(v, 1, 1))
            dst[pl.ds(2 * n + 1, 48, stride=16), :] = jnp.where(lane2 % 2 == 1, v, roll(v, -1, 1))

    for upper, ref in ((True, l1.up), (False, l1.low)):
        def body(i, ref=ref, upper=upper):
            put(tb, i * 16, 0.25 * coarse_faces(*own_pairs(ref, i), 32, upper, 1, 1))

        loop(2, body)
        second_pack(pzf, 0 if upper else 48)
    faces_z = second_edges(pzf, 0, 0) + second_edges(pzf, 48, 1)
    for copy in faces_z:
        copy.start()
    edges_up.finish()
    edges_low.finish()
    make_coefs(l1, 32)
    for copy in faces_z:
        copy.wait_recv()
    ygf[j] = pzf[...]
    faces_y = y_gather(pzf, ygf, 0)
    for copy in faces_y:
        copy.start()

    right_first.wait_recv()
    for copy in right_second:
        copy.start()
    for copy in faces_y:
        copy.wait_recv()
    second_unpack(ygf, 0, l2.up)
    second_unpack(ygf, 48, l2.low)
    for copy in right_second:
        copy.wait_recv()
    x_unpack(xg1, 0, l1.f)
    edges = Wide(4, 4, l1.f, 0, 3)
    edges.start()
    make_coefs(l2, 32)
    edges.finish()
    downward(l1)

    def body(i):
        first, second = own_pairs(l1.r, i)
        put(tb, i * 16, 0.125 * both(both(first + second, 1, 1), 1, 2))

    loop(2, body)
    second_pack(pz1, 0)
    right_z = second_edges(pz1, 0, 2)
    for copy in right_z:
        copy.start()
    edges1 = Wide(5, 4, l1.r, 0, 2)
    edges1.start()

    t = lane % 4

    def third(ref, upper=None):
        even, odd = (ref[pl.ds(128 + d, 256, stride=2), :].reshape(16, 2, 8, 128) for d in range(2))
        if upper is None:
            v = even + odd
            v = 0.125 * both(v[:, 0] + v[:, 1], 2, 2)
        else:
            g = lane // 32
            side = odd if upper else even
            first, second = (jnp.where(g == 1, side[:, d], even[:, d] + odd[:, d]) for d in range(2))
            v = jnp.where(g == 2, second if upper else first, first + second)
            v = 0.25 * jnp.where(g == 0, pick(v, 2, 2, upper), both(v, 2, 2))
        v = v.reshape(4, 4, 8, 128)
        out = v[:, 0]
        for u in range(1, 4):
            out = jnp.where(t == u, v[:, u], out)
        return out

    def z_gather(g, n):
        rows = pl.ds(pl.multiple_of(k * 32, 8), 32)
        return [remote(g.at[rows], g.at[rows], zg_send.at[n, u], zg_recv.at[n, u], gz=lax.rem(k + u, 8))
                for u in range(1, 8)]

    put(l3.up, 4 * k, third(l2.up, True))
    put(l3.low, 4 * k, third(l2.low, False))
    third_faces = z_gather(l3.up, 0) + z_gather(l3.low, 1)

    for copy in right_z:
        copy.wait_recv()
    yg1[j] = pz1[...]
    right_y = y_gather(pz1, yg1, 1)
    for copy in right_y:
        copy.start()
    for copy in third_faces:
        copy.start()
    for copy in third_faces:
        copy.wait_recv()
    make_coefs(l3, 32)
    for upper in (True, False):
        src, dst = (l3.up, l4.up) if upper else (l3.low, l4.low)

        def body(i, src=src, dst=dst, upper=upper):
            g = lane // 32
            v = l3.get(src, i)
            v = jnp.where(g == 2, pick(v, 1, 2, upper), both(v, 1, 2))
            v = jnp.where(g == 1, pick(v, 1, 1, upper), both(v, 1, 1))
            l4.put(dst, i, 0.25 * jnp.where(g == 0, pick(v, 4, 2, upper), both(v, 4, 2)))

        loop(l3.turns, body)
    make_coefs(l4, 32)
    for copy in right_y:
        copy.wait_recv()
    second_unpack(yg1, 0, l2.f)
    downward(l2)
    put(l3.f, 4 * k, third(l2.r))
    third_right = z_gather(l3.f, 2)
    for copy in third_right:
        copy.start()

    for copy in rx:
        copy.wait_recv()
    for g in range(8):
        v = slots(l0.r, 4 + 8 * g, 8)
        own = v[:, :8]
        own = jnp.where(slot // 2 == 1, roll(rxr[0].reshape(8, 8, 128), 2 - 2 * g, 2), own)
        own = jnp.where(slot // 2 == 6, roll(rxr[1].reshape(8, 8, 128), 12 - 2 * g, 2), own)
        put(l0.r, 4 + 8 * g, jnp.concatenate([own, v[:, 8:]], axis=1))
    edges0 = Wide(6, 8, l0.r, 0, 2)
    edges0.start()

    for copy in third_right:
        copy.wait_recv()

    downward(l3)

    def body(i):
        l4.put(l4.f, i, 0.125 * both(both(both(l3.get(l3.r, i), 1, 2), 1, 1), 4, 2))

    loop(l3.turns, body)
    solve_theta, solve_steps = SOLVE
    init_down(l4, solve_theta)
    w, w_next = l4.wa, l4.wb
    for n, (alpha, beta) in enumerate(solve_steps):
        step(l4, w, w_next, alpha, beta, last=n == len(solve_steps) - 1)
        w, w_next = w_next, w
    upward(l3, lambda i: l4.get(l4.x, i))

    for q in range(6):
        v = l3.x[pl.ds(pl.multiple_of(lax.rem(4 * k + q + 31, 32) * 8, 8), 8), :].reshape(1, 8, 128)
        for z in range(4):
            moved = v
            for u in range(4):
                if u != z:
                    moved = jnp.where(t == u, roll(v, u - z, 2), moved)
            first = (4 * q + z) * 16
            eb2[pl.ds(first, 8, stride=2), :] = moved.reshape(8, 128)
            eb2[pl.ds(first + 1, 8, stride=2), :] = moved.reshape(8, 128)

    def twice(ref, offset):
        def chunk(i):
            v = slots(ref, i * 4 + offset, 4)
            return jnp.broadcast_to(v[:, None], (4, 2, 16, 128)).reshape(8, 16, 128)

        return chunk

    upward(l2, twice(eb2, 0))

    for i, from_y in ((0, 0), (1, 1), (2, 2), (3, 3), (6, 14), (7, 15)):
        v = l2.x[pl.ds(lax.rem(2 * j + from_y, 16), 48, stride=16), :]
        eb1[pl.ds(2 * i, 48, stride=16), :] = v
        eb1[pl.ds(2 * i + 1, 48, stride=16), :] = v
    edges1.finish()
    upward(l1, twice(eb1, 6))
    edges = Wide(7, 4, l1.x, 0, 2)
    edges.start()
    edges0.finish()
    edges.finish()

    source = lax.broadcasted_iota(jnp.int32, (128, 128), 0)
    target = lax.broadcasted_iota(jnp.int32, (128, 128), 1)
    hit = (source // 32 == (target % 64) // 16) & (source % 32 == 4 * b - 2 + (target % 16) // 2)
    v = slots(l1.x, 0, 72)
    v = jnp.where(sub < 6, v[:, :8], v[:, 8:]).reshape(576, 128)
    v = jnp.dot(v, jnp.where(hit, 1.0, 0.0).astype(F32), precision=HIGHEST, preferred_element_type=F32)
    eb0[pl.ds(0, 576, stride=2), :] = v
    eb0[pl.ds(1, 576, stride=2), :] = v

    def top_chunk(i):
        v = jnp.where(lane16 < 64, slots(eb0, i * 4 + 2, 4), slots(eb0, i * 4 + 34, 4))
        return jnp.broadcast_to(v[:, None], (4, 2, 16, 128)).reshape(8, 16, 128)

    upward(l0, top_chunk)

    for y in range(0, 8, 2):
        first = l0.x[pl.ds(64 + y, 64, stride=16), :]
        second = l0.x[pl.ds(65 + y, 64, stride=16), :]
        low = jnp.where(half_lane, first, pltpu.roll(second, 64, 1))
        high = jnp.where(half_lane, pltpu.roll(first, 64, 1), second)
        turned = pltpu.roll(jnp.concatenate([low, high], axis=0), 124, 1).T
        for d in range(2):
            for v in range(4):
                start = d * 64 + v * 16
                out_ref[pl.ds(v * 64 + y + d, 8, stride=8), :] = turned[start:start + 8]

    for copy in (strips + [faces_first, right_first] + faces_second + right_second + rx + faces_z + right_z + faces_y
                 + right_y + third_faces + third_right):
        copy.wait_send()


def solution(mesh):
    def per_device(right_side, affinity):
        nx = affinity.shape[1] * mesh.shape["gx"]
        ny = affinity.shape[2] * mesh.shape["gy"]
        nz = affinity.shape[3] * mesh.shape["gz"]
        scratch = []
        for z, rows, *_ in LEVELS:
            scratch += level_shapes(z, rows)
        scratch += [pltpu.VMEM(shape, F32) for shape in (
            (4, 16, 8, 128), (4, 16, 8, 128),
            (8, 2, 4, 64, 128), (8, 2, 4, 64, 128), (8, 2, 32, 128), (8, 2, 3, 32, 128),
            (256, 128), (512, 128), (8, 32, 128), (8, 64, 128), (2, 64, 128), (2, 64, 128),
            (48, 128), (96, 128), (8, 48, 128), (8, 96, 128), (384, 128), (768, 128), (1152, 128))]
        dma = pltpu.SemaphoreType.DMA
        scratch += [dma(shape) for shape in (
            (2,), (4,), (4,), (8, 8), (8, 8), (2, 4), (2, 4), (2,), (2,), (3, 2), (3, 2), (2, 8), (2, 8), (3, 8), (3, 8))]
        out = pl.pallas_call(
            functools.partial(kernel, nx, ny, nz),
            out_shape=jax.ShapeDtypeStruct((256, 128), F32),
            in_specs=[pl.BlockSpec(memory_space=pl.ANY)] * 2,
            out_specs=pl.BlockSpec(memory_space=pltpu.VMEM),
            scratch_shapes=scratch,
            compiler_params=pltpu.CompilerParams(
                collective_id=0, has_side_effects=True, vmem_limit_bytes=60 * 1024 * 1024),
        )(right_side, affinity)
        return out.reshape(right_side.shape)

    spec = P(None, "gx", "gy", "gz")
    return jax.shard_map(per_device, mesh=mesh, in_specs=(spec, spec), out_specs=spec, check_vma=False)
```

```python
import functools

import jax
import jax.numpy as jnp
from jax import lax
from jax.experimental import pallas as pl
from jax.experimental.pallas import tpu as pltpu
from jax.sharding import PartitionSpec as P

MESH = pl.DeviceIdType.MESH
HIGHEST = lax.Precision.HIGHEST
F32 = jnp.float32

DEGREE = 3
COARSE_DEGREE = 8
SHIFT = 0.02
SMOOTH_LOWER = 0.5
UPPER = 2.0 + SHIFT


def cheb_coefs(a, b, m):
    theta, delta = 0.5 * (b + a), 0.5 * (b - a)
    sigma = theta / delta
    rho = 1.0 / sigma
    steps = []
    for _ in range(m - 1):
        nxt = 1.0 / (2.0 * sigma - rho)
        steps.append((nxt * rho, 2.0 * nxt / delta))
        rho = nxt
    return 1.0 / theta, steps


SMOOTH = cheb_coefs(SMOOTH_LOWER, UPPER, DEGREE)
SOLVE = cheb_coefs(SHIFT, UPPER, COARSE_DEGREE)


def iota(dim, shape=(1, 8, 128)):
    return lax.broadcasted_iota(jnp.int32, shape, dim)


def roll(x, shift, axis):
    shift = shift % x.shape[axis]
    return x if shift == 0 else pltpu.roll(x, shift, axis)


def both(x, k, axis):
    bit = (iota(axis, (1,) + x.shape[1:]) // k) % 2
    return x + jnp.where(bit == 0, roll(x, -k, axis), roll(x, k, axis))


def pick(x, k, axis, upper):
    bit = (iota(axis, (1,) + x.shape[1:]) // k) % 2
    if upper:
        return jnp.where(bit == 1, x, roll(x, -k, axis))
    return jnp.where(bit == 0, x, roll(x, k, axis))


def slots(ref, start, count, rows=16):
    if not isinstance(start, int):
        start = pl.multiple_of(start * rows, rows)
    else:
        start = start * rows
    return ref[pl.ds(start, count * rows), :].reshape(count, rows, 128)


def put(ref, start, value):
    count, rows = value.shape[:2]
    if not isinstance(start, int):
        start = pl.multiple_of(start * rows, rows)
    else:
        start = start * rows
    ref[pl.ds(start, count * rows), :] = value.reshape(count * rows, 128)


def loop(count, body):
    def run(i, carry):
        body(i)
        return carry

    lax.fori_loop(0, count, run, 0)


class Level:
    def __init__(self, z, rows, sy, sx, mode, refs):
        self.z, self.rows, self.sy, self.sx, self.mode = z, rows, sy, sx, mode
        self.ch = 128 // rows
        self.parts = z // self.ch if rows == 8 else 3
        (self.coef, self.scale, self.f, self.r, self.d, self.x, self.wa, self.wb, self.up, self.low,
         self.r_next, self.d_next, self.x_next) = refs

    def loop(self, body):
        def turn(i, carry):
            for part in range(self.parts):
                body(i * self.parts + part)
            return carry

        turns = self.z // (self.ch * self.parts)
        if turns == 1:
            turn(0, 0)
        else:
            lax.fori_loop(0, turns, turn, 0)

    def get(self, ref, i, offset=0):
        return slots(ref, i * self.ch + offset, self.ch, self.rows)

    def put(self, ref, i, value, offset=0):
        put(ref, i * self.ch + offset, value)


LEVELS = ((72, 16, 1, 1, 0), (72, 16, 1, 1, 0), (48, 16, 1, 2, 0), (32, 8, 1, 4, 1), (32, 8, 2, 8, 2))


def level_shapes(z, rows):
    n = z * rows
    pad = (z + 2) * rows
    return [pltpu.VMEM((6 * n, 128), F32)] + [pltpu.VMEM((n, 128), F32)] * 5 + [pltpu.VMEM((pad, 128), F32)] * 2 + [
        pltpu.VMEM((n, 128), F32)] * 5


def neighbours(lv, w_ref, i):
    w, before, after = lv.get(w_ref, i, 1), lv.get(w_ref, i, 0), lv.get(w_ref, i, 2)
    xd, xu = roll(w, lv.sx, 2), roll(w, -lv.sx, 2)
    yd, yu = roll(w, lv.sy, 1), roll(w, -lv.sy, 1)
    if lv.mode == 0:
        zd, zu = before, after
    else:
        s = lv.mode
        t = iota(2) % 4
        zu = jnp.where(t < 4 - s, roll(w, -s, 2), roll(after, 4 - s, 2))
        zd = jnp.where(t >= s, roll(w, s, 2), roll(before, s - 4, 2))
    return w, xd, xu, yd, yu, zd, zu


def apply_at(lv, w_ref, i):
    _, *near = neighbours(lv, w_ref, i)
    total = None
    for k, value in enumerate(near):
        term = slots(lv.coef, k * lv.z + i * lv.ch, lv.ch, lv.rows) * value
        total = term if total is None else total + term
    return total


def init_down(lv, over_theta):
    def body(i):
        f = lv.get(lv.f, i)
        d = f * over_theta
        lv.put(lv.r, i, f)
        lv.put(lv.d, i, d)
        lv.put(lv.x, i, d)
        lv.put(lv.wa, i, lv.get(lv.scale, i) * d, 1)

    lv.loop(body)


def init_up(lv, coarse_at):
    def body(i):
        d = coarse_at(i)
        lv.put(lv.d, i, d)
        lv.put(lv.x_next, i, lv.get(lv.x, i) + d)
        lv.put(lv.wa, i, lv.get(lv.scale, i) * d, 1)

    lv.loop(body)
    lv.x, lv.x_next = lv.x_next, lv.x


def step(lv, w_ref, w_next, alpha=None, beta=None, last=False):
    def body(i):
        d = lv.get(lv.d, i)
        r = lv.get(lv.r, i) - ((1.0 + SHIFT) * d - apply_at(lv, w_ref, i))
        if not last:
            lv.put(lv.r_next, i, r)
        if beta is None:
            return
        d = beta * r if alpha is None else alpha * d + beta * r
        lv.put(lv.x_next, i, lv.get(lv.x, i) + d)
        if not last:
            lv.put(lv.d_next, i, d)
            lv.put(w_next, i, lv.get(lv.scale, i) * d, 1)

    lv.loop(body)
    if not last:
        lv.r, lv.r_next = lv.r_next, lv.r
    if beta is not None:
        lv.x, lv.x_next = lv.x_next, lv.x
        lv.d, lv.d_next = lv.d_next, lv.d


def make_coefs(lv, group):
    g = (iota(2, (1, lv.rows, 128)) // group) % 4

    def spread(value, k):
        out = value
        for to in range(4):
            if to != k:
                out = jnp.where(g == to, roll(value, group * (to - k), 2), out)
        return out

    def body(i):
        low, up = lv.get(lv.low, i), lv.get(lv.up, i)
        faces = []
        for k in range(3):
            faces += [spread(low, k), spread(up, k)]
        total = faces[0] + faces[1] + faces[2] + faces[3] + faces[4] + faces[5]
        scale = jnp.where(total > 0.0, lax.rsqrt(total), 0.0)
        lv.put(lv.scale, i, scale)
        for k in range(6):
            put(lv.coef, k * lv.z + i * lv.ch, scale * faces[k])

    lv.loop(body)


def own_pairs(ref, i):
    v = slots(ref, 4 + 32 * i, 32)[:, :8].reshape(16, 2, 8, 128)
    return v[:, 0], v[:, 1]


def coarse_faces(first, second, group, upper, ky, kx):
    g = (iota(2) // group) % 4
    v = jnp.where(g == 2, second if upper else first, first + second)
    v = jnp.where(g == 1, pick(v, ky, 1, upper), both(v, ky, 1))
    if kx is not None:
        v = jnp.where(g == 0, pick(v, kx, 2, upper), both(v, kx, 2))
    return v


def kernel(nx, ny, nz, f_hbm, a_hbm, out_ref, *scratch):
    refs = list(scratch)

    def take(count):
        got = refs[:count]
        del refs[:count]
        return got

    levels = [Level(*shape, take(13)) for shape in LEVELS]
    (fext, aext, ys, yr, zs, zr, tb, tmp, xg1, xgf, rxs, rxr, pz1, pzf, yg1, ygf, eb2, eb1, eb0) = take(19)
    (local_sem, strip_send, strip_recv, ex_send, ex_recv, xg_send, xg_recv, rx_send, rx_recv,
     pz_send, pz_recv, yg_send, yg_recv, zg_send, zg_recv) = take(15)
    l0, l1, l2, l3, l4 = levels

    b, j, k = lax.axis_index("gx"), lax.axis_index("gy"), lax.axis_index("gz")
    sub, lane, lane16 = iota(1), iota(2), iota(2, (1, 16, 128))
    lane2 = lax.broadcasted_iota(jnp.int32, (1, 128), 1)

    def remote(src, dst, send, recv, **to):
        return pltpu.make_async_remote_copy(
            src_ref=src, dst_ref=dst, send_sem=send, recv_sem=recv, device_id=to, device_id_type=MESH)

    own_f = pltpu.make_async_copy(f_hbm, fext.at[:, pl.ds(4, 8)], local_sem.at[0])
    own_a = pltpu.make_async_copy(a_hbm, aext.at[pl.ds(0, 3), pl.ds(4, 8)], local_sem.at[1])
    own_a.start()
    own_f.start()
    zr[...] = jnp.zeros_like(zr)

    barrier = pltpu.get_barrier_semaphore()
    partners = [{"gx": lax.rem(b + t, 8)} for t in (1, 2, 4, 6, 7)]
    partners += [{"gy": lax.rem(j + t, 8)} for t in range(1, 8)]
    partners += [{"gz": lax.rem(k + t, 8)} for t in range(1, 8)]
    partners += [{"gy": lax.rem(j + t, 8), "gz": lax.rem(k + u, 8)} for t in (1, 7) for u in (1, 7)]
    for to in partners:
        pl.semaphore_signal(barrier, inc=1, device_id=to, device_id_type=MESH)

    fext[:, 0] = jnp.zeros((4, 8, 128), F32)
    fext[:, 15] = jnp.zeros((4, 8, 128), F32)
    aext[3] = jnp.zeros((16, 8, 128), F32)
    for n in (1, 2):
        aext[n, 0] = jnp.zeros((8, 128), F32)
        aext[n, 15] = jnp.zeros((8, 128), F32)
    for ref in (l0.f, l0.wa, l1.f, l1.up, l1.low, eb1):
        ref[...] = jnp.zeros_like(ref)
    for lv in levels:
        for w in (lv.wa, lv.wb):
            w[pl.ds(0, lv.rows), :] = jnp.zeros((lv.rows, 128), F32)
            w[pl.ds((lv.z + 1) * lv.rows, lv.rows), :] = jnp.zeros((lv.rows, 128), F32)
    pl.semaphore_wait(barrier, len(partners))

    b_up, b_down = lax.rem(b + 1, 8), lax.rem(b + 7, 8)
    strips = [
        remote(a_hbm.at[:, pl.ds(5, 3)], aext.at[pl.ds(0, 3), pl.ds(1, 3)],
               strip_send.at[0], strip_recv.at[0], gx=b_up),
        remote(a_hbm.at[:, pl.ds(0, 3)], aext.at[pl.ds(0, 3), pl.ds(12, 3)],
               strip_send.at[1], strip_recv.at[1], gx=b_down),
        remote(a_hbm.at[0, 4], aext.at[0, 0], strip_send.at[4], strip_recv.at[4], gx=b_up),
        remote(a_hbm.at[0, 3], aext.at[0, 15], strip_send.at[5], strip_recv.at[5], gx=b_down),
        remote(f_hbm.at[:, pl.ds(5, 3)], fext.at[:, pl.ds(1, 3)],
               strip_send.at[2], strip_recv.at[2], gx=b_up),
        remote(f_hbm.at[:, pl.ds(0, 3)], fext.at[:, pl.ds(12, 3)],
               strip_send.at[3], strip_recv.at[3], gx=b_down),
    ]
    for copy in strips[:4]:
        copy.start()
    for copy in strips[:4]:
        copy.wait_send()
    for copy in strips[4:]:
        copy.start()

    class Wide:
        def __init__(self, n, block, ref, base, h):
            self.n, self.block, self.ref, self.base, self.h = n, block, ref, base, h
            rows, part = pl.ds(0, h), pl.ds(0, h * 8)
            j_up, j_down = jnp.minimum(j + 1, 7), jnp.maximum(j - 1, 0)
            k_to = (lax.rem(k + 1, 8), lax.rem(k + 7, 8))

            def make(src, dst, index, **to):
                return remote(src, dst, ex_send.at[n, index], ex_recv.at[n, index], **to)

            self.up = [make(ys.at[n, 0, rows], yr.at[n, 0, rows], 0, gy=j_up)]
            self.down = [make(ys.at[n, 1, rows], yr.at[n, 1, rows], 1, gy=j_down)]
            self.flat = []
            for dz in range(2):
                self.flat.append(make(zs.at[n, dz, part], zr.at[n, dz, 0, part], 2 + dz, gz=k_to[dz]))
                self.up.append(make(zs.at[n, dz, part], zr.at[n, dz, 1, part], 4 + dz, gy=j_up, gz=k_to[dz]))
                self.down.append(make(zs.at[n, dz, part], zr.at[n, dz, 2, part], 6 + dz, gy=j_down, gz=k_to[dz]))

        def start(self):
            n, block, ref, base, h = self.n, self.block, self.ref, self.base, self.h
            for i in range(h):
                ys[n, 0, i] = ref[pl.ds((base + 4) * 16 + block - h + i, 64, stride=16), :]
                ys[n, 1, i] = ref[pl.ds((base + 4) * 16 + i, 64, stride=16), :]
                zs[n, 0, pl.ds(i * 8, 8), :] = ref[pl.ds((base + 68 - h + i) * 16, 8), :]
                zs[n, 1, pl.ds(i * 8, 8), :] = ref[pl.ds((base + 4 + i) * 16, 8), :]

            @pl.when(j < 7)
            def _():
                for copy in self.up:
                    copy.start()

            @pl.when(j > 0)
            def _():
                for copy in self.down:
                    copy.start()

            for copy in self.flat:
                copy.start()

        def finish(self):
            n, block, ref, base, h = self.n, self.block, self.ref, self.base, self.h

            @pl.when(j > 0)
            def _():
                for copy in self.up:
                    copy.wait_recv()
                for i in range(h):
                    ref[pl.ds((base + 4) * 16 + 16 - h + i, 64, stride=16), :] = yr[n, 0, i]

            @pl.when(j < 7)
            def _():
                for copy in self.down:
                    copy.wait_recv()
                for i in range(h):
                    ref[pl.ds((base + 4) * 16 + block + i, 64, stride=16), :] = yr[n, 1, i]

            for copy in self.flat:
                copy.wait_recv()
            for dz in range(2):
                here, low, high = (zr[n, dz, m, pl.ds(0, h * 8), :].reshape(h, 8, 128) for m in range(3))
                if block == 8:
                    pair = [here, jnp.where(sub < 4, high, low)]
                else:
                    pair = [jnp.where(sub < 4, here, roll(high, 4, 1)), roll(low, 4, 1)]
                v = jnp.concatenate(pair, axis=1)
                if block == 8:
                    if dz == 0:
                        v = roll(jnp.where(lane16 < 64, slots(ref, base + 68 - h, h), v), 64, 2)
                    else:
                        v = roll(jnp.where(lane16 < 64, v, slots(ref, base + 4, h)), 64, 2)
                put(ref, base + (4 - h if dz == 0 else 68), v)

            @pl.when(j < 7)
            def _():
                for copy in self.up:
                    copy.wait_send()

            @pl.when(j > 0)
            def _():
                for copy in self.down:
                    copy.wait_send()

            for copy in self.flat:
                copy.wait_send()

    half_lane = lax.broadcasted_iota(jnp.int32, (64, 128), 1) < 64

    def to_tiles(src, dst, base):
        for y in range(0, 8, 2):
            rows = [src[pl.ds(y + d, 64, stride=8), :] for d in range(2)]
            turned = jnp.concatenate(rows, axis=0).T
            low, high = turned[:64], turned[64:]
            first = (base + 4) * 16 + y
            dst[pl.ds(first, 64, stride=16), :] = jnp.where(half_lane, low, pltpu.roll(high, 64, 1))
            dst[pl.ds(first + 1, 64, stride=16), :] = jnp.where(half_lane, pltpu.roll(low, 64, 1), high)

    fext_rows, aext_rows = fext.reshape(512, 128), aext.reshape(512, 128)

    def x_gather(xg, n):
        first = remote(xg.at[b], xg.at[b], xg_send.at[n, 0], xg_recv.at[n, 0], gx=b + 1 - 2 * lax.rem(b, 2))
        pair = pl.ds((b // 2) * 2, 2)
        second = [remote(xg.at[pair], xg.at[pair], xg_send.at[n, t], xg_recv.at[n, t], gx=lax.rem(b + 2 * t, 8))
                  for t in range(1, 4)]
        return first, second

    def x_pack(weight, xg, first, upper=None):
        source = lax.broadcasted_iota(jnp.int32, (128, 256), 0)
        target = lax.broadcasted_iota(jnp.int32, (128, 256), 1)
        slot, inner = source % 16, (target % 128) % 32
        hit = (source // 64 == target // 128) & ((source % 64) // 16 == (target % 128) // 32) & (inner < 4)
        pair = (slot // 2 == inner + 2) & hit
        if upper is not None:
            pair = pair & (((source % 64) // 16 != 0) | (slot % 2 == (1 if upper else 0)))
        matrix = jnp.where(pair, weight, 0.0).astype(F32)
        moved = jnp.dot(tb[...], matrix, precision=HIGHEST, preferred_element_type=F32)
        parts = [moved[:, :128].reshape(32, 8, 128), moved[:, 128:].reshape(32, 8, 128)]
        total = None
        for g in range(8):
            part = roll(parts[g // 4][(g % 4) * 8:(g % 4) * 8 + 8], 4 * g, 2)
            total = part if total is None else total + part
        packed = jnp.where(sub % 2 == 0, total[:4], total[4:])
        xg[b, pl.ds(first * 8, 32), :] = packed.reshape(32, 128)

    def x_unpack(xg, first, dst):
        g = (lane // 4) % 8
        for q in range(4):
            for odd in range(2):
                v = []
                for n in range(8):
                    tile = xg[n, pl.ds((first + q) * 8, 8), :].reshape(1, 8, 128)
                    v.append(jnp.where(sub % 2 == 1, tile, roll(tile, -1, 1)) if odd
                             else jnp.where(sub % 2 == 0, tile, roll(tile, 1, 1)))
                for s in (1, 2, 4):
                    high = (g // s) % 2 == 1
                    for n in range(8):
                        if n & s == 0:
                            lo, hi = v[n], v[n + s]
                            v[n] = jnp.where(high, roll(hi, 4 * s, 2), lo)
                            v[n + s] = jnp.where(high, hi, roll(lo, -4 * s, 2))
                for n in range(8):
                    put(tmp, n * 8 + 4 * odd + q, v[n])
        for i in range(4):
            dst[pl.ds(64 + i, 64, stride=16), :] = tmp[pl.ds(2 * i, 64, stride=8), :]

    own_a.wait()
    for copy in strips[:4]:
        copy.wait_recv()
    to_tiles(aext_rows, l0.wa, 1)
    edges = Wide(0, 8, l0.wa, 1, 4)
    edges.start()
    edges.finish()
    group0 = (lane16 // 16) % 4
    row16 = iota(1, (1, 16, 128))
    x_at = 8 * b + lane16 % 16 - 4
    y_at = 8 * j + jnp.where(row16 < 12, row16, row16 - 16)

    def face_body(i):
        a, xd, xu, yd, yu, zd, zu = neighbours(l0, l0.wa, i)
        z_at = 128 * k + 64 * (iota(2, a.shape) // 64) + i * l0.ch - 4 + iota(0, a.shape)
        side_up = jnp.where(group0 == 0, xu, jnp.where(group0 == 1, yu, zu))
        side_low = jnp.where(group0 == 0, xd, jnp.where(group0 == 1, yd, zd))
        where = jnp.where(group0 == 0, x_at, jnp.where(group0 == 1, y_at, z_at))
        end = jnp.where(group0 == 0, nx - 1, jnp.where(group0 == 1, ny - 1, nz - 1))
        l0.put(l0.up, i, jnp.where(where == end, 0.0, 0.5 * (a + side_up)))
        l0.put(l0.low, i, jnp.where(where == 0, 0.0, 0.5 * (a + side_low)))

    l0.loop(face_body)

    for upper, ref in ((True, l0.up), (False, l0.low)):
        def body(i, ref=ref, upper=upper):
            put(tb, i * 16, coarse_faces(*own_pairs(ref, i), 16, upper, 1, None))

        loop(2, body)
        x_pack(0.25, xgf, 0 if upper else 4, upper)
    faces_first, faces_second = x_gather(xgf, 1)
    faces_first.start()
    make_coefs(l0, 16)

    own_f.wait()
    for copy in strips[4:]:
        copy.wait_recv()
    to_tiles(fext_rows, l0.f, 0)
    edges = Wide(1, 8, l0.f, 0, 3)
    edges.start()
    edges.finish()

    over_theta, ((a1, b1), (a2, b2)) = SMOOTH

    def downward(lv):
        init_down(lv, over_theta)
        step(lv, lv.wa, lv.wb, a1, b1)
        step(lv, lv.wb, lv.wa, a2, b2)
        step(lv, lv.wa, None)

    def upward(lv, coarse_at):
        init_up(lv, coarse_at)
        step(lv, lv.wa, lv.wb, None, over_theta)
        step(lv, lv.wb, lv.wa, a1, b1)
        step(lv, lv.wa, None, a2, b2, last=True)

    downward(l0)

    def body(i):
        first, second = own_pairs(l0.r, i)
        put(tb, i * 16, both(first + second, 1, 1))

    loop(2, body)
    x_pack(0.125, xg1, 0)
    right_first, right_second = x_gather(xg1, 0)
    right_first.start()
    faces_first.wait_recv()
    for copy in faces_second:
        copy.start()

    slot = lane % 16
    for side, first in ((0, 10), (1, 4)):
        packed = jnp.zeros((8, 8, 128), F32)
        for g in range(8):
            v = slots(l0.r, 4 + 8 * g, 8)[:, :8]
            packed = jnp.where(slot // 2 == g, roll(v, 2 * g - first, 2), packed)
        rxs[side] = packed.reshape(64, 128)
    rx = [remote(rxs.at[0], rxr.at[0], rx_send.at[0], rx_recv.at[0], gx=b_up),
          remote(rxs.at[1], rxr.at[1], rx_send.at[1], rx_recv.at[1], gx=b_down)]
    for copy in rx:
        copy.start()

    for copy in faces_second:
        copy.wait_recv()
    x_unpack(xgf, 0, l1.up)
    x_unpack(xgf, 4, l1.low)
    edges_up, edges_low = Wide(2, 4, l1.up, 0, 3), Wide(3, 4, l1.low, 0, 3)
    edges_up.start()
    edges_low.start()

    def second_pack(pz, first):
        v = jnp.where(lane2 % 2 == 0, tb[pl.ds(0, 32, stride=8), :], tb[pl.ds(2, 32, stride=8), :])
        pz[pl.ds(first + 8, 32), :] = v

    def second_edges(pz, first, n):
        up, down = pl.ds(first + 32, 8), pl.ds(first + 8, 8)
        return [remote(pz.at[up], pz.at[pl.ds(first, 8)], pz_send.at[n, 0], pz_recv.at[n, 0], gz=lax.rem(k + 1, 8)),
                remote(pz.at[down], pz.at[pl.ds(first + 40, 8)], pz_send.at[n, 1], pz_recv.at[n, 1],
                       gz=lax.rem(k + 7, 8))]

    def y_gather(pz, yg, n):
        return [remote(pz, yg.at[j], yg_send.at[n, t], yg_recv.at[n, t], gy=lax.rem(j + t, 8)) for t in range(1, 8)]

    def second_unpack(yg, first, dst):
        for n in range(8):
            v = yg[n, pl.ds(first, 48), :]
            dst[pl.ds(2 * n, 48, stride=16), :] = jnp.where(lane2 % 2 == 0, v, roll(v, 1, 1))
            dst[pl.ds(2 * n + 1, 48, stride=16), :] = jnp.where(lane2 % 2 == 1, v, roll(v, -1, 1))

    for upper, ref in ((True, l1.up), (False, l1.low)):
        def body(i, ref=ref, upper=upper):
            put(tb, i * 16, 0.25 * coarse_faces(*own_pairs(ref, i), 32, upper, 1, 1))

        loop(2, body)
        second_pack(pzf, 0 if upper else 48)
    faces_z = second_edges(pzf, 0, 0) + second_edges(pzf, 48, 1)
    for copy in faces_z:
        copy.start()
    edges_up.finish()
    edges_low.finish()
    make_coefs(l1, 32)
    for copy in faces_z:
        copy.wait_recv()
    ygf[j] = pzf[...]
    faces_y = y_gather(pzf, ygf, 0)
    for copy in faces_y:
        copy.start()

    right_first.wait_recv()
    for copy in right_second:
        copy.start()
    for copy in right_second:
        copy.wait_recv()
    x_unpack(xg1, 0, l1.f)
    edges = Wide(4, 4, l1.f, 0, 3)
    edges.start()
    edges.finish()
    downward(l1)

    def body(i):
        first, second = own_pairs(l1.r, i)
        put(tb, i * 16, 0.125 * both(both(first + second, 1, 1), 1, 2))

    loop(2, body)
    second_pack(pz1, 0)
    right_z = second_edges(pz1, 0, 2)
    for copy in right_z:
        copy.start()
    edges1 = Wide(5, 4, l1.r, 0, 2)
    edges1.start()

    for copy in faces_y:
        copy.wait_recv()
    second_unpack(ygf, 0, l2.up)
    second_unpack(ygf, 48, l2.low)

    t = lane % 4

    def third(ref, upper=None):
        even, odd = (ref[pl.ds(128 + d, 256, stride=2), :].reshape(16, 2, 8, 128) for d in range(2))
        if upper is None:
            v = even + odd
            v = 0.125 * both(v[:, 0] + v[:, 1], 2, 2)
        else:
            g = lane // 32
            side = odd if upper else even
            first, second = (jnp.where(g == 1, side[:, d], even[:, d] + odd[:, d]) for d in range(2))
            v = jnp.where(g == 2, second if upper else first, first + second)
            v = 0.25 * jnp.where(g == 0, pick(v, 2, 2, upper), both(v, 2, 2))
        v = v.reshape(4, 4, 8, 128)
        out = v[:, 0]
        for u in range(1, 4):
            out = jnp.where(t == u, v[:, u], out)
        return out

    def z_gather(g, n):
        rows = pl.ds(pl.multiple_of(k * 32, 8), 32)
        return [remote(g.at[rows], g.at[rows], zg_send.at[n, u], zg_recv.at[n, u], gz=lax.rem(k + u, 8))
                for u in range(1, 8)]

    put(l3.up, 4 * k, third(l2.up, True))
    put(l3.low, 4 * k, third(l2.low, False))
    third_faces = z_gather(l3.up, 0) + z_gather(l3.low, 1)

    for copy in right_z:
        copy.wait_recv()
    yg1[j] = pz1[...]
    right_y = y_gather(pz1, yg1, 1)
    for copy in right_y:
        copy.start()
    for copy in third_faces:
        copy.start()
    make_coefs(l2, 32)
    for copy in third_faces:
        copy.wait_recv()
    make_coefs(l3, 32)
    for upper in (True, False):
        src, dst = (l3.up, l4.up) if upper else (l3.low, l4.low)

        def body(i, src=src, dst=dst, upper=upper):
            g = lane // 32
            v = l3.get(src, i)
            v = jnp.where(g == 2, pick(v, 1, 2, upper), both(v, 1, 2))
            v = jnp.where(g == 1, pick(v, 1, 1, upper), both(v, 1, 1))
            l4.put(dst, i, 0.25 * jnp.where(g == 0, pick(v, 4, 2, upper), both(v, 4, 2)))

        l3.loop(body)
    make_coefs(l4, 32)
    for copy in right_y:
        copy.wait_recv()
    second_unpack(yg1, 0, l2.f)
    downward(l2)
    put(l3.f, 4 * k, third(l2.r))
    third_right = z_gather(l3.f, 2)
    for copy in third_right:
        copy.start()

    for copy in rx:
        copy.wait_recv()
    for g in range(8):
        v = slots(l0.r, 4 + 8 * g, 8)
        own = v[:, :8]
        own = jnp.where(slot // 2 == 1, roll(rxr[0].reshape(8, 8, 128), 2 - 2 * g, 2), own)
        own = jnp.where(slot // 2 == 6, roll(rxr[1].reshape(8, 8, 128), 12 - 2 * g, 2), own)
        put(l0.r, 4 + 8 * g, jnp.concatenate([own, v[:, 8:]], axis=1))
    edges0 = Wide(6, 8, l0.r, 0, 2)
    edges0.start()

    for copy in third_right:
        copy.wait_recv()

    downward(l3)

    def body(i):
        l4.put(l4.f, i, 0.125 * both(both(both(l3.get(l3.r, i), 1, 2), 1, 1), 4, 2))

    l3.loop(body)
    solve_theta, solve_steps = SOLVE
    init_down(l4, solve_theta)
    w, w_next = l4.wa, l4.wb
    for n, (alpha, beta) in enumerate(solve_steps):
        step(l4, w, w_next, alpha, beta, last=n == len(solve_steps) - 1)
        w, w_next = w_next, w
    upward(l3, lambda i: l4.get(l4.x, i))

    for q in range(6):
        v = l3.x[pl.ds(pl.multiple_of(lax.rem(4 * k + q + 31, 32) * 8, 8), 8), :].reshape(1, 8, 128)
        for z in range(4):
            moved = v
            for u in range(4):
                if u != z:
                    moved = jnp.where(t == u, roll(v, u - z, 2), moved)
            first = (4 * q + z) * 16
            eb2[pl.ds(first, 8, stride=2), :] = moved.reshape(8, 128)
            eb2[pl.ds(first + 1, 8, stride=2), :] = moved.reshape(8, 128)

    def twice(ref, offset):
        def chunk(i):
            v = slots(ref, i * 4 + offset, 4)
            return jnp.broadcast_to(v[:, None], (4, 2, 16, 128)).reshape(8, 16, 128)

        return chunk

    upward(l2, twice(eb2, 0))

    for i, from_y in ((0, 0), (1, 1), (2, 2), (3, 3), (6, 14), (7, 15)):
        v = l2.x[pl.ds(lax.rem(2 * j + from_y, 16), 48, stride=16), :]
        eb1[pl.ds(2 * i, 48, stride=16), :] = v
        eb1[pl.ds(2 * i + 1, 48, stride=16), :] = v
    edges1.finish()
    upward(l1, twice(eb1, 6))
    edges = Wide(7, 4, l1.x, 0, 2)
    edges.start()
    edges0.finish()
    edges.finish()

    source = lax.broadcasted_iota(jnp.int32, (128, 128), 0)
    target = lax.broadcasted_iota(jnp.int32, (128, 128), 1)
    hit = (source // 32 == (target % 64) // 16) & (source % 32 == 4 * b - 2 + (target % 16) // 2)
    v = slots(l1.x, 0, 72)
    v = jnp.where(sub < 6, v[:, :8], v[:, 8:]).reshape(576, 128)
    v = jnp.dot(v, jnp.where(hit, 1.0, 0.0).astype(F32), precision=HIGHEST, preferred_element_type=F32)
    eb0[pl.ds(0, 576, stride=2), :] = v
    eb0[pl.ds(1, 576, stride=2), :] = v

    def top_chunk(i):
        v = jnp.where(lane16 < 64, slots(eb0, i * 4 + 2, 4), slots(eb0, i * 4 + 34, 4))
        return jnp.broadcast_to(v[:, None], (4, 2, 16, 128)).reshape(8, 16, 128)

    upward(l0, top_chunk)

    for y in range(0, 8, 2):
        first = l0.x[pl.ds(64 + y, 64, stride=16), :]
        second = l0.x[pl.ds(65 + y, 64, stride=16), :]
        low = jnp.where(half_lane, first, pltpu.roll(second, 64, 1))
        high = jnp.where(half_lane, pltpu.roll(first, 64, 1), second)
        turned = pltpu.roll(jnp.concatenate([low, high], axis=0), 124, 1).T
        for d in range(2):
            for v in range(4):
                start = d * 64 + v * 16
                out_ref[pl.ds(v * 64 + y + d, 8, stride=8), :] = turned[start:start + 8]

    for copy in (strips[4:] + [faces_first, right_first] + faces_second + right_second + rx + faces_z + right_z + faces_y
                 + right_y + third_faces + third_right):
        copy.wait_send()


def solution(mesh):
    def per_device(right_side, affinity):
        nx = affinity.shape[1] * mesh.shape["gx"]
        ny = affinity.shape[2] * mesh.shape["gy"]
        nz = affinity.shape[3] * mesh.shape["gz"]
        scratch = []
        for z, rows, *_ in LEVELS:
            scratch += level_shapes(z, rows)
        scratch += [pltpu.VMEM(shape, F32) for shape in (
            (4, 16, 8, 128), (4, 16, 8, 128),
            (8, 2, 4, 64, 128), (8, 2, 4, 64, 128), (8, 2, 32, 128), (8, 2, 3, 32, 128),
            (256, 128), (512, 128), (8, 32, 128), (8, 64, 128), (2, 64, 128), (2, 64, 128),
            (48, 128), (96, 128), (8, 48, 128), (8, 96, 128), (384, 128), (768, 128), (1152, 128))]
        dma = pltpu.SemaphoreType.DMA
        scratch += [dma(shape) for shape in (
            (2,), (6,), (6,), (8, 8), (8, 8), (2, 4), (2, 4), (2,), (2,), (3, 2), (3, 2), (2, 8), (2, 8), (3, 8), (3, 8))]
        out = pl.pallas_call(
            functools.partial(kernel, nx, ny, nz),
            out_shape=jax.ShapeDtypeStruct((256, 128), F32),
            in_specs=[pl.BlockSpec(memory_space=pl.ANY)] * 2,
            out_specs=pl.BlockSpec(memory_space=pltpu.VMEM),
            scratch_shapes=scratch,
            compiler_params=pltpu.CompilerParams(
                collective_id=0, has_side_effects=True, vmem_limit_bytes=60 * 1024 * 1024),
        )(right_side, affinity)
        return out.reshape(right_side.shape)

    spec = P(None, "gx", "gy", "gz")
    return jax.shard_map(per_device, mesh=mesh, in_specs=(spec, spec), out_specs=spec, check_vma=False)
```

```python
import functools

import jax
import jax.numpy as jnp
from jax import lax
from jax.experimental import pallas as pl
from jax.experimental.pallas import tpu as pltpu
from jax.sharding import PartitionSpec as P

MESH = pl.DeviceIdType.MESH
HIGHEST = lax.Precision.HIGHEST
F32 = jnp.float32

DEGREE = 3
COARSE_DEGREE = 8
SHIFT = 0.02
SMOOTH_LOWER = 0.5
UPPER = 2.0 + SHIFT


def cheb_coefs(a, b, m):
    theta, delta = 0.5 * (b + a), 0.5 * (b - a)
    sigma = theta / delta
    rho = 1.0 / sigma
    steps = []
    for _ in range(m - 1):
        nxt = 1.0 / (2.0 * sigma - rho)
        steps.append((nxt * rho, 2.0 * nxt / delta))
        rho = nxt
    return 1.0 / theta, steps


SMOOTH = cheb_coefs(SMOOTH_LOWER, UPPER, DEGREE)
SOLVE = cheb_coefs(SHIFT, UPPER, COARSE_DEGREE)


def iota(dim, shape=(1, 8, 128)):
    return lax.broadcasted_iota(jnp.int32, shape, dim)


def roll(x, shift, axis):
    shift = shift % x.shape[axis]
    return x if shift == 0 else pltpu.roll(x, shift, axis)


def both(x, k, axis):
    bit = (iota(axis, (1,) + x.shape[1:]) // k) % 2
    return x + jnp.where(bit == 0, roll(x, -k, axis), roll(x, k, axis))


def pick(x, k, axis, upper):
    bit = (iota(axis, (1,) + x.shape[1:]) // k) % 2
    if upper:
        return jnp.where(bit == 1, x, roll(x, -k, axis))
    return jnp.where(bit == 0, x, roll(x, k, axis))


def slots(ref, start, count, rows=16):
    if not isinstance(start, int):
        start = pl.multiple_of(start * rows, rows)
    else:
        start = start * rows
    return ref[pl.ds(start, count * rows), :].reshape(count, rows, 128)


def put(ref, start, value):
    count, rows = value.shape[:2]
    if not isinstance(start, int):
        start = pl.multiple_of(start * rows, rows)
    else:
        start = start * rows
    ref[pl.ds(start, count * rows), :] = value.reshape(count * rows, 128)


def loop(count, body):
    def run(i, carry):
        body(i)
        return carry

    lax.fori_loop(0, count, run, 0)


class Level:
    def __init__(self, z, rows, sy, sx, mode, refs):
        self.z, self.rows, self.sy, self.sx, self.mode = z, rows, sy, sx, mode
        self.ch = 128 // rows
        self.parts = z // self.ch if rows == 8 else 3
        (self.coef, self.scale, self.root, self.f, self.r, self.x, self.wa, self.wb, self.up, self.low,
         self.r_next, self.x_next) = refs

    def loop(self, body):
        def turn(i, carry):
            for part in range(self.parts):
                body(i * self.parts + part)
            return carry

        turns = self.z // (self.ch * self.parts)
        if turns == 1:
            turn(0, 0)
        else:
            lax.fori_loop(0, turns, turn, 0)

    def get(self, ref, i, offset=0):
        return slots(ref, i * self.ch + offset, self.ch, self.rows)

    def put(self, ref, i, value, offset=0):
        put(ref, i * self.ch + offset, value)


LEVELS = ((72, 16, 1, 1, 0), (72, 16, 1, 1, 0), (48, 16, 1, 2, 0), (32, 8, 1, 4, 1), (32, 8, 2, 8, 2))


def level_shapes(z, rows):
    n = z * rows
    pad = (z + 2) * rows
    return [pltpu.VMEM((6 * n, 128), F32)] + [pltpu.VMEM((n, 128), F32)] * 5 + [pltpu.VMEM((pad, 128), F32)] * 2 + [
        pltpu.VMEM((n, 128), F32)] * 4


def neighbours(lv, w_ref, i):
    w, before, after = lv.get(w_ref, i, 1), lv.get(w_ref, i, 0), lv.get(w_ref, i, 2)
    xd, xu = roll(w, lv.sx, 2), roll(w, -lv.sx, 2)
    yd, yu = roll(w, lv.sy, 1), roll(w, -lv.sy, 1)
    if lv.mode == 0:
        zd, zu = before, after
    else:
        s = lv.mode
        t = iota(2) % 4
        zu = jnp.where(t < 4 - s, roll(w, -s, 2), roll(after, 4 - s, 2))
        zd = jnp.where(t >= s, roll(w, s, 2), roll(before, s - 4, 2))
    return w, xd, xu, yd, yu, zd, zu


def init_down(lv, over_theta):
    def body(i):
        r = lv.get(lv.scale, i) * lv.get(lv.f, i)
        lv.put(lv.r, i, r)
        lv.put(lv.wa, i, r * over_theta, 1)

    lv.loop(body)


def init_up(lv, coarse_at):
    def body(i):
        lv.put(lv.wa, i, lv.get(lv.scale, i) * coarse_at(i), 1)

    lv.loop(body)


def step(lv, w_ref, w_next, alpha=None, beta=None, add="", last=False):
    def body(i):
        w, *near = neighbours(lv, w_ref, i)
        total = None
        for k, value in enumerate(near):
            term = slots(lv.coef, k * lv.z + i * lv.ch, lv.ch, lv.rows) * value
            total = term if total is None else total + term
        r = lv.get(lv.r, i) - ((1.0 + SHIFT) * w - total)
        if not last:
            lv.put(lv.r_next, i, r)
        if beta is None:
            return
        new = beta * r if alpha is None else alpha * w + beta * r
        if add:
            x = new + w if "w" in add else new
            if "x" in add:
                x = x + lv.get(lv.x, i)
            lv.put(lv.x_next, i, x * lv.get(lv.root, i) if last else x)
        if not last:
            lv.put(w_next, i, new, 1)

    lv.loop(body)
    if not last:
        lv.r, lv.r_next = lv.r_next, lv.r
    if add:
        lv.x, lv.x_next = lv.x_next, lv.x


def make_coefs(lv, group):
    g = (iota(2, (1, lv.rows, 128)) // group) % 4

    def spread(value, k):
        out = value
        for to in range(4):
            if to != k:
                out = jnp.where(g == to, roll(value, group * (to - k), 2), out)
        return out

    def body(i):
        low, up = lv.get(lv.low, i), lv.get(lv.up, i)
        faces = []
        for k in range(3):
            faces += [spread(low, k), spread(up, k)]
        total = faces[0] + faces[1] + faces[2] + faces[3] + faces[4] + faces[5]
        scale = jnp.where(total > 0.0, lax.rsqrt(total), 0.0)
        lv.put(lv.scale, i, scale)
        lv.put(lv.root, i, scale * total)
        square = scale * scale
        for k in range(6):
            put(lv.coef, k * lv.z + i * lv.ch, square * faces[k])

    lv.loop(body)


def own_pairs(ref, i):
    v = slots(ref, 4 + 32 * i, 32)[:, :8].reshape(16, 2, 8, 128)
    return v[:, 0], v[:, 1]


def coarse_faces(first, second, group, upper, ky, kx):
    g = (iota(2) // group) % 4
    v = jnp.where(g == 2, second if upper else first, first + second)
    v = jnp.where(g == 1, pick(v, ky, 1, upper), both(v, ky, 1))
    if kx is not None:
        v = jnp.where(g == 0, pick(v, kx, 2, upper), both(v, kx, 2))
    return v


def kernel(nx, ny, nz, f_hbm, a_hbm, out_ref, *scratch):
    refs = list(scratch)

    def take(count):
        got = refs[:count]
        del refs[:count]
        return got

    levels = [Level(*shape, take(12)) for shape in LEVELS]
    (fext, aext, ys, yr, zs, zr, tb, tmp, xg1, xgf, rxs, rxr, pz1, pzf, yg1, ygf, eb2, eb1, eb0) = take(19)
    (local_sem, strip_send, strip_recv, ex_send, ex_recv, xg_send, xg_recv, rx_send, rx_recv,
     pz_send, pz_recv, yg_send, yg_recv, zg_send, zg_recv) = take(15)
    l0, l1, l2, l3, l4 = levels

    b, j, k = lax.axis_index("gx"), lax.axis_index("gy"), lax.axis_index("gz")
    sub, lane, lane16 = iota(1), iota(2), iota(2, (1, 16, 128))
    lane2 = lax.broadcasted_iota(jnp.int32, (1, 128), 1)

    def remote(src, dst, send, recv, **to):
        return pltpu.make_async_remote_copy(
            src_ref=src, dst_ref=dst, send_sem=send, recv_sem=recv, device_id=to, device_id_type=MESH)

    own_f = pltpu.make_async_copy(f_hbm, fext.at[:, pl.ds(4, 8)], local_sem.at[0])
    own_a = pltpu.make_async_copy(a_hbm, aext.at[pl.ds(0, 3), pl.ds(4, 8)], local_sem.at[1])
    own_a.start()
    own_f.start()
    zr[...] = jnp.zeros_like(zr)

    barrier = pltpu.get_barrier_semaphore()
    partners = [{"gx": lax.rem(b + t, 8)} for t in (1, 2, 4, 6, 7)]
    partners += [{"gy": lax.rem(j + t, 8)} for t in range(1, 8)]
    partners += [{"gz": lax.rem(k + t, 8)} for t in range(1, 8)]
    partners += [{"gy": lax.rem(j + t, 8), "gz": lax.rem(k + u, 8)} for t in (1, 7) for u in (1, 7)]
    for to in partners:
        pl.semaphore_signal(barrier, inc=1, device_id=to, device_id_type=MESH)

    fext[:, 0] = jnp.zeros((4, 8, 128), F32)
    fext[:, 15] = jnp.zeros((4, 8, 128), F32)
    aext[3] = jnp.zeros((16, 8, 128), F32)
    for n in (1, 2):
        aext[n, 0] = jnp.zeros((8, 128), F32)
        aext[n, 15] = jnp.zeros((8, 128), F32)
    for ref in (l0.f, l0.wa, l1.f, l1.up, l1.low, eb1):
        ref[...] = jnp.zeros_like(ref)
    for lv in levels:
        for w in (lv.wa, lv.wb):
            w[pl.ds(0, lv.rows), :] = jnp.zeros((lv.rows, 128), F32)
            w[pl.ds((lv.z + 1) * lv.rows, lv.rows), :] = jnp.zeros((lv.rows, 128), F32)
    pl.semaphore_wait(barrier, len(partners))

    b_up, b_down = lax.rem(b + 1, 8), lax.rem(b + 7, 8)
    strips = [
        remote(a_hbm.at[:, pl.ds(5, 3)], aext.at[pl.ds(0, 3), pl.ds(1, 3)],
               strip_send.at[0], strip_recv.at[0], gx=b_up),
        remote(a_hbm.at[:, pl.ds(0, 3)], aext.at[pl.ds(0, 3), pl.ds(12, 3)],
               strip_send.at[1], strip_recv.at[1], gx=b_down),
        remote(a_hbm.at[0, 4], aext.at[0, 0], strip_send.at[4], strip_recv.at[4], gx=b_up),
        remote(a_hbm.at[0, 3], aext.at[0, 15], strip_send.at[5], strip_recv.at[5], gx=b_down),
        remote(f_hbm.at[:, pl.ds(5, 3)], fext.at[:, pl.ds(1, 3)],
               strip_send.at[2], strip_recv.at[2], gx=b_up),
        remote(f_hbm.at[:, pl.ds(0, 3)], fext.at[:, pl.ds(12, 3)],
               strip_send.at[3], strip_recv.at[3], gx=b_down),
    ]
    for copy in strips[:4]:
        copy.start()
    for copy in strips[:4]:
        copy.wait_send()
    for copy in strips[4:]:
        copy.start()

    class Wide:
        def __init__(self, n, block, ref, base, h):
            self.n, self.block, self.ref, self.base, self.h = n, block, ref, base, h
            rows, part = pl.ds(0, h), pl.ds(0, h * 8)
            j_up, j_down = jnp.minimum(j + 1, 7), jnp.maximum(j - 1, 0)
            k_to = (lax.rem(k + 1, 8), lax.rem(k + 7, 8))

            def make(src, dst, index, **to):
                return remote(src, dst, ex_send.at[n, index], ex_recv.at[n, index], **to)

            self.up = [make(ys.at[n, 0, rows], yr.at[n, 0, rows], 0, gy=j_up)]
            self.down = [make(ys.at[n, 1, rows], yr.at[n, 1, rows], 1, gy=j_down)]
            self.flat = []
            for dz in range(2):
                self.flat.append(make(zs.at[n, dz, part], zr.at[n, dz, 0, part], 2 + dz, gz=k_to[dz]))
                self.up.append(make(zs.at[n, dz, part], zr.at[n, dz, 1, part], 4 + dz, gy=j_up, gz=k_to[dz]))
                self.down.append(make(zs.at[n, dz, part], zr.at[n, dz, 2, part], 6 + dz, gy=j_down, gz=k_to[dz]))

        def start(self):
            n, block, ref, base, h = self.n, self.block, self.ref, self.base, self.h
            for i in range(h):
                ys[n, 0, i] = ref[pl.ds((base + 4) * 16 + block - h + i, 64, stride=16), :]
                ys[n, 1, i] = ref[pl.ds((base + 4) * 16 + i, 64, stride=16), :]
                zs[n, 0, pl.ds(i * 8, 8), :] = ref[pl.ds((base + 68 - h + i) * 16, 8), :]
                zs[n, 1, pl.ds(i * 8, 8), :] = ref[pl.ds((base + 4 + i) * 16, 8), :]

            @pl.when(j < 7)
            def _():
                for copy in self.up:
                    copy.start()

            @pl.when(j > 0)
            def _():
                for copy in self.down:
                    copy.start()

            for copy in self.flat:
                copy.start()

        def finish(self):
            n, block, ref, base, h = self.n, self.block, self.ref, self.base, self.h

            @pl.when(j > 0)
            def _():
                for copy in self.up:
                    copy.wait_recv()
                for i in range(h):
                    ref[pl.ds((base + 4) * 16 + 16 - h + i, 64, stride=16), :] = yr[n, 0, i]

            @pl.when(j < 7)
            def _():
                for copy in self.down:
                    copy.wait_recv()
                for i in range(h):
                    ref[pl.ds((base + 4) * 16 + block + i, 64, stride=16), :] = yr[n, 1, i]

            for copy in self.flat:
                copy.wait_recv()
            for dz in range(2):
                here, low, high = (zr[n, dz, m, pl.ds(0, h * 8), :].reshape(h, 8, 128) for m in range(3))
                if block == 8:
                    pair = [here, jnp.where(sub < 4, high, low)]
                else:
                    pair = [jnp.where(sub < 4, here, roll(high, 4, 1)), roll(low, 4, 1)]
                v = jnp.concatenate(pair, axis=1)
                if block == 8:
                    if dz == 0:
                        v = roll(jnp.where(lane16 < 64, slots(ref, base + 68 - h, h), v), 64, 2)
                    else:
                        v = roll(jnp.where(lane16 < 64, v, slots(ref, base + 4, h)), 64, 2)
                put(ref, base + (4 - h if dz == 0 else 68), v)

            @pl.when(j < 7)
            def _():
                for copy in self.up:
                    copy.wait_send()

            @pl.when(j > 0)
            def _():
                for copy in self.down:
                    copy.wait_send()

            for copy in self.flat:
                copy.wait_send()

    half_lane = lax.broadcasted_iota(jnp.int32, (64, 128), 1) < 64

    def to_tiles(src, dst, base):
        for y in range(0, 8, 2):
            rows = [src[pl.ds(y + d, 64, stride=8), :] for d in range(2)]
            turned = jnp.concatenate(rows, axis=0).T
            low, high = turned[:64], turned[64:]
            first = (base + 4) * 16 + y
            dst[pl.ds(first, 64, stride=16), :] = jnp.where(half_lane, low, pltpu.roll(high, 64, 1))
            dst[pl.ds(first + 1, 64, stride=16), :] = jnp.where(half_lane, pltpu.roll(low, 64, 1), high)

    fext_rows, aext_rows = fext.reshape(512, 128), aext.reshape(512, 128)

    def x_gather(xg, n):
        first = remote(xg.at[b], xg.at[b], xg_send.at[n, 0], xg_recv.at[n, 0], gx=b + 1 - 2 * lax.rem(b, 2))
        pair = pl.ds((b // 2) * 2, 2)
        second = [remote(xg.at[pair], xg.at[pair], xg_send.at[n, t], xg_recv.at[n, t], gx=lax.rem(b + 2 * t, 8))
                  for t in range(1, 4)]
        return first, second

    def x_pack(weight, xg, first, upper=None):
        source = lax.broadcasted_iota(jnp.int32, (128, 256), 0)
        target = lax.broadcasted_iota(jnp.int32, (128, 256), 1)
        slot, inner = source % 16, (target % 128) % 32
        hit = (source // 64 == target // 128) & ((source % 64) // 16 == (target % 128) // 32) & (inner < 4)
        pair = (slot // 2 == inner + 2) & hit
        if upper is not None:
            pair = pair & (((source % 64) // 16 != 0) | (slot % 2 == (1 if upper else 0)))
        matrix = jnp.where(pair, weight, 0.0).astype(F32)
        moved = jnp.dot(tb[...], matrix, precision=HIGHEST, preferred_element_type=F32)
        parts = [moved[:, :128].reshape(32, 8, 128), moved[:, 128:].reshape(32, 8, 128)]
        total = None
        for g in range(8):
            part = roll(parts[g // 4][(g % 4) * 8:(g % 4) * 8 + 8], 4 * g, 2)
            total = part if total is None else total + part
        packed = jnp.where(sub % 2 == 0, total[:4], total[4:])
        xg[b, pl.ds(first * 8, 32), :] = packed.reshape(32, 128)

    def x_unpack(xg, first, dst):
        g = (lane // 4) % 8
        for q in range(4):
            for odd in range(2):
                v = []
                for n in range(8):
                    tile = xg[n, pl.ds((first + q) * 8, 8), :].reshape(1, 8, 128)
                    v.append(jnp.where(sub % 2 == 1, tile, roll(tile, -1, 1)) if odd
                             else jnp.where(sub % 2 == 0, tile, roll(tile, 1, 1)))
                for s in (1, 2, 4):
                    high = (g // s) % 2 == 1
                    for n in range(8):
                        if n & s == 0:
                            lo, hi = v[n], v[n + s]
                            v[n] = jnp.where(high, roll(hi, 4 * s, 2), lo)
                            v[n + s] = jnp.where(high, hi, roll(lo, -4 * s, 2))
                for n in range(8):
                    put(tmp, n * 8 + 4 * odd + q, v[n])
        for i in range(4):
            dst[pl.ds(64 + i, 64, stride=16), :] = tmp[pl.ds(2 * i, 64, stride=8), :]

    own_a.wait()
    for copy in strips[:4]:
        copy.wait_recv()
    to_tiles(aext_rows, l0.wa, 1)
    edges = Wide(0, 8, l0.wa, 1, 4)
    edges.start()
    edges.finish()
    group0 = (lane16 // 16) % 4
    row16 = iota(1, (1, 16, 128))
    x_at = 8 * b + lane16 % 16 - 4
    y_at = 8 * j + jnp.where(row16 < 12, row16, row16 - 16)

    def face_body(i):
        a, xd, xu, yd, yu, zd, zu = neighbours(l0, l0.wa, i)
        z_at = 128 * k + 64 * (iota(2, a.shape) // 64) + i * l0.ch - 4 + iota(0, a.shape)
        side_up = jnp.where(group0 == 0, xu, jnp.where(group0 == 1, yu, zu))
        side_low = jnp.where(group0 == 0, xd, jnp.where(group0 == 1, yd, zd))
        where = jnp.where(group0 == 0, x_at, jnp.where(group0 == 1, y_at, z_at))
        end = jnp.where(group0 == 0, nx - 1, jnp.where(group0 == 1, ny - 1, nz - 1))
        l0.put(l0.up, i, jnp.where(where == end, 0.0, 0.5 * (a + side_up)))
        l0.put(l0.low, i, jnp.where(where == 0, 0.0, 0.5 * (a + side_low)))

    l0.loop(face_body)

    own_f.wait()
    for copy in strips[4:]:
        copy.wait_recv()
    to_tiles(fext_rows, l0.f, 0)
    edges = Wide(1, 8, l0.f, 0, 3)
    edges.start()
    for upper, ref in ((True, l0.up), (False, l0.low)):
        def body(i, ref=ref, upper=upper):
            put(tb, i * 16, coarse_faces(*own_pairs(ref, i), 16, upper, 1, None))

        loop(2, body)
        x_pack(0.25, xgf, 0 if upper else 4, upper)
    faces_first, faces_second = x_gather(xgf, 1)
    faces_first.start()
    make_coefs(l0, 16)

    edges.finish()

    over_theta, ((a1, b1), (a2, b2)) = SMOOTH

    def downward(lv):
        init_down(lv, over_theta)
        step(lv, lv.wa, lv.wb, a1, b1, add="w")
        step(lv, lv.wb, lv.wa, a2, b2, add="x")
        step(lv, lv.wa, None)

    def upward(lv, coarse_at):
        init_up(lv, coarse_at)
        step(lv, lv.wa, lv.wb, None, over_theta, add="xw")
        step(lv, lv.wb, lv.wa, a1, b1)
        step(lv, lv.wa, None, a2, b2, add="xw", last=True)

    def own_sums(lv, i):
        pairs, roots = own_pairs(lv.r, i), own_pairs(lv.root, i)
        return pairs[0] * roots[0] + pairs[1] * roots[1]

    downward(l0)

    def body(i):
        put(tb, i * 16, both(own_sums(l0, i), 1, 1))

    loop(2, body)
    x_pack(0.125, xg1, 0)
    right_first, right_second = x_gather(xg1, 0)
    right_first.start()
    faces_first.wait_recv()
    for copy in faces_second:
        copy.start()

    slot = lane % 16
    for side, first in ((0, 10), (1, 4)):
        packed = jnp.zeros((8, 8, 128), F32)
        for g in range(8):
            v = slots(l0.r, 4 + 8 * g, 8)[:, :8]
            packed = jnp.where(slot // 2 == g, roll(v, 2 * g - first, 2), packed)
        rxs[side] = packed.reshape(64, 128)
    rx = [remote(rxs.at[0], rxr.at[0], rx_send.at[0], rx_recv.at[0], gx=b_up),
          remote(rxs.at[1], rxr.at[1], rx_send.at[1], rx_recv.at[1], gx=b_down)]
    for copy in rx:
        copy.start()

    for copy in faces_second:
        copy.wait_recv()
    x_unpack(xgf, 0, l1.up)
    x_unpack(xgf, 4, l1.low)
    edges_up, edges_low = Wide(2, 4, l1.up, 0, 3), Wide(3, 4, l1.low, 0, 3)
    edges_up.start()
    edges_low.start()

    def second_pack(pz, first):
        v = jnp.where(lane2 % 2 == 0, tb[pl.ds(0, 32, stride=8), :], tb[pl.ds(2, 32, stride=8), :])
        pz[pl.ds(first + 8, 32), :] = v

    def second_edges(pz, first, n):
        up, down = pl.ds(first + 32, 8), pl.ds(first + 8, 8)
        return [remote(pz.at[up], pz.at[pl.ds(first, 8)], pz_send.at[n, 0], pz_recv.at[n, 0], gz=lax.rem(k + 1, 8)),
                remote(pz.at[down], pz.at[pl.ds(first + 40, 8)], pz_send.at[n, 1], pz_recv.at[n, 1],
                       gz=lax.rem(k + 7, 8))]

    def y_gather(pz, yg, n):
        return [remote(pz, yg.at[j], yg_send.at[n, t], yg_recv.at[n, t], gy=lax.rem(j + t, 8)) for t in range(1, 8)]

    def second_unpack(yg, first, dst):
        for n in range(8):
            v = yg[n, pl.ds(first, 48), :]
            dst[pl.ds(2 * n, 48, stride=16), :] = jnp.where(lane2 % 2 == 0, v, roll(v, 1, 1))
            dst[pl.ds(2 * n + 1, 48, stride=16), :] = jnp.where(lane2 % 2 == 1, v, roll(v, -1, 1))

    for upper, ref in ((True, l1.up), (False, l1.low)):
        def body(i, ref=ref, upper=upper):
            put(tb, i * 16, 0.25 * coarse_faces(*own_pairs(ref, i), 32, upper, 1, 1))

        loop(2, body)
        second_pack(pzf, 0 if upper else 48)
    faces_z = second_edges(pzf, 0, 0) + second_edges(pzf, 48, 1)
    for copy in faces_z:
        copy.start()
    edges_up.finish()
    edges_low.finish()
    right_first.wait_recv()
    for copy in right_second:
        copy.start()
    make_coefs(l1, 32)
    for copy in faces_z:
        copy.wait_recv()
    ygf[j] = pzf[...]
    faces_y = y_gather(pzf, ygf, 0)
    for copy in faces_y:
        copy.start()

    for copy in right_second:
        copy.wait_recv()
    x_unpack(xg1, 0, l1.f)
    edges = Wide(4, 4, l1.f, 0, 3)
    edges.start()
    edges.finish()
    downward(l1)

    def body(i):
        put(tb, i * 16, 0.125 * both(both(own_sums(l1, i), 1, 1), 1, 2))

    loop(2, body)
    second_pack(pz1, 0)
    right_z = second_edges(pz1, 0, 2)
    for copy in right_z:
        copy.start()
    edges1 = Wide(5, 4, l1.r, 0, 2)
    edges1.start()

    for copy in faces_y:
        copy.wait_recv()
    second_unpack(ygf, 0, l2.up)
    second_unpack(ygf, 48, l2.low)

    t = lane % 4

    def third(ref, upper=None):
        even, odd = (ref[pl.ds(128 + d, 256, stride=2), :].reshape(16, 2, 8, 128) for d in range(2))
        if upper is None:
            roots = [l2.root[pl.ds(128 + d, 256, stride=2), :].reshape(16, 2, 8, 128) for d in range(2)]
            v = even * roots[0] + odd * roots[1]
            v = 0.125 * both(v[:, 0] + v[:, 1], 2, 2)
        else:
            g = lane // 32
            side = odd if upper else even
            first, second = (jnp.where(g == 1, side[:, d], even[:, d] + odd[:, d]) for d in range(2))
            v = jnp.where(g == 2, second if upper else first, first + second)
            v = 0.25 * jnp.where(g == 0, pick(v, 2, 2, upper), both(v, 2, 2))
        v = v.reshape(4, 4, 8, 128)
        out = v[:, 0]
        for u in range(1, 4):
            out = jnp.where(t == u, v[:, u], out)
        return out

    def z_gather(g, n):
        rows = pl.ds(pl.multiple_of(k * 32, 8), 32)
        return [remote(g.at[rows], g.at[rows], zg_send.at[n, u], zg_recv.at[n, u], gz=lax.rem(k + u, 8))
                for u in range(1, 8)]

    put(l3.up, 4 * k, third(l2.up, True))
    put(l3.low, 4 * k, third(l2.low, False))
    third_faces = z_gather(l3.up, 0) + z_gather(l3.low, 1)

    for copy in right_z:
        copy.wait_recv()
    yg1[j] = pz1[...]
    right_y = y_gather(pz1, yg1, 1)
    for copy in right_y:
        copy.start()
    for copy in third_faces:
        copy.start()
    make_coefs(l2, 32)
    for copy in third_faces:
        copy.wait_recv()
    make_coefs(l3, 32)
    for upper in (True, False):
        src, dst = (l3.up, l4.up) if upper else (l3.low, l4.low)

        def body(i, src=src, dst=dst, upper=upper):
            g = lane // 32
            v = l3.get(src, i)
            v = jnp.where(g == 2, pick(v, 1, 2, upper), both(v, 1, 2))
            v = jnp.where(g == 1, pick(v, 1, 1, upper), both(v, 1, 1))
            l4.put(dst, i, 0.25 * jnp.where(g == 0, pick(v, 4, 2, upper), both(v, 4, 2)))

        l3.loop(body)
    make_coefs(l4, 32)
    for copy in right_y:
        copy.wait_recv()
    second_unpack(yg1, 0, l2.f)
    downward(l2)
    put(l3.f, 4 * k, third(l2.r))
    third_right = z_gather(l3.f, 2)
    for copy in third_right:
        copy.start()

    for copy in rx:
        copy.wait_recv()
    for g in range(8):
        v = slots(l0.r, 4 + 8 * g, 8)
        own = v[:, :8]
        own = jnp.where(slot // 2 == 1, roll(rxr[0].reshape(8, 8, 128), 2 - 2 * g, 2), own)
        own = jnp.where(slot // 2 == 6, roll(rxr[1].reshape(8, 8, 128), 12 - 2 * g, 2), own)
        put(l0.r, 4 + 8 * g, jnp.concatenate([own, v[:, 8:]], axis=1))
    edges0 = Wide(6, 8, l0.r, 0, 2)
    edges0.start()

    for copy in third_right:
        copy.wait_recv()

    downward(l3)

    def body(i):
        l4.put(l4.f, i, 0.125 * both(both(both(l3.get(l3.r, i) * l3.get(l3.root, i), 1, 2), 1, 1), 4, 2))

    l3.loop(body)
    solve_theta, solve_steps = SOLVE
    init_down(l4, solve_theta)
    w, w_next = l4.wa, l4.wb
    for n, (alpha, beta) in enumerate(solve_steps):
        step(l4, w, w_next, alpha, beta, add="x" if n else "w", last=n == len(solve_steps) - 1)
        w, w_next = w_next, w
    upward(l3, lambda i: l4.get(l4.x, i))

    for q in range(6):
        v = l3.x[pl.ds(pl.multiple_of(lax.rem(4 * k + q + 31, 32) * 8, 8), 8), :].reshape(1, 8, 128)
        for z in range(4):
            moved = v
            for u in range(4):
                if u != z:
                    moved = jnp.where(t == u, roll(v, u - z, 2), moved)
            first = (4 * q + z) * 16
            eb2[pl.ds(first, 8, stride=2), :] = moved.reshape(8, 128)
            eb2[pl.ds(first + 1, 8, stride=2), :] = moved.reshape(8, 128)

    def twice(ref, offset):
        def chunk(i):
            v = slots(ref, i * 4 + offset, 4)
            return jnp.broadcast_to(v[:, None], (4, 2, 16, 128)).reshape(8, 16, 128)

        return chunk

    upward(l2, twice(eb2, 0))

    for i, from_y in ((0, 0), (1, 1), (2, 2), (3, 3), (6, 14), (7, 15)):
        v = l2.x[pl.ds(lax.rem(2 * j + from_y, 16), 48, stride=16), :]
        eb1[pl.ds(2 * i, 48, stride=16), :] = v
        eb1[pl.ds(2 * i + 1, 48, stride=16), :] = v
    edges1.finish()
    upward(l1, twice(eb1, 6))
    edges = Wide(7, 4, l1.x, 0, 2)
    edges.start()
    edges0.finish()
    edges.finish()

    source = lax.broadcasted_iota(jnp.int32, (128, 128), 0)
    target = lax.broadcasted_iota(jnp.int32, (128, 128), 1)
    hit = (source // 32 == (target % 64) // 16) & (source % 32 == 4 * b - 2 + (target % 16) // 2)
    v = slots(l1.x, 0, 72)
    v = jnp.where(sub < 6, v[:, :8], v[:, 8:]).reshape(576, 128)
    v = jnp.dot(v, jnp.where(hit, 1.0, 0.0).astype(F32), precision=HIGHEST, preferred_element_type=F32)
    eb0[pl.ds(0, 576, stride=2), :] = v
    eb0[pl.ds(1, 576, stride=2), :] = v

    def top_chunk(i):
        v = jnp.where(lane16 < 64, slots(eb0, i * 4 + 2, 4), slots(eb0, i * 4 + 34, 4))
        return jnp.broadcast_to(v[:, None], (4, 2, 16, 128)).reshape(8, 16, 128)

    upward(l0, top_chunk)

    for y in range(0, 8, 2):
        first = l0.x[pl.ds(64 + y, 64, stride=16), :]
        second = l0.x[pl.ds(65 + y, 64, stride=16), :]
        low = jnp.where(half_lane, first, pltpu.roll(second, 64, 1))
        high = jnp.where(half_lane, pltpu.roll(first, 64, 1), second)
        turned = pltpu.roll(jnp.concatenate([low, high], axis=0), 124, 1).T
        for d in range(2):
            for v in range(4):
                start = d * 64 + v * 16
                out_ref[pl.ds(v * 64 + y + d, 8, stride=8), :] = turned[start:start + 8]

    for copy in (strips[4:] + [faces_first, right_first] + faces_second + right_second + rx + faces_z + right_z + faces_y
                 + right_y + third_faces + third_right):
        copy.wait_send()


def solution(mesh):
    def per_device(right_side, affinity):
        nx = affinity.shape[1] * mesh.shape["gx"]
        ny = affinity.shape[2] * mesh.shape["gy"]
        nz = affinity.shape[3] * mesh.shape["gz"]
        scratch = []
        for z, rows, *_ in LEVELS:
            scratch += level_shapes(z, rows)
        scratch += [pltpu.VMEM(shape, F32) for shape in (
            (4, 16, 8, 128), (4, 16, 8, 128),
            (8, 2, 4, 64, 128), (8, 2, 4, 64, 128), (8, 2, 32, 128), (8, 2, 3, 32, 128),
            (256, 128), (512, 128), (8, 32, 128), (8, 64, 128), (2, 64, 128), (2, 64, 128),
            (48, 128), (96, 128), (8, 48, 128), (8, 96, 128), (384, 128), (768, 128), (1152, 128))]
        dma = pltpu.SemaphoreType.DMA
        scratch += [dma(shape) for shape in (
            (2,), (6,), (6,), (8, 8), (8, 8), (2, 4), (2, 4), (2,), (2,), (3, 2), (3, 2), (2, 8), (2, 8), (3, 8), (3, 8))]
        out = pl.pallas_call(
            functools.partial(kernel, nx, ny, nz),
            out_shape=jax.ShapeDtypeStruct((256, 128), F32),
            in_specs=[pl.BlockSpec(memory_space=pl.ANY)] * 2,
            out_specs=pl.BlockSpec(memory_space=pltpu.VMEM),
            scratch_shapes=scratch,
            compiler_params=pltpu.CompilerParams(
                collective_id=0, has_side_effects=True, vmem_limit_bytes=60 * 1024 * 1024),
        )(right_side, affinity)
        return out.reshape(right_side.shape)

    spec = P(None, "gx", "gy", "gz")
    return jax.shard_map(per_device, mesh=mesh, in_specs=(spec, spec), out_specs=spec, check_vma=False)
```

```python
import functools

import jax
import jax.numpy as jnp
from jax import lax
from jax.experimental import pallas as pl
from jax.experimental.pallas import tpu as pltpu
from jax.sharding import PartitionSpec as P

MESH = pl.DeviceIdType.MESH
HIGHEST = lax.Precision.HIGHEST
F32 = jnp.float32

DEGREE = 3
COARSE_DEGREE = 8
SHIFT = 0.02
SMOOTH_LOWER = 0.5
UPPER = 2.0 + SHIFT


def cheb_coefs(a, b, m):
    theta, delta = 0.5 * (b + a), 0.5 * (b - a)
    sigma = theta / delta
    rho = 1.0 / sigma
    steps = []
    for _ in range(m - 1):
        nxt = 1.0 / (2.0 * sigma - rho)
        steps.append((nxt * rho, 2.0 * nxt / delta))
        rho = nxt
    return 1.0 / theta, steps


SMOOTH = cheb_coefs(SMOOTH_LOWER, UPPER, DEGREE)
SOLVE = cheb_coefs(SHIFT, UPPER, COARSE_DEGREE)


def iota(dim, shape=(1, 8, 128)):
    return lax.broadcasted_iota(jnp.int32, shape, dim)


def roll(x, shift, axis):
    shift = shift % x.shape[axis]
    return x if shift == 0 else pltpu.roll(x, shift, axis)


def both(x, k, axis):
    bit = (iota(axis, (1,) + x.shape[1:]) // k) % 2
    return x + jnp.where(bit == 0, roll(x, -k, axis), roll(x, k, axis))


def pick(x, k, axis, upper):
    bit = (iota(axis, (1,) + x.shape[1:]) // k) % 2
    if upper:
        return jnp.where(bit == 1, x, roll(x, -k, axis))
    return jnp.where(bit == 0, x, roll(x, k, axis))


def slots(ref, start, count, rows=16):
    if not isinstance(start, int):
        start = pl.multiple_of(start * rows, rows)
    else:
        start = start * rows
    return ref[pl.ds(start, count * rows), :].reshape(count, rows, 128)


def put(ref, start, value):
    count, rows = value.shape[:2]
    if not isinstance(start, int):
        start = pl.multiple_of(start * rows, rows)
    else:
        start = start * rows
    ref[pl.ds(start, count * rows), :] = value.reshape(count * rows, 128)


def loop(count, body):
    def run(i, carry):
        body(i)
        return carry

    lax.fori_loop(0, count, run, 0)


class Level:
    def __init__(self, z, rows, sy, sx, mode, refs):
        self.z, self.rows, self.sy, self.sx, self.mode = z, rows, sy, sx, mode
        self.ch = 128 // rows
        self.parts = z // self.ch if rows == 8 else 3
        (self.coef, self.scale, self.root, self.f, self.r, self.x, self.wa, self.wb, self.up, self.low,
         self.r_next, self.x_next) = refs

    def loop(self, body):
        def turn(i, carry):
            for part in range(self.parts):
                body(i * self.parts + part)
            return carry

        turns = self.z // (self.ch * self.parts)
        if turns == 1:
            turn(0, 0)
        else:
            lax.fori_loop(0, turns, turn, 0)

    def get(self, ref, i, offset=0):
        return slots(ref, i * self.ch + offset, self.ch, self.rows)

    def put(self, ref, i, value, offset=0):
        put(ref, i * self.ch + offset, value)


LEVELS = ((72, 16, 1, 1, 0), (72, 16, 1, 1, 0), (48, 16, 1, 2, 0), (32, 8, 1, 4, 1), (32, 8, 2, 8, 2))


def level_shapes(z, rows):
    n = z * rows
    pad = (z + 2) * rows
    return [pltpu.VMEM((6 * n, 128), F32)] + [pltpu.VMEM((n, 128), F32)] * 5 + [pltpu.VMEM((pad, 128), F32)] * 2 + [
        pltpu.VMEM((n, 128), F32)] * 4


def neighbours(lv, w_ref, i):
    w, before, after = lv.get(w_ref, i, 1), lv.get(w_ref, i, 0), lv.get(w_ref, i, 2)
    xd, xu = roll(w, lv.sx, 2), roll(w, -lv.sx, 2)
    yd, yu = roll(w, lv.sy, 1), roll(w, -lv.sy, 1)
    if lv.mode == 0:
        zd, zu = before, after
    else:
        s = lv.mode
        t = iota(2) % 4
        zu = jnp.where(t < 4 - s, roll(w, -s, 2), roll(after, 4 - s, 2))
        zd = jnp.where(t >= s, roll(w, s, 2), roll(before, s - 4, 2))
    return w, xd, xu, yd, yu, zd, zu


def init_down(lv, over_theta):
    def body(i):
        r = lv.get(lv.scale, i) * lv.get(lv.f, i)
        lv.put(lv.r, i, r)
        lv.put(lv.wa, i, r * over_theta, 1)

    lv.loop(body)


def init_up(lv, coarse_at):
    def body(i):
        lv.put(lv.wa, i, lv.get(lv.scale, i) * coarse_at(i), 1)

    lv.loop(body)


def step(lv, w_ref, w_next, alpha=None, beta=None, add="", last=False):
    def body(i):
        w, *near = neighbours(lv, w_ref, i)
        total = None
        for k, value in enumerate(near):
            term = slots(lv.coef, k * lv.z + i * lv.ch, lv.ch, lv.rows) * value
            total = term if total is None else total + term
        r = lv.get(lv.r, i) - ((1.0 + SHIFT) * w - total)
        if not last:
            lv.put(lv.r_next, i, r)
        if beta is None:
            return
        new = beta * r if alpha is None else alpha * w + beta * r
        if add:
            x = new + w if "w" in add else new
            if "x" in add:
                x = x + lv.get(lv.x, i)
            lv.put(lv.x_next, i, x * lv.get(lv.root, i) if last else x)
        if not last:
            lv.put(w_next, i, new, 1)

    lv.loop(body)
    if not last:
        lv.r, lv.r_next = lv.r_next, lv.r
    if add:
        lv.x, lv.x_next = lv.x_next, lv.x


def make_coefs(lv, group):
    g = (iota(2, (1, lv.rows, 128)) // group) % 4

    def spread(value, k):
        out = value
        for to in range(4):
            if to != k:
                out = jnp.where(g == to, roll(value, group * (to - k), 2), out)
        return out

    def body(i):
        low, up = lv.get(lv.low, i), lv.get(lv.up, i)
        faces = []
        for k in range(3):
            faces += [spread(low, k), spread(up, k)]
        total = faces[0] + faces[1] + faces[2] + faces[3] + faces[4] + faces[5]
        scale = jnp.where(total > 0.0, lax.rsqrt(total), 0.0)
        lv.put(lv.scale, i, scale)
        lv.put(lv.root, i, scale * total)
        square = scale * scale
        for k in range(6):
            put(lv.coef, k * lv.z + i * lv.ch, square * faces[k])

    lv.loop(body)


def own_pairs(ref, i):
    v = slots(ref, 4 + 32 * i, 32)[:, :8].reshape(16, 2, 8, 128)
    return v[:, 0], v[:, 1]


def coarse_faces(first, second, group, upper, ky, kx):
    g = (iota(2) // group) % 4
    v = jnp.where(g == 2, second if upper else first, first + second)
    v = jnp.where(g == 1, pick(v, ky, 1, upper), both(v, ky, 1))
    if kx is not None:
        v = jnp.where(g == 0, pick(v, kx, 2, upper), both(v, kx, 2))
    return v


def kernel(nx, ny, nz, f_hbm, a_hbm, out_ref, *scratch):
    refs = list(scratch)

    def take(count):
        got = refs[:count]
        del refs[:count]
        return got

    levels = [Level(*shape, take(12)) for shape in LEVELS]
    (fext, aext, ys, yr, zs, zr, tb, tmp, xg1, xgf, rxs, rxr, q1, qf, yg1, ygf, zh1, zhf, eb2, eb1, eb0) = take(21)
    (local_sem, strip_send, strip_recv, ex_send, ex_recv, xg_send, xg_recv, rx_send, rx_recv,
     h_send, h_recv, yg_send, yg_recv, yc_send, yc_recv, zg_send, zg_recv) = take(17)
    l0, l1, l2, l3, l4 = levels

    b, j, k = lax.axis_index("gx"), lax.axis_index("gy"), lax.axis_index("gz")
    sub, lane, lane16 = iota(1), iota(2), iota(2, (1, 16, 128))
    lane2 = lax.broadcasted_iota(jnp.int32, (1, 128), 1)

    def remote(src, dst, send, recv, **to):
        return pltpu.make_async_remote_copy(
            src_ref=src, dst_ref=dst, send_sem=send, recv_sem=recv, device_id=to, device_id_type=MESH)

    own_f = pltpu.make_async_copy(f_hbm, fext.at[:, pl.ds(4, 8)], local_sem.at[0])
    own_a = pltpu.make_async_copy(a_hbm, aext.at[pl.ds(0, 3), pl.ds(4, 8)], local_sem.at[1])
    own_a.start()
    own_f.start()
    zr[...] = jnp.zeros_like(zr)

    barrier = pltpu.get_barrier_semaphore()
    partners = [{"gx": lax.rem(b + t, 8)} for t in (1, 2, 4, 6, 7)]
    partners += [{"gy": lax.rem(j + t, 8)} for t in range(1, 8)]
    partners += [{"gz": lax.rem(k + t, 8)} for t in range(1, 8)]
    partners += [{"gy": lax.rem(j + t, 8), "gz": lax.rem(k + u, 8)} for t in (1, 7) for u in (1, 7)]
    for to in partners:
        pl.semaphore_signal(barrier, inc=1, device_id=to, device_id_type=MESH)

    fext[:, 0] = jnp.zeros((4, 8, 128), F32)
    fext[:, 15] = jnp.zeros((4, 8, 128), F32)
    aext[3] = jnp.zeros((16, 8, 128), F32)
    for n in (1, 2):
        aext[n, 0] = jnp.zeros((8, 128), F32)
        aext[n, 15] = jnp.zeros((8, 128), F32)
    for ref in (l0.f, l0.wa, l1.f, l1.up, l1.low, eb1):
        ref[...] = jnp.zeros_like(ref)
    for lv in levels:
        for w in (lv.wa, lv.wb):
            w[pl.ds(0, lv.rows), :] = jnp.zeros((lv.rows, 128), F32)
            w[pl.ds((lv.z + 1) * lv.rows, lv.rows), :] = jnp.zeros((lv.rows, 128), F32)
    pl.semaphore_wait(barrier, len(partners))

    b_up, b_down = lax.rem(b + 1, 8), lax.rem(b + 7, 8)
    strips = [
        remote(a_hbm.at[:, pl.ds(5, 3)], aext.at[pl.ds(0, 3), pl.ds(1, 3)],
               strip_send.at[0], strip_recv.at[0], gx=b_up),
        remote(a_hbm.at[:, pl.ds(0, 3)], aext.at[pl.ds(0, 3), pl.ds(12, 3)],
               strip_send.at[1], strip_recv.at[1], gx=b_down),
        remote(a_hbm.at[0, 4], aext.at[0, 0], strip_send.at[4], strip_recv.at[4], gx=b_up),
        remote(a_hbm.at[0, 3], aext.at[0, 15], strip_send.at[5], strip_recv.at[5], gx=b_down),
        remote(f_hbm.at[:, pl.ds(5, 3)], fext.at[:, pl.ds(1, 3)],
               strip_send.at[2], strip_recv.at[2], gx=b_up),
        remote(f_hbm.at[:, pl.ds(0, 3)], fext.at[:, pl.ds(12, 3)],
               strip_send.at[3], strip_recv.at[3], gx=b_down),
    ]
    for copy in strips[:4]:
        copy.start()
    for copy in strips[:4]:
        copy.wait_send()
    for copy in strips[4:]:
        copy.start()

    class Wide:
        def __init__(self, n, block, ref, base, h):
            self.n, self.block, self.ref, self.base, self.h = n, block, ref, base, h
            rows, part = pl.ds(0, h), pl.ds(0, h * 8)
            j_up, j_down = jnp.minimum(j + 1, 7), jnp.maximum(j - 1, 0)
            k_to = (lax.rem(k + 1, 8), lax.rem(k + 7, 8))

            def make(src, dst, index, **to):
                return remote(src, dst, ex_send.at[n, index], ex_recv.at[n, index], **to)

            self.up = [make(ys.at[n, 0, rows], yr.at[n, 0, rows], 0, gy=j_up)]
            self.down = [make(ys.at[n, 1, rows], yr.at[n, 1, rows], 1, gy=j_down)]
            self.flat = []
            for dz in range(2):
                self.flat.append(make(zs.at[n, dz, part], zr.at[n, dz, 0, part], 2 + dz, gz=k_to[dz]))
                self.up.append(make(zs.at[n, dz, part], zr.at[n, dz, 1, part], 4 + dz, gy=j_up, gz=k_to[dz]))
                self.down.append(make(zs.at[n, dz, part], zr.at[n, dz, 2, part], 6 + dz, gy=j_down, gz=k_to[dz]))

        def start(self):
            n, block, ref, base, h = self.n, self.block, self.ref, self.base, self.h
            for i in range(h):
                ys[n, 0, i] = ref[pl.ds((base + 4) * 16 + block - h + i, 64, stride=16), :]
                ys[n, 1, i] = ref[pl.ds((base + 4) * 16 + i, 64, stride=16), :]
                zs[n, 0, pl.ds(i * 8, 8), :] = ref[pl.ds((base + 68 - h + i) * 16, 8), :]
                zs[n, 1, pl.ds(i * 8, 8), :] = ref[pl.ds((base + 4 + i) * 16, 8), :]

            @pl.when(j < 7)
            def _():
                for copy in self.up:
                    copy.start()

            @pl.when(j > 0)
            def _():
                for copy in self.down:
                    copy.start()

            for copy in self.flat:
                copy.start()

        def finish(self):
            n, block, ref, base, h = self.n, self.block, self.ref, self.base, self.h

            @pl.when(j > 0)
            def _():
                for copy in self.up:
                    copy.wait_recv()
                for i in range(h):
                    ref[pl.ds((base + 4) * 16 + 16 - h + i, 64, stride=16), :] = yr[n, 0, i]

            @pl.when(j < 7)
            def _():
                for copy in self.down:
                    copy.wait_recv()
                for i in range(h):
                    ref[pl.ds((base + 4) * 16 + block + i, 64, stride=16), :] = yr[n, 1, i]

            for copy in self.flat:
                copy.wait_recv()
            for dz in range(2):
                here, low, high = (zr[n, dz, m, pl.ds(0, h * 8), :].reshape(h, 8, 128) for m in range(3))
                if block == 8:
                    pair = [here, jnp.where(sub < 4, high, low)]
                else:
                    pair = [jnp.where(sub < 4, here, roll(high, 4, 1)), roll(low, 4, 1)]
                v = jnp.concatenate(pair, axis=1)
                if block == 8:
                    if dz == 0:
                        v = roll(jnp.where(lane16 < 64, slots(ref, base + 68 - h, h), v), 64, 2)
                    else:
                        v = roll(jnp.where(lane16 < 64, v, slots(ref, base + 4, h)), 64, 2)
                put(ref, base + (4 - h if dz == 0 else 68), v)

            @pl.when(j < 7)
            def _():
                for copy in self.up:
                    copy.wait_send()

            @pl.when(j > 0)
            def _():
                for copy in self.down:
                    copy.wait_send()

            for copy in self.flat:
                copy.wait_send()

    half_lane = lax.broadcasted_iota(jnp.int32, (64, 128), 1) < 64

    def to_tiles(src, dst, base):
        for y in range(0, 8, 2):
            rows = [src[pl.ds(y + d, 64, stride=8), :] for d in range(2)]
            turned = jnp.concatenate(rows, axis=0).T
            low, high = turned[:64], turned[64:]
            first = (base + 4) * 16 + y
            dst[pl.ds(first, 64, stride=16), :] = jnp.where(half_lane, low, pltpu.roll(high, 64, 1))
            dst[pl.ds(first + 1, 64, stride=16), :] = jnp.where(half_lane, pltpu.roll(low, 64, 1), high)

    fext_rows, aext_rows = fext.reshape(512, 128), aext.reshape(512, 128)

    def x_gather(xg, n):
        first = remote(xg.at[b], xg.at[b], xg_send.at[n, 0], xg_recv.at[n, 0], gx=b + 1 - 2 * lax.rem(b, 2))
        pair = pl.ds((b // 2) * 2, 2)
        second = [remote(xg.at[pair], xg.at[pair], xg_send.at[n, t], xg_recv.at[n, t], gx=lax.rem(b + 2 * t, 8))
                  for t in range(1, 4)]
        return first, second

    def x_pack(weight, xg, first, upper=None):
        source = lax.broadcasted_iota(jnp.int32, (128, 256), 0)
        target = lax.broadcasted_iota(jnp.int32, (128, 256), 1)
        slot, inner = source % 16, (target % 128) % 32
        hit = (source // 64 == target // 128) & ((source % 64) // 16 == (target % 128) // 32) & (inner < 4)
        pair = (slot // 2 == inner + 2) & hit
        if upper is not None:
            pair = pair & (((source % 64) // 16 != 0) | (slot % 2 == (1 if upper else 0)))
        matrix = jnp.where(pair, weight, 0.0).astype(F32)
        moved = jnp.dot(tb[...], matrix, precision=HIGHEST, preferred_element_type=F32)
        parts = [moved[:, :128].reshape(32, 8, 128), moved[:, 128:].reshape(32, 8, 128)]
        total = None
        for g in range(8):
            part = roll(parts[g // 4][(g % 4) * 8:(g % 4) * 8 + 8], 4 * g, 2)
            total = part if total is None else total + part
        packed = jnp.where(sub % 2 == 0, total[:4], total[4:])
        xg[b, pl.ds(first * 8, 32), :] = packed.reshape(32, 128)

    def x_unpack(xg, first, dst):
        g = (lane // 4) % 8
        for q in range(4):
            for odd in range(2):
                v = []
                for n in range(8):
                    tile = xg[n, pl.ds((first + q) * 8, 8), :].reshape(1, 8, 128)
                    v.append(jnp.where(sub % 2 == 1, tile, roll(tile, -1, 1)) if odd
                             else jnp.where(sub % 2 == 0, tile, roll(tile, 1, 1)))
                for s in (1, 2, 4):
                    high = (g // s) % 2 == 1
                    for n in range(8):
                        if n & s == 0:
                            lo, hi = v[n], v[n + s]
                            v[n] = jnp.where(high, roll(hi, 4 * s, 2), lo)
                            v[n + s] = jnp.where(high, hi, roll(lo, -4 * s, 2))
                for n in range(8):
                    put(tmp, n * 8 + 4 * odd + q, v[n])
        for i in range(4):
            dst[pl.ds(64 + i, 64, stride=16), :] = tmp[pl.ds(2 * i, 64, stride=8), :]

    own_a.wait()
    for copy in strips[:4]:
        copy.wait_recv()
    to_tiles(aext_rows, l0.wa, 1)
    edges = Wide(0, 8, l0.wa, 1, 4)
    edges.start()
    edges.finish()
    group0 = (lane16 // 16) % 4
    row16 = iota(1, (1, 16, 128))
    x_at = 8 * b + lane16 % 16 - 4
    y_at = 8 * j + jnp.where(row16 < 12, row16, row16 - 16)

    def face_body(i):
        a, xd, xu, yd, yu, zd, zu = neighbours(l0, l0.wa, i)
        z_at = 128 * k + 64 * (iota(2, a.shape) // 64) + i * l0.ch - 4 + iota(0, a.shape)
        side_up = jnp.where(group0 == 0, xu, jnp.where(group0 == 1, yu, zu))
        side_low = jnp.where(group0 == 0, xd, jnp.where(group0 == 1, yd, zd))
        where = jnp.where(group0 == 0, x_at, jnp.where(group0 == 1, y_at, z_at))
        end = jnp.where(group0 == 0, nx - 1, jnp.where(group0 == 1, ny - 1, nz - 1))
        l0.put(l0.up, i, jnp.where(where == end, 0.0, 0.5 * (a + side_up)))
        l0.put(l0.low, i, jnp.where(where == 0, 0.0, 0.5 * (a + side_low)))

    l0.loop(face_body)

    own_f.wait()
    for copy in strips[4:]:
        copy.wait_recv()
    to_tiles(fext_rows, l0.f, 0)
    edges = Wide(1, 8, l0.f, 0, 3)
    edges.start()
    for upper, ref in ((True, l0.up), (False, l0.low)):
        def body(i, ref=ref, upper=upper):
            put(tb, i * 16, coarse_faces(*own_pairs(ref, i), 16, upper, 1, None))

        loop(2, body)
        x_pack(0.25, xgf, 0 if upper else 4, upper)
    faces_first, faces_second = x_gather(xgf, 1)
    faces_first.start()
    make_coefs(l0, 16)

    edges.finish()

    over_theta, ((a1, b1), (a2, b2)) = SMOOTH

    def downward(lv):
        init_down(lv, over_theta)
        step(lv, lv.wa, lv.wb, a1, b1, add="w")
        step(lv, lv.wb, lv.wa, a2, b2, add="x")
        step(lv, lv.wa, None)

    def upward(lv, coarse_at):
        init_up(lv, coarse_at)
        step(lv, lv.wa, lv.wb, None, over_theta, add="xw")
        step(lv, lv.wb, lv.wa, a1, b1)
        step(lv, lv.wa, None, a2, b2, add="xw", last=True)

    def own_sums(lv, i):
        pairs, roots = own_pairs(lv.r, i), own_pairs(lv.root, i)
        return pairs[0] * roots[0] + pairs[1] * roots[1]

    downward(l0)

    def body(i):
        put(tb, i * 16, both(own_sums(l0, i), 1, 1))

    loop(2, body)
    x_pack(0.125, xg1, 0)
    right_first, right_second = x_gather(xg1, 0)
    right_first.start()
    faces_first.wait_recv()
    for copy in faces_second:
        copy.start()

    slot = lane % 16
    for side, first in ((0, 10), (1, 4)):
        packed = jnp.zeros((8, 8, 128), F32)
        for g in range(8):
            v = slots(l0.r, 4 + 8 * g, 8)[:, :8]
            packed = jnp.where(slot // 2 == g, roll(v, 2 * g - first, 2), packed)
        rxs[side] = packed.reshape(64, 128)
    rx = [remote(rxs.at[0], rxr.at[0], rx_send.at[0], rx_recv.at[0], gx=b_up),
          remote(rxs.at[1], rxr.at[1], rx_send.at[1], rx_recv.at[1], gx=b_down)]

    for copy in faces_second:
        copy.wait_recv()
    x_unpack(xgf, 0, l1.up)
    x_unpack(xgf, 4, l1.low)
    edges_up, edges_low = Wide(2, 4, l1.up, 0, 3), Wide(3, 4, l1.low, 0, 3)
    edges_up.start()
    edges_low.start()

    def second_pack(q, first):
        start = pl.multiple_of((b // 2) * 64, 64)
        q[pl.ds(first, 8), :] = jnp.where(lane2 % 2 == 0, tb[pl.ds(start, 8, stride=8), :],
                                          tb[pl.ds(start + 2, 8, stride=8), :])

    def second_gather(q, yg, zh, n):
        c = b // 2
        along = [remote(q, yg.at[c, j], yg_send.at[n, t], yg_recv.at[n, t], gy=lax.rem(j + t, 8)) for t in range(1, 8)]
        quarters = [remote(yg.at[c], yg.at[c], yc_send.at[n, t], yc_recv.at[n, t], gx=lax.rem(b + 2 * t, 8))
                    for t in range(1, 4)]
        halo = [remote(yg.at[3], zh.at[0], h_send.at[n, 0], h_recv.at[n, 0], gz=lax.rem(k + 1, 8)),
                remote(yg.at[0], zh.at[1], h_send.at[n, 1], h_recv.at[n, 1], gz=lax.rem(k + 7, 8))]
        return along, quarters, halo

    def second_unpack(yg, zh, first, dst):
        rows = pl.ds(first, 8)
        for n in range(8):
            parts = [zh[0, n, rows, :]] + [yg[c, n, rows, :] for c in range(4)] + [zh[1, n, rows, :]]
            v = jnp.concatenate(parts, axis=0)
            dst[pl.ds(2 * n, 48, stride=16), :] = jnp.where(lane2 % 2 == 0, v, roll(v, 1, 1))
            dst[pl.ds(2 * n + 1, 48, stride=16), :] = jnp.where(lane2 % 2 == 1, v, roll(v, -1, 1))

    for upper, ref in ((True, l1.up), (False, l1.low)):
        def body(i, ref=ref, upper=upper):
            put(tb, i * 16, 0.25 * coarse_faces(*own_pairs(ref, i), 32, upper, 1, 1))

        loop(2, body)
        second_pack(qf, 0 if upper else 8)
    ygf[b // 2, j] = qf[...]
    faces_y, faces_c, faces_h = second_gather(qf, ygf, zhf, 0)
    edges_up.finish()
    edges_low.finish()
    right_first.wait_recv()
    for copy in right_second:
        copy.start()
    for copy in faces_y:
        copy.start()
    make_coefs(l1, 32)

    for copy in right_second:
        copy.wait_recv()
    x_unpack(xg1, 0, l1.f)
    edges = Wide(4, 4, l1.f, 0, 3)
    edges.start()
    edges.finish()
    for copy in faces_y:
        copy.wait_recv()
    for copy in faces_c:
        copy.start()
    downward(l1)

    def body(i):
        put(tb, i * 16, 0.125 * both(both(own_sums(l1, i), 1, 1), 1, 2))

    loop(2, body)
    second_pack(q1, 0)
    yg1[b // 2, j] = q1[...]
    right_y, right_c, right_h = second_gather(q1, yg1, zh1, 1)
    for copy in right_y:
        copy.start()
    for copy in faces_c:
        copy.wait_recv()
    for copy in faces_h:
        copy.start()
    for copy in faces_h:
        copy.wait_recv()
    second_unpack(ygf, zhf, 0, l2.up)
    second_unpack(ygf, zhf, 8, l2.low)

    t = lane % 4

    def third(ref, upper=None):
        even, odd = (ref[pl.ds(128 + d, 256, stride=2), :].reshape(16, 2, 8, 128) for d in range(2))
        if upper is None:
            roots = [l2.root[pl.ds(128 + d, 256, stride=2), :].reshape(16, 2, 8, 128) for d in range(2)]
            v = even * roots[0] + odd * roots[1]
            v = 0.125 * both(v[:, 0] + v[:, 1], 2, 2)
        else:
            g = lane // 32
            side = odd if upper else even
            first, second = (jnp.where(g == 1, side[:, d], even[:, d] + odd[:, d]) for d in range(2))
            v = jnp.where(g == 2, second if upper else first, first + second)
            v = 0.25 * jnp.where(g == 0, pick(v, 2, 2, upper), both(v, 2, 2))
        v = v.reshape(4, 4, 8, 128)
        out = v[:, 0]
        for u in range(1, 4):
            out = jnp.where(t == u, v[:, u], out)
        return out

    def z_gather(g, n):
        rows = pl.ds(pl.multiple_of(k * 32, 8), 32)
        return [remote(g.at[rows], g.at[rows], zg_send.at[n, u], zg_recv.at[n, u], gz=lax.rem(k + u, 8))
                for u in range(1, 8)]

    put(l3.up, 4 * k, third(l2.up, True))
    put(l3.low, 4 * k, third(l2.low, False))
    third_faces = z_gather(l3.up, 0) + z_gather(l3.low, 1)

    for copy in third_faces:
        copy.start()
    make_coefs(l2, 32)
    for copy in right_y:
        copy.wait_recv()
    for copy in right_c:
        copy.start()
    for copy in third_faces:
        copy.wait_recv()
    make_coefs(l3, 32)
    for upper in (True, False):
        src, dst = (l3.up, l4.up) if upper else (l3.low, l4.low)

        def body(i, src=src, dst=dst, upper=upper):
            g = lane // 32
            v = l3.get(src, i)
            v = jnp.where(g == 2, pick(v, 1, 2, upper), both(v, 1, 2))
            v = jnp.where(g == 1, pick(v, 1, 1, upper), both(v, 1, 1))
            l4.put(dst, i, 0.25 * jnp.where(g == 0, pick(v, 4, 2, upper), both(v, 4, 2)))

        l3.loop(body)
    for copy in right_c:
        copy.wait_recv()
    for copy in right_h:
        copy.start()
    make_coefs(l4, 32)
    for copy in right_h:
        copy.wait_recv()
    second_unpack(yg1, zh1, 0, l2.f)
    edges1 = Wide(5, 4, l1.r, 0, 2)
    edges1.start()
    for copy in rx:
        copy.start()
    downward(l2)
    put(l3.f, 4 * k, third(l2.r))
    third_right = z_gather(l3.f, 2)
    for copy in third_right:
        copy.start()

    for copy in third_right:
        copy.wait_recv()

    downward(l3)

    def body(i):
        l4.put(l4.f, i, 0.125 * both(both(both(l3.get(l3.r, i) * l3.get(l3.root, i), 1, 2), 1, 1), 4, 2))

    l3.loop(body)
    solve_theta, solve_steps = SOLVE
    init_down(l4, solve_theta)
    w, w_next = l4.wa, l4.wb
    for n, (alpha, beta) in enumerate(solve_steps):
        step(l4, w, w_next, alpha, beta, add="x" if n else "w", last=n == len(solve_steps) - 1)
        w, w_next = w_next, w
    upward(l3, lambda i: l4.get(l4.x, i))

    for q in range(6):
        v = l3.x[pl.ds(pl.multiple_of(lax.rem(4 * k + q + 31, 32) * 8, 8), 8), :].reshape(1, 8, 128)
        for z in range(4):
            moved = v
            for u in range(4):
                if u != z:
                    moved = jnp.where(t == u, roll(v, u - z, 2), moved)
            first = (4 * q + z) * 16
            eb2[pl.ds(first, 8, stride=2), :] = moved.reshape(8, 128)
            eb2[pl.ds(first + 1, 8, stride=2), :] = moved.reshape(8, 128)

    def twice(ref, offset):
        def chunk(i):
            v = slots(ref, i * 4 + offset, 4)
            return jnp.broadcast_to(v[:, None], (4, 2, 16, 128)).reshape(8, 16, 128)

        return chunk

    upward(l2, twice(eb2, 0))

    for copy in rx:
        copy.wait_recv()
    for g in range(8):
        v = slots(l0.r, 4 + 8 * g, 8)
        own = v[:, :8]
        own = jnp.where(slot // 2 == 1, roll(rxr[0].reshape(8, 8, 128), 2 - 2 * g, 2), own)
        own = jnp.where(slot // 2 == 6, roll(rxr[1].reshape(8, 8, 128), 12 - 2 * g, 2), own)
        put(l0.r, 4 + 8 * g, jnp.concatenate([own, v[:, 8:]], axis=1))
    edges0 = Wide(6, 8, l0.r, 0, 2)
    edges0.start()

    for i, from_y in ((0, 0), (1, 1), (2, 2), (3, 3), (6, 14), (7, 15)):
        v = l2.x[pl.ds(lax.rem(2 * j + from_y, 16), 48, stride=16), :]
        eb1[pl.ds(2 * i, 48, stride=16), :] = v
        eb1[pl.ds(2 * i + 1, 48, stride=16), :] = v
    edges1.finish()
    upward(l1, twice(eb1, 6))
    edges = Wide(7, 4, l1.x, 0, 2)
    edges.start()
    edges0.finish()
    edges.finish()

    source = lax.broadcasted_iota(jnp.int32, (128, 128), 0)
    target = lax.broadcasted_iota(jnp.int32, (128, 128), 1)
    hit = (source // 32 == (target % 64) // 16) & (source % 32 == 4 * b - 2 + (target % 16) // 2)
    v = slots(l1.x, 0, 72)
    v = jnp.where(sub < 6, v[:, :8], v[:, 8:]).reshape(576, 128)
    v = jnp.dot(v, jnp.where(hit, 1.0, 0.0).astype(F32), precision=HIGHEST, preferred_element_type=F32)
    eb0[pl.ds(0, 576, stride=2), :] = v
    eb0[pl.ds(1, 576, stride=2), :] = v

    def top_chunk(i):
        v = jnp.where(lane16 < 64, slots(eb0, i * 4 + 2, 4), slots(eb0, i * 4 + 34, 4))
        return jnp.broadcast_to(v[:, None], (4, 2, 16, 128)).reshape(8, 16, 128)

    upward(l0, top_chunk)

    for y in range(0, 8, 2):
        first = l0.x[pl.ds(64 + y, 64, stride=16), :]
        second = l0.x[pl.ds(65 + y, 64, stride=16), :]
        low = jnp.where(half_lane, first, pltpu.roll(second, 64, 1))
        high = jnp.where(half_lane, pltpu.roll(first, 64, 1), second)
        turned = pltpu.roll(jnp.concatenate([low, high], axis=0), 124, 1).T
        for d in range(2):
            for v in range(4):
                start = d * 64 + v * 16
                out_ref[pl.ds(v * 64 + y + d, 8, stride=8), :] = turned[start:start + 8]

    for copy in (strips[4:] + [faces_first, right_first] + faces_second + right_second + rx + faces_y + right_y + faces_c
                 + right_c + faces_h + right_h + third_faces + third_right):
        copy.wait_send()


def solution(mesh):
    def per_device(right_side, affinity):
        nx = affinity.shape[1] * mesh.shape["gx"]
        ny = affinity.shape[2] * mesh.shape["gy"]
        nz = affinity.shape[3] * mesh.shape["gz"]
        scratch = []
        for z, rows, *_ in LEVELS:
            scratch += level_shapes(z, rows)
        scratch += [pltpu.VMEM(shape, F32) for shape in (
            (4, 16, 8, 128), (4, 16, 8, 128),
            (8, 2, 4, 64, 128), (8, 2, 4, 64, 128), (8, 2, 32, 128), (8, 2, 3, 32, 128),
            (256, 128), (512, 128), (8, 32, 128), (8, 64, 128), (2, 64, 128), (2, 64, 128),
            (8, 128), (16, 128), (4, 8, 8, 128), (4, 8, 16, 128), (2, 8, 8, 128), (2, 8, 16, 128), (384, 128), (768, 128), (1152, 128))]
        dma = pltpu.SemaphoreType.DMA
        scratch += [dma(shape) for shape in (
            (2,), (6,), (6,), (8, 8), (8, 8), (2, 4), (2, 4), (2,), (2,), (2, 2), (2, 2), (2, 8), (2, 8), (2, 4), (2, 4), (3, 8), (3, 8))]
        out = pl.pallas_call(
            functools.partial(kernel, nx, ny, nz),
            out_shape=jax.ShapeDtypeStruct((256, 128), F32),
            in_specs=[pl.BlockSpec(memory_space=pl.ANY)] * 2,
            out_specs=pl.BlockSpec(memory_space=pltpu.VMEM),
            scratch_shapes=scratch,
            compiler_params=pltpu.CompilerParams(
                collective_id=0, has_side_effects=True, vmem_limit_bytes=60 * 1024 * 1024),
        )(right_side, affinity)
        return out.reshape(right_side.shape)

    spec = P(None, "gx", "gy", "gz")
    return jax.shard_map(per_device, mesh=mesh, in_specs=(spec, spec), out_specs=spec, check_vma=False)
```

```python
import functools

import jax
import jax.numpy as jnp
from jax import lax
from jax.experimental import pallas as pl
from jax.experimental.pallas import tpu as pltpu
from jax.sharding import PartitionSpec as P

MESH = pl.DeviceIdType.MESH
HIGHEST = lax.Precision.HIGHEST
F32 = jnp.float32

DEGREE = 3
COARSE_DEGREE = 8
SHIFT = 0.02
SMOOTH_LOWER = 0.5
UPPER = 2.0 + SHIFT


def cheb_coefs(a, b, m):
    theta, delta = 0.5 * (b + a), 0.5 * (b - a)
    sigma = theta / delta
    rho = 1.0 / sigma
    steps = []
    for _ in range(m - 1):
        nxt = 1.0 / (2.0 * sigma - rho)
        steps.append((nxt * rho, 2.0 * nxt / delta))
        rho = nxt
    return 1.0 / theta, steps


SMOOTH = cheb_coefs(SMOOTH_LOWER, UPPER, DEGREE)
SOLVE = cheb_coefs(SHIFT, UPPER, COARSE_DEGREE)


def iota(dim, shape=(1, 8, 128)):
    return lax.broadcasted_iota(jnp.int32, shape, dim)


def roll(x, shift, axis):
    shift = shift % x.shape[axis]
    return x if shift == 0 else pltpu.roll(x, shift, axis)


def both(x, k, axis):
    bit = (iota(axis, (1,) + x.shape[1:]) // k) % 2
    return x + jnp.where(bit == 0, roll(x, -k, axis), roll(x, k, axis))


def pick(x, k, axis):
    bit = (iota(axis, (1,) + x.shape[1:]) // k) % 2
    return jnp.where(bit == 1, x, roll(x, -k, axis))


def slots(ref, start, count, rows=16):
    if not isinstance(start, int):
        start = pl.multiple_of(start * rows, rows)
    else:
        start = start * rows
    return ref[pl.ds(start, count * rows), :].reshape(count, rows, 128)


def put(ref, start, value):
    count, rows = value.shape[:2]
    if not isinstance(start, int):
        start = pl.multiple_of(start * rows, rows)
    else:
        start = start * rows
    ref[pl.ds(start, count * rows), :] = value.reshape(count * rows, 128)


def loop(count, body):
    def run(i, carry):
        body(i)
        return carry

    lax.fori_loop(0, count, run, 0)


class Level:
    def __init__(self, z, rows, sy, sx, mode, refs):
        self.z, self.rows, self.sy, self.sx, self.mode = z, rows, sy, sx, mode
        self.ch = 128 // rows
        self.parts = z // self.ch if rows == 8 else 3
        (self.coef, self.scale, self.root, self.f, self.r, self.x, self.wa, self.wb, self.up, self.low,
         self.r_next, self.x_next) = refs

    def loop(self, body):
        def turn(i, carry):
            for part in range(self.parts):
                body(i * self.parts + part)
            return carry

        turns = self.z // (self.ch * self.parts)
        if turns == 1:
            turn(0, 0)
        else:
            lax.fori_loop(0, turns, turn, 0)

    def get(self, ref, i, offset=0):
        return slots(ref, i * self.ch + offset, self.ch, self.rows)

    def put(self, ref, i, value, offset=0):
        put(ref, i * self.ch + offset, value)


LEVELS = ((72, 16, 1, 1, 0), (72, 16, 1, 1, 0), (48, 16, 1, 2, 0), (32, 8, 1, 4, 1), (32, 8, 2, 8, 2))


def level_shapes(z, rows):
    n = z * rows
    pad = (z + 2) * rows
    return [pltpu.VMEM((6 * n, 128), F32)] + [pltpu.VMEM((n, 128), F32)] * 5 + [pltpu.VMEM((pad, 128), F32)] * 4 + [
        pltpu.VMEM((n, 128), F32)] * 2


def neighbours(lv, w_ref, i):
    w, before, after = lv.get(w_ref, i, 1), lv.get(w_ref, i, 0), lv.get(w_ref, i, 2)
    xd, xu = roll(w, lv.sx, 2), roll(w, -lv.sx, 2)
    yd, yu = roll(w, lv.sy, 1), roll(w, -lv.sy, 1)
    if lv.mode == 0:
        zd, zu = before, after
    else:
        s = lv.mode
        t = iota(2) % 4
        zu = jnp.where(t < 4 - s, roll(w, -s, 2), roll(after, 4 - s, 2))
        zd = jnp.where(t >= s, roll(w, s, 2), roll(before, s - 4, 2))
    return w, xd, xu, yd, yu, zd, zu


def init_down(lv, over_theta):
    def body(i):
        r = lv.get(lv.scale, i) * lv.get(lv.f, i)
        lv.put(lv.r, i, r)
        lv.put(lv.wa, i, r * over_theta, 1)

    lv.loop(body)


def init_up(lv, coarse_at):
    def body(i):
        lv.put(lv.wa, i, lv.get(lv.scale, i) * coarse_at(i), 1)

    lv.loop(body)


def step(lv, w_ref, w_next, alpha=None, beta=None, add="", last=False):
    def body(i):
        w, *near = neighbours(lv, w_ref, i)
        total = None
        for k, value in enumerate(near):
            term = slots(lv.coef, k * lv.z + i * lv.ch, lv.ch, lv.rows) * value
            total = term if total is None else total + term
        r = lv.get(lv.r, i) - ((1.0 + SHIFT) * w - total)
        if not last:
            lv.put(lv.r_next, i, r)
        if beta is None:
            return
        new = beta * r if alpha is None else alpha * w + beta * r
        if add:
            x = new + w if "w" in add else new
            if "x" in add:
                x = x + lv.get(lv.x, i)
            lv.put(lv.x_next, i, x * lv.get(lv.root, i) if last else x)
        if not last:
            lv.put(w_next, i, new, 1)

    lv.loop(body)
    if not last:
        lv.r, lv.r_next = lv.r_next, lv.r
    if add:
        lv.x, lv.x_next = lv.x_next, lv.x


def make_coefs(lv, group):
    g = (iota(2, (1, lv.rows, 128)) // group) % 4

    def spread(value, k):
        out = value
        for to in range(4):
            if to != k:
                out = jnp.where(g == to, roll(value, group * (to - k), 2), out)
        return out

    def body(i):
        if group == 16:
            up = lv.get(lv.up, i)
            lows = [lv.get(lv.low, i)] * 3
        else:
            up, x_low, _, y_low, _, z_low, _ = neighbours(lv, lv.up, i)
            lows = [jnp.where(iota(2, (1, lv.rows, 128)) % 32 < lv.sx, 0.0, x_low), y_low, z_low]
        faces = []
        for k in range(3):
            faces += [spread(lows[k], k), spread(up, k)]
        total = faces[0] + faces[1] + faces[2] + faces[3] + faces[4] + faces[5]
        scale = jnp.where(total > 0.0, lax.rsqrt(total), 0.0)
        lv.put(lv.scale, i, scale)
        lv.put(lv.root, i, scale * total)
        square = scale * scale
        for k in range(6):
            put(lv.coef, k * lv.z + i * lv.ch, square * faces[k])

    lv.loop(body)


def own_pairs(ref, i, base=0):
    v = slots(ref, base + 4 + 32 * i, 32)[:, :8].reshape(16, 2, 8, 128)
    return v[:, 0], v[:, 1]


def coarse_faces(first, second, group, ky, kx):
    g = (iota(2) // group) % 4
    v = jnp.where(g == 2, second, first + second)
    v = jnp.where(g == 1, pick(v, ky, 1), both(v, ky, 1))
    if kx is not None:
        v = jnp.where(g == 0, pick(v, kx, 2), both(v, kx, 2))
    return v


def own_step(lv, w_ref, alpha=None, beta=None):
    def body(i):
        first = 4 + 8 * i
        here = slots(w_ref, first + 1, 8)
        w = here[:, :8]
        near = [roll(w, 1, 2), roll(w, -1, 2), roll(here, 1, 1)[:, :8], roll(here, -1, 1)[:, :8],
                slots(w_ref, first, 8)[:, :8], slots(w_ref, first + 2, 8)[:, :8]]
        total = None
        for k, value in enumerate(near):
            term = slots(lv.coef, k * lv.z + first, 8)[:, :8] * value
            total = term if total is None else total + term
        r = slots(lv.r, first, 8)[:, :8] - ((1.0 + SHIFT) * w - total)
        if beta is not None:
            x = slots(lv.x, first, 8)[:, :8] + w + (alpha * w + beta * r)
            r = x * slots(lv.root, first, 8)[:, :8]
        target = lv.r_next if beta is None else lv.x_next
        for n in range(8):
            target[pl.ds(pl.multiple_of((first + n) * 16, 16), 8), :] = r[n]

    def turn(i, carry):
        for part in range(4):
            body(4 * i + part)
        return carry

    lax.fori_loop(0, 2, turn, 0)
    if beta is None:
        lv.r, lv.r_next = lv.r_next, lv.r
    else:
        lv.x, lv.x_next = lv.x_next, lv.x


def kernel(nx, ny, nz, f_hbm, a_hbm, out_ref, *scratch):
    refs = list(scratch)

    def take(count):
        got = refs[:count]
        del refs[:count]
        return got

    levels = [Level(*shape, take(12)) for shape in LEVELS]
    (fext, aext, ys, yr, zs, zr, tb, tmp, xg1, xgf, rxs, rxr, q1, qf, yg1, ygf, zh1, zhf, eb2, eb1, eb0) = take(21)
    (local_sem, strip_send, strip_recv, ex_send, ex_recv, xg_send, xg_recv, rx_send, rx_recv,
     h_send, h_recv, yg_send, yg_recv, yc_send, yc_recv, zg_send, zg_recv) = take(17)
    l0, l1, l2, l3, l4 = levels

    b, j, k = lax.axis_index("gx"), lax.axis_index("gy"), lax.axis_index("gz")
    sub, lane, lane16 = iota(1), iota(2), iota(2, (1, 16, 128))
    lane2 = lax.broadcasted_iota(jnp.int32, (1, 128), 1)

    def remote(src, dst, send, recv, **to):
        return pltpu.make_async_remote_copy(
            src_ref=src, dst_ref=dst, send_sem=send, recv_sem=recv, device_id=to, device_id_type=MESH)

    own_f = pltpu.make_async_copy(f_hbm, fext.at[:, pl.ds(4, 8)], local_sem.at[0])
    own_a = pltpu.make_async_copy(a_hbm, aext.at[pl.ds(0, 3), pl.ds(4, 8)], local_sem.at[1])
    own_a.start()
    own_f.start()
    zr[...] = jnp.zeros_like(zr)

    barrier = pltpu.get_barrier_semaphore()
    partners = [{"gx": lax.rem(b + t, 8)} for t in (1, 2, 4, 6, 7)]
    partners += [{"gy": lax.rem(j + t, 8)} for t in range(1, 8)]
    partners += [{"gz": lax.rem(k + t, 8)} for t in range(1, 8)]
    partners += [{"gy": lax.rem(j + t, 8), "gz": lax.rem(k + u, 8)} for t in (1, 7) for u in (1, 7)]
    partners += [{"gx": lax.rem(b + t, 8), "gz": lax.rem(k + u, 8)} for t in (2, 4, 6) for u in (1, 7)]
    for to in partners:
        pl.semaphore_signal(barrier, inc=1, device_id=to, device_id_type=MESH)

    fext[:, 0] = jnp.zeros((4, 8, 128), F32)
    fext[:, 15] = jnp.zeros((4, 8, 128), F32)
    aext[3] = jnp.zeros((16, 8, 128), F32)
    for n in (1, 2):
        aext[n, 0] = jnp.zeros((8, 128), F32)
        aext[n, 15] = jnp.zeros((8, 128), F32)
    for ref in (l0.f, l0.wa, l1.f, l1.up, eb1):
        ref[...] = jnp.zeros_like(ref)
    for lv in levels:
        for w in (lv.wa, lv.wb, lv.up):
            w[pl.ds(0, lv.rows), :] = jnp.zeros((lv.rows, 128), F32)
            w[pl.ds((lv.z + 1) * lv.rows, lv.rows), :] = jnp.zeros((lv.rows, 128), F32)
    pl.semaphore_wait(barrier, len(partners))

    b_up, b_down = lax.rem(b + 1, 8), lax.rem(b + 7, 8)
    strips = [
        remote(a_hbm.at[:, pl.ds(5, 3)], aext.at[pl.ds(0, 3), pl.ds(1, 3)],
               strip_send.at[0], strip_recv.at[0], gx=b_up),
        remote(a_hbm.at[:, pl.ds(0, 3)], aext.at[pl.ds(0, 3), pl.ds(12, 3)],
               strip_send.at[1], strip_recv.at[1], gx=b_down),
        remote(a_hbm.at[0, 4], aext.at[0, 0], strip_send.at[4], strip_recv.at[4], gx=b_up),
        remote(a_hbm.at[0, 3], aext.at[0, 15], strip_send.at[5], strip_recv.at[5], gx=b_down),
        remote(f_hbm.at[:, pl.ds(5, 3)], fext.at[:, pl.ds(1, 3)],
               strip_send.at[2], strip_recv.at[2], gx=b_up),
        remote(f_hbm.at[:, pl.ds(0, 3)], fext.at[:, pl.ds(12, 3)],
               strip_send.at[3], strip_recv.at[3], gx=b_down),
    ]
    for copy in strips[:4]:
        copy.start()
    for copy in strips[:4]:
        copy.wait_send()
    for copy in strips[4:]:
        copy.start()

    class Wide:
        def __init__(self, n, block, ref, base, h):
            self.n, self.block, self.ref, self.base, self.h = n, block, ref, base, h
            rows, part = pl.ds(0, h), pl.ds(0, h * 8)
            j_up, j_down = jnp.minimum(j + 1, 7), jnp.maximum(j - 1, 0)
            k_to = (lax.rem(k + 1, 8), lax.rem(k + 7, 8))

            def make(src, dst, index, **to):
                return remote(src, dst, ex_send.at[n, index], ex_recv.at[n, index], **to)

            self.up = [make(ys.at[n, 0, rows], yr.at[n, 0, rows], 0, gy=j_up)]
            self.down = [make(ys.at[n, 1, rows], yr.at[n, 1, rows], 1, gy=j_down)]
            self.flat = []
            for dz in range(2):
                self.flat.append(make(zs.at[n, dz, part], zr.at[n, dz, 0, part], 2 + dz, gz=k_to[dz]))
                self.up.append(make(zs.at[n, dz, part], zr.at[n, dz, 1, part], 4 + dz, gy=j_up, gz=k_to[dz]))
                self.down.append(make(zs.at[n, dz, part], zr.at[n, dz, 2, part], 6 + dz, gy=j_down, gz=k_to[dz]))

        def start(self):
            n, block, ref, base, h = self.n, self.block, self.ref, self.base, self.h
            for i in range(h):
                ys[n, 0, i] = ref[pl.ds((base + 4) * 16 + block - h + i, 64, stride=16), :]
                ys[n, 1, i] = ref[pl.ds((base + 4) * 16 + i, 64, stride=16), :]
                zs[n, 0, pl.ds(i * 8, 8), :] = ref[pl.ds((base + 68 - h + i) * 16, 8), :]
                zs[n, 1, pl.ds(i * 8, 8), :] = ref[pl.ds((base + 4 + i) * 16, 8), :]

            @pl.when(j < 7)
            def _():
                for copy in self.up:
                    copy.start()

            @pl.when(j > 0)
            def _():
                for copy in self.down:
                    copy.start()

            for copy in self.flat:
                copy.start()

        def finish(self):
            n, block, ref, base, h = self.n, self.block, self.ref, self.base, self.h

            @pl.when(j > 0)
            def _():
                for copy in self.up:
                    copy.wait_recv()
                for i in range(h):
                    ref[pl.ds((base + 4) * 16 + 16 - h + i, 64, stride=16), :] = yr[n, 0, i]

            @pl.when(j < 7)
            def _():
                for copy in self.down:
                    copy.wait_recv()
                for i in range(h):
                    ref[pl.ds((base + 4) * 16 + block + i, 64, stride=16), :] = yr[n, 1, i]

            for copy in self.flat:
                copy.wait_recv()
            for dz in range(2):
                here, low, high = (zr[n, dz, m, pl.ds(0, h * 8), :].reshape(h, 8, 128) for m in range(3))
                if block == 8:
                    pair = [here, jnp.where(sub < 4, high, low)]
                else:
                    pair = [jnp.where(sub < 4, here, roll(high, 4, 1)), roll(low, 4, 1)]
                v = jnp.concatenate(pair, axis=1)
                if block == 8:
                    if dz == 0:
                        v = roll(jnp.where(lane16 < 64, slots(ref, base + 68 - h, h), v), 64, 2)
                    else:
                        v = roll(jnp.where(lane16 < 64, v, slots(ref, base + 4, h)), 64, 2)
                put(ref, base + (4 - h if dz == 0 else 68), v)

            @pl.when(j < 7)
            def _():
                for copy in self.up:
                    copy.wait_send()

            @pl.when(j > 0)
            def _():
                for copy in self.down:
                    copy.wait_send()

            for copy in self.flat:
                copy.wait_send()

    half_lane = lax.broadcasted_iota(jnp.int32, (64, 128), 1) < 64

    def to_tiles(src, dst, base):
        for y in range(0, 8, 2):
            rows = [src[pl.ds(y + d, 64, stride=8), :] for d in range(2)]
            turned = jnp.concatenate(rows, axis=0).T
            low, high = turned[:64], turned[64:]
            first = (base + 4) * 16 + y
            dst[pl.ds(first, 64, stride=16), :] = jnp.where(half_lane, low, pltpu.roll(high, 64, 1))
            dst[pl.ds(first + 1, 64, stride=16), :] = jnp.where(half_lane, pltpu.roll(low, 64, 1), high)

    fext_rows, aext_rows = fext.reshape(512, 128), aext.reshape(512, 128)

    def x_gather(xg, n):
        first = remote(xg.at[b], xg.at[b], xg_send.at[n, 0], xg_recv.at[n, 0], gx=b + 1 - 2 * lax.rem(b, 2))
        pair = pl.ds((b // 2) * 2, 2)
        second = [remote(xg.at[pair], xg.at[pair], xg_send.at[n, t], xg_recv.at[n, t], gx=lax.rem(b + 2 * t, 8))
                  for t in range(1, 4)]
        return first, second

    def x_pack(weight, xg, faces=False):
        source = lax.broadcasted_iota(jnp.int32, (128, 256), 0)
        target = lax.broadcasted_iota(jnp.int32, (128, 256), 1)
        slot, inner = source % 16, (target % 128) % 32
        hit = (source // 64 == target // 128) & ((source % 64) // 16 == (target % 128) // 32) & (inner < 4)
        pair = (slot // 2 == inner + 2) & hit
        if faces:
            pair = pair & (((source % 64) // 16 != 0) | (slot % 2 == 1))
        matrix = jnp.where(pair, weight, 0.0).astype(F32)
        moved = jnp.dot(tb[...], matrix, precision=HIGHEST, preferred_element_type=F32)
        parts = [moved[:, :128].reshape(32, 8, 128), moved[:, 128:].reshape(32, 8, 128)]
        total = None
        for g in range(8):
            part = roll(parts[g // 4][(g % 4) * 8:(g % 4) * 8 + 8], 4 * g, 2)
            total = part if total is None else total + part
        packed = jnp.where(sub % 2 == 0, total[:4], total[4:])
        xg[b] = packed.reshape(32, 128)

    def x_unpack(xg, dst, base):
        g = (lane // 4) % 8
        for q in range(4):
            for odd in range(2):
                v = []
                for n in range(8):
                    tile = xg[n, pl.ds(q * 8, 8), :].reshape(1, 8, 128)
                    v.append(jnp.where(sub % 2 == 1, tile, roll(tile, -1, 1)) if odd
                             else jnp.where(sub % 2 == 0, tile, roll(tile, 1, 1)))
                for s in (1, 2, 4):
                    high = (g // s) % 2 == 1
                    for n in range(8):
                        if n & s == 0:
                            lo, hi = v[n], v[n + s]
                            v[n] = jnp.where(high, roll(hi, 4 * s, 2), lo)
                            v[n + s] = jnp.where(high, hi, roll(lo, -4 * s, 2))
                for n in range(8):
                    put(tmp, n * 8 + 4 * odd + q, v[n])
        for i in range(4):
            dst[pl.ds((base + 4) * 16 + i, 64, stride=16), :] = tmp[pl.ds(2 * i, 64, stride=8), :]

    own_a.wait()
    for copy in strips[:4]:
        copy.wait_recv()
    to_tiles(aext_rows, l0.wa, 1)
    edges = Wide(0, 8, l0.wa, 1, 4)
    edges.start()
    edges.finish()
    group0 = (lane16 // 16) % 4
    row16 = iota(1, (1, 16, 128))
    x_at = 8 * b + lane16 % 16 - 4
    y_at = 8 * j + jnp.where(row16 < 12, row16, row16 - 16)

    def face_body(i):
        a, xd, xu, yd, yu, zd, zu = neighbours(l0, l0.wa, i)
        z_at = 128 * k + 64 * (iota(2, a.shape) // 64) + i * l0.ch - 4 + iota(0, a.shape)
        side_up = jnp.where(group0 == 0, xu, jnp.where(group0 == 1, yu, zu))
        side_low = jnp.where(group0 == 0, xd, jnp.where(group0 == 1, yd, zd))
        where = jnp.where(group0 == 0, x_at, jnp.where(group0 == 1, y_at, z_at))
        end = jnp.where(group0 == 0, nx - 1, jnp.where(group0 == 1, ny - 1, nz - 1))
        l0.put(l0.up, i, jnp.where(where == end, 0.0, 0.5 * (a + side_up)))
        l0.put(l0.low, i, jnp.where(where == 0, 0.0, 0.5 * (a + side_low)))

    l0.loop(face_body)

    own_f.wait()
    for copy in strips[4:]:
        copy.wait_recv()
    to_tiles(fext_rows, l0.f, 0)
    edges = Wide(1, 8, l0.f, 0, 3)
    edges.start()

    def body(i):
        put(tb, i * 16, coarse_faces(*own_pairs(l0.up, i), 16, 1, None))

    loop(2, body)
    x_pack(0.25, xgf, True)
    faces_first, faces_second = x_gather(xgf, 1)
    faces_first.start()
    make_coefs(l0, 16)

    edges.finish()

    over_theta, ((a1, b1), (a2, b2)) = SMOOTH

    def downward(lv):
        init_down(lv, over_theta)
        step(lv, lv.wa, lv.wb, a1, b1, add="w")
        step(lv, lv.wb, lv.wa, a2, b2, add="x")
        if lv in (l0, l1):
            own_step(lv, lv.wa)
        else:
            step(lv, lv.wa, None)

    def upward(lv, coarse_at):
        init_up(lv, coarse_at)
        step(lv, lv.wa, lv.wb, None, over_theta, add="xw")
        step(lv, lv.wb, lv.wa, a1, b1)
        if lv in (l0, l1):
            own_step(lv, lv.wa, a2, b2)
        else:
            step(lv, lv.wa, None, a2, b2, add="xw", last=True)

    def own_sums(lv, i):
        pairs, roots = own_pairs(lv.r, i), own_pairs(lv.root, i)
        return pairs[0] * roots[0] + pairs[1] * roots[1]

    downward(l0)

    def body(i):
        put(tb, i * 16, both(own_sums(l0, i), 1, 1))

    loop(2, body)
    x_pack(0.125, xg1)
    right_first, right_second = x_gather(xg1, 0)
    right_first.start()
    faces_first.wait_recv()
    for copy in faces_second:
        copy.start()

    slot = lane % 16
    for side, first in ((0, 10), (1, 4)):
        packed = jnp.zeros((8, 8, 128), F32)
        for g in range(8):
            v = slots(l0.r, 4 + 8 * g, 8)[:, :8]
            packed = jnp.where(slot // 2 == g, roll(v, 2 * g - first, 2), packed)
        rxs[side] = packed.reshape(64, 128)
    rx = [remote(rxs.at[0], rxr.at[0], rx_send.at[0], rx_recv.at[0], gx=b_up),
          remote(rxs.at[1], rxr.at[1], rx_send.at[1], rx_recv.at[1], gx=b_down)]

    for copy in faces_second:
        copy.wait_recv()
    x_unpack(xgf, l1.up, 1)
    edges = Wide(2, 4, l1.up, 1, 4)
    edges.start()

    c = b // 2

    def second_pack(q):
        start = pl.multiple_of(c * 64, 64)
        q[...] = jnp.where(lane2 % 2 == 0, tb[pl.ds(start, 8, stride=8), :], tb[pl.ds(start + 2, 8, stride=8), :])

    class Second:
        def __init__(self, q, yg, zh, n):
            yg[c, j] = q[...]
            self.along = [remote(q, yg.at[c, j], yg_send.at[n, t], yg_recv.at[n, t], gy=lax.rem(j + t, 8))
                          for t in range(1, 8)]
            self.quarters = [remote(yg.at[c], yg.at[c], yc_send.at[n, t], yc_recv.at[n, t], gx=lax.rem(b + 2 * t, 8))
                             for t in range(1, 4)]
            self.above = [remote(yg.at[3], zh.at[0], h_send.at[n, 0, t], h_recv.at[n, 0],
                                 gx=lax.rem(b + 2 * t, 8), gz=lax.rem(k + 1, 8)) for t in range(4)]
            self.below = [remote(yg.at[0], zh.at[1], h_send.at[n, 1, t], h_recv.at[n, 1],
                                 gx=lax.rem(b + 2 * t, 8), gz=lax.rem(k + 7, 8)) for t in range(4)]
            self.yg, self.zh = yg, zh
            for copy in self.along:
                copy.start()

        def spread(self):
            for copy in self.along:
                copy.wait_recv()
            for copy in self.quarters:
                copy.start()

            @pl.when(c == 3)
            def _():
                for copy in self.above:
                    copy.start()

            @pl.when(c == 0)
            def _():
                for copy in self.below:
                    copy.start()

        def finish(self, dst, base):
            for copy in self.quarters + [self.above[0], self.below[0]]:
                copy.wait_recv()
            yg, zh = self.yg, self.zh
            for n in range(8):
                v = jnp.concatenate([zh[0, n]] + [yg[m, n] for m in range(4)] + [zh[1, n]], axis=0)
                dst[pl.ds(base * 16 + 2 * n, 48, stride=16), :] = jnp.where(lane2 % 2 == 0, v, roll(v, 1, 1))
                dst[pl.ds(base * 16 + 2 * n + 1, 48, stride=16), :] = jnp.where(lane2 % 2 == 1, v, roll(v, -1, 1))

        def wait_send(self):
            for copy in self.along + self.quarters:
                copy.wait_send()

            @pl.when(c == 3)
            def _():
                for copy in self.above:
                    copy.wait_send()

            @pl.when(c == 0)
            def _():
                for copy in self.below:
                    copy.wait_send()

    def body(i):
        put(tb, i * 16, 0.25 * coarse_faces(*own_pairs(l1.up, i, 1), 32, 1, 1))

    loop(2, body)
    second_pack(qf)
    faces_second_level = Second(qf, ygf, zhf, 0)
    edges.finish()
    right_first.wait_recv()
    for copy in right_second:
        copy.start()
    make_coefs(l1, 32)

    for copy in right_second:
        copy.wait_recv()
    x_unpack(xg1, l1.f, 0)
    edges = Wide(3, 4, l1.f, 0, 3)
    edges.start()
    edges.finish()
    faces_second_level.spread()
    downward(l1)

    def body(i):
        put(tb, i * 16, 0.125 * both(both(own_sums(l1, i), 1, 1), 1, 2))

    loop(2, body)
    second_pack(q1)
    right_second_level = Second(q1, yg1, zh1, 1)
    faces_second_level.finish(l2.up, 1)

    t = lane % 4

    def third(ref, faces=False):
        first_row = 144 if faces else 128
        even, odd = (ref[pl.ds(first_row + d, 256, stride=2), :].reshape(16, 2, 8, 128) for d in range(2))
        if faces:
            g = lane // 32
            first, second = (jnp.where(g == 1, odd[:, d], even[:, d] + odd[:, d]) for d in range(2))
            v = jnp.where(g == 2, second, first + second)
            v = 0.25 * jnp.where(g == 0, pick(v, 2, 2), both(v, 2, 2))
        else:
            roots = [l2.root[pl.ds(128 + d, 256, stride=2), :].reshape(16, 2, 8, 128) for d in range(2)]
            v = even * roots[0] + odd * roots[1]
            v = 0.125 * both(v[:, 0] + v[:, 1], 2, 2)
        v = v.reshape(4, 4, 8, 128)
        out = v[:, 0]
        for u in range(1, 4):
            out = jnp.where(t == u, v[:, u], out)
        return out

    def z_gather(g, n, base):
        rows = pl.ds(pl.multiple_of((4 * k + base) * 8, 8), 32)
        return [remote(g.at[rows], g.at[rows], zg_send.at[n, u], zg_recv.at[n, u], gz=lax.rem(k + u, 8))
                for u in range(1, 8)]

    put(l3.up, 4 * k + 1, third(l2.up, True))
    third_faces = z_gather(l3.up, 0, 1)

    for copy in third_faces:
        copy.start()
    make_coefs(l2, 32)
    right_second_level.spread()
    for copy in third_faces:
        copy.wait_recv()
    make_coefs(l3, 32)

    def body(i):
        g = lane // 32
        v = l3.get(l3.up, i, 1)
        v = jnp.where(g == 2, pick(v, 1, 2), both(v, 1, 2))
        v = jnp.where(g == 1, pick(v, 1, 1), both(v, 1, 1))
        l4.put(l4.up, i, 0.25 * jnp.where(g == 0, pick(v, 4, 2), both(v, 4, 2)), 1)

    l3.loop(body)
    make_coefs(l4, 32)
    right_second_level.finish(l2.f, 0)
    edges1 = Wide(4, 4, l1.r, 0, 2)
    edges1.start()
    for copy in rx:
        copy.start()
    downward(l2)
    put(l3.f, 4 * k, third(l2.r))
    third_right = z_gather(l3.f, 1, 0)
    for copy in third_right:
        copy.start()

    for copy in third_right:
        copy.wait_recv()

    downward(l3)

    def body(i):
        l4.put(l4.f, i, 0.125 * both(both(both(l3.get(l3.r, i) * l3.get(l3.root, i), 1, 2), 1, 1), 4, 2))

    l3.loop(body)
    solve_theta, solve_steps = SOLVE
    init_down(l4, solve_theta)
    w, w_next = l4.wa, l4.wb
    for n, (alpha, beta) in enumerate(solve_steps):
        step(l4, w, w_next, alpha, beta, add="x" if n else "w", last=n == len(solve_steps) - 1)
        w, w_next = w_next, w
    upward(l3, lambda i: l4.get(l4.x, i))

    for q in range(6):
        v = l3.x[pl.ds(pl.multiple_of(lax.rem(4 * k + q + 31, 32) * 8, 8), 8), :].reshape(1, 8, 128)
        for z in range(4):
            moved = v
            for u in range(4):
                if u != z:
                    moved = jnp.where(t == u, roll(v, u - z, 2), moved)
            first = (4 * q + z) * 16
            eb2[pl.ds(first, 8, stride=2), :] = moved.reshape(8, 128)
            eb2[pl.ds(first + 1, 8, stride=2), :] = moved.reshape(8, 128)

    def twice(ref, offset):
        def chunk(i):
            v = slots(ref, i * 4 + offset, 4)
            return jnp.broadcast_to(v[:, None], (4, 2, 16, 128)).reshape(8, 16, 128)

        return chunk

    upward(l2, twice(eb2, 0))

    for copy in rx:
        copy.wait_recv()
    for g in range(8):
        v = slots(l0.r, 4 + 8 * g, 8)
        own = v[:, :8]
        own = jnp.where(slot // 2 == 1, roll(rxr[0].reshape(8, 8, 128), 2 - 2 * g, 2), own)
        own = jnp.where(slot // 2 == 6, roll(rxr[1].reshape(8, 8, 128), 12 - 2 * g, 2), own)
        put(l0.r, 4 + 8 * g, jnp.concatenate([own, v[:, 8:]], axis=1))
    edges0 = Wide(5, 8, l0.r, 0, 2)
    edges0.start()

    for i, from_y in ((0, 0), (1, 1), (2, 2), (3, 3), (6, 14), (7, 15)):
        v = l2.x[pl.ds(lax.rem(2 * j + from_y, 16), 48, stride=16), :]
        eb1[pl.ds(2 * i, 48, stride=16), :] = v
        eb1[pl.ds(2 * i + 1, 48, stride=16), :] = v
    edges1.finish()
    upward(l1, twice(eb1, 6))
    edges = Wide(6, 4, l1.x, 0, 2)
    edges.start()
    edges0.finish()
    edges.finish()

    source = lax.broadcasted_iota(jnp.int32, (128, 128), 0)
    target = lax.broadcasted_iota(jnp.int32, (128, 128), 1)
    hit = (source // 32 == (target % 64) // 16) & (source % 32 == 4 * b - 2 + (target % 16) // 2)
    v = slots(l1.x, 0, 72)
    v = jnp.where(sub < 6, v[:, :8], v[:, 8:]).reshape(576, 128)
    v = jnp.dot(v, jnp.where(hit, 1.0, 0.0).astype(F32), precision=HIGHEST, preferred_element_type=F32)
    eb0[pl.ds(0, 576, stride=2), :] = v
    eb0[pl.ds(1, 576, stride=2), :] = v

    def top_chunk(i):
        v = jnp.where(lane16 < 64, slots(eb0, i * 4 + 2, 4), slots(eb0, i * 4 + 34, 4))
        return jnp.broadcast_to(v[:, None], (4, 2, 16, 128)).reshape(8, 16, 128)

    upward(l0, top_chunk)

    for y in range(0, 8, 2):
        first = l0.x[pl.ds(64 + y, 64, stride=16), :]
        second = l0.x[pl.ds(65 + y, 64, stride=16), :]
        low = jnp.where(half_lane, first, pltpu.roll(second, 64, 1))
        high = jnp.where(half_lane, pltpu.roll(first, 64, 1), second)
        turned = pltpu.roll(jnp.concatenate([low, high], axis=0), 124, 1).T
        for d in range(2):
            for v in range(4):
                start = d * 64 + v * 16
                out_ref[pl.ds(v * 64 + y + d, 8, stride=8), :] = turned[start:start + 8]

    for copy in (strips[4:] + [faces_first, right_first] + faces_second + right_second + rx + third_faces + third_right):
        copy.wait_send()
    faces_second_level.wait_send()
    right_second_level.wait_send()


def solution(mesh):
    def per_device(right_side, affinity):
        nx = affinity.shape[1] * mesh.shape["gx"]
        ny = affinity.shape[2] * mesh.shape["gy"]
        nz = affinity.shape[3] * mesh.shape["gz"]
        scratch = []
        for z, rows, *_ in LEVELS:
            scratch += level_shapes(z, rows)
        scratch += [pltpu.VMEM(shape, F32) for shape in (
            (4, 16, 8, 128), (4, 16, 8, 128),
            (7, 2, 4, 64, 128), (7, 2, 4, 64, 128), (7, 2, 32, 128), (7, 2, 3, 32, 128),
            (256, 128), (512, 128), (8, 32, 128), (8, 32, 128), (2, 64, 128), (2, 64, 128),
            (8, 128), (8, 128), (4, 8, 8, 128), (4, 8, 8, 128), (2, 8, 8, 128), (2, 8, 8, 128), (384, 128), (768, 128), (1152, 128))]
        dma = pltpu.SemaphoreType.DMA
        scratch += [dma(shape) for shape in (
            (2,), (6,), (6,), (7, 8), (7, 8), (2, 4), (2, 4), (2,), (2,), (2, 2, 4), (2, 2), (2, 8), (2, 8), (2, 4), (2, 4), (2, 8), (2, 8))]
        out = pl.pallas_call(
            functools.partial(kernel, nx, ny, nz),
            out_shape=jax.ShapeDtypeStruct((256, 128), F32),
            in_specs=[pl.BlockSpec(memory_space=pl.ANY)] * 2,
            out_specs=pl.BlockSpec(memory_space=pltpu.VMEM),
            scratch_shapes=scratch,
            compiler_params=pltpu.CompilerParams(
                collective_id=0, has_side_effects=True, vmem_limit_bytes=60 * 1024 * 1024),
        )(right_side, affinity)
        return out.reshape(right_side.shape)

    spec = P(None, "gx", "gy", "gz")
    return jax.shard_map(per_device, mesh=mesh, in_specs=(spec, spec), out_specs=spec, check_vma=False)
```

```python
import functools

import jax
import jax.numpy as jnp
from jax import lax
from jax.experimental import pallas as pl
from jax.experimental.pallas import tpu as pltpu
from jax.sharding import PartitionSpec as P

MESH = pl.DeviceIdType.MESH
HIGHEST = lax.Precision.HIGHEST
F32 = jnp.float32

DEGREE = 3
COARSE_DEGREE = 8
SHIFT = 0.02
SMOOTH_LOWER = 0.5
UPPER = 2.0 + SHIFT


def cheb_coefs(a, b, m):
    theta, delta = 0.5 * (b + a), 0.5 * (b - a)
    sigma = theta / delta
    rho = 1.0 / sigma
    steps = []
    for _ in range(m - 1):
        nxt = 1.0 / (2.0 * sigma - rho)
        steps.append((nxt * rho, 2.0 * nxt / delta))
        rho = nxt
    return 1.0 / theta, steps


SMOOTH = cheb_coefs(SMOOTH_LOWER, UPPER, DEGREE)
SOLVE = cheb_coefs(SHIFT, UPPER, COARSE_DEGREE)


def iota(dim, shape=(1, 8, 128)):
    return lax.broadcasted_iota(jnp.int32, shape, dim)


def roll(x, shift, axis):
    shift = shift % x.shape[axis]
    return x if shift == 0 else pltpu.roll(x, shift, axis)


def both(x, k, axis):
    bit = (iota(axis, (1,) + x.shape[1:]) // k) % 2
    return x + jnp.where(bit == 0, roll(x, -k, axis), roll(x, k, axis))


def pick(x, k, axis):
    bit = (iota(axis, (1,) + x.shape[1:]) // k) % 2
    return jnp.where(bit == 1, x, roll(x, -k, axis))


def slots(ref, start, count, rows=16):
    if not isinstance(start, int):
        start = pl.multiple_of(start * rows, rows)
    else:
        start = start * rows
    return ref[pl.ds(start, count * rows), :].reshape(count, rows, 128)


def put(ref, start, value):
    count, rows = value.shape[:2]
    if not isinstance(start, int):
        start = pl.multiple_of(start * rows, rows)
    else:
        start = start * rows
    ref[pl.ds(start, count * rows), :] = value.reshape(count * rows, 128)


def loop(count, body):
    def run(i, carry):
        body(i)
        return carry

    lax.fori_loop(0, count, run, 0)


class Level:
    def __init__(self, z, rows, sy, sx, mode, refs):
        self.z, self.rows, self.sy, self.sx, self.mode = z, rows, sy, sx, mode
        self.ch = 128 // rows
        self.parts = z // self.ch if rows == 8 else 3
        (self.coef, self.scale, self.root, self.f, self.r, self.x, self.wa, self.wb, self.up, self.low,
         self.r_next, self.x_next) = refs

    def loop(self, body):
        def turn(i, carry):
            for part in range(self.parts):
                body(i * self.parts + part)
            return carry

        turns = self.z // (self.ch * self.parts)
        if turns == 1:
            turn(0, 0)
        else:
            lax.fori_loop(0, turns, turn, 0)

    def get(self, ref, i, offset=0):
        return slots(ref, i * self.ch + offset, self.ch, self.rows)

    def put(self, ref, i, value, offset=0):
        put(ref, i * self.ch + offset, value)


LEVELS = ((72, 16, 1, 1, 0), (72, 16, 1, 1, 0), (48, 16, 1, 2, 0), (32, 8, 1, 4, 1), (32, 8, 2, 8, 2))


def level_shapes(z, rows):
    n = z * rows
    pad = (z + 2) * rows
    return [pltpu.VMEM((6 * n, 128), F32)] + [pltpu.VMEM((n, 128), F32)] * 5 + [pltpu.VMEM((pad, 128), F32)] * 4 + [
        pltpu.VMEM((n, 128), F32)] * 2


def neighbours(lv, w_ref, i):
    w, before, after = lv.get(w_ref, i, 1), lv.get(w_ref, i, 0), lv.get(w_ref, i, 2)
    xd, xu = roll(w, lv.sx, 2), roll(w, -lv.sx, 2)
    yd, yu = roll(w, lv.sy, 1), roll(w, -lv.sy, 1)
    if lv.mode == 0:
        zd, zu = before, after
    else:
        s = lv.mode
        t = iota(2) % 4
        zu = jnp.where(t < 4 - s, roll(w, -s, 2), roll(after, 4 - s, 2))
        zd = jnp.where(t >= s, roll(w, s, 2), roll(before, s - 4, 2))
    return w, xd, xu, yd, yu, zd, zu


def init_down(lv, over_theta):
    def body(i):
        r = lv.get(lv.scale, i) * lv.get(lv.f, i)
        lv.put(lv.r, i, r)
        lv.put(lv.wa, i, r * over_theta, 1)

    lv.loop(body)


def init_up(lv, coarse_at):
    def body(i):
        lv.put(lv.wa, i, lv.get(lv.scale, i) * coarse_at(i), 1)

    lv.loop(body)


def step(lv, w_ref, w_next, alpha=None, beta=None, add="", last=False):
    def body(i):
        w, *near = neighbours(lv, w_ref, i)
        total = None
        for k, value in enumerate(near):
            term = slots(lv.coef, k * lv.z + i * lv.ch, lv.ch, lv.rows) * value
            total = term if total is None else total + term
        r = lv.get(lv.r, i) - ((1.0 + SHIFT) * w - total)
        if not last:
            lv.put(lv.r_next, i, r)
        if beta is None:
            return
        new = beta * r if alpha is None else alpha * w + beta * r
        if add:
            x = new + w if "w" in add else new
            if "x" in add:
                x = x + lv.get(lv.x, i)
            lv.put(lv.x_next, i, x * lv.get(lv.root, i) if last else x)
        if not last:
            lv.put(w_next, i, new, 1)

    lv.loop(body)
    if not last:
        lv.r, lv.r_next = lv.r_next, lv.r
    if add:
        lv.x, lv.x_next = lv.x_next, lv.x


def make_coefs(lv, group):
    g = (iota(2, (1, lv.rows, 128)) // group) % 4

    def spread(value, k):
        out = value
        for to in range(4):
            if to != k:
                out = jnp.where(g == to, roll(value, group * (to - k), 2), out)
        return out

    def body(i):
        if group == 16:
            up = lv.get(lv.up, i)
            lows = [lv.get(lv.low, i)] * 3
        else:
            up, x_low, _, y_low, _, z_low, _ = neighbours(lv, lv.up, i)
            lows = [jnp.where(iota(2, (1, lv.rows, 128)) % 32 < lv.sx, 0.0, x_low), y_low, z_low]
        faces = []
        for k in range(3):
            faces += [spread(lows[k], k), spread(up, k)]
        total = faces[0] + faces[1] + faces[2] + faces[3] + faces[4] + faces[5]
        scale = jnp.where(total > 0.0, lax.rsqrt(total), 0.0)
        lv.put(lv.scale, i, scale)
        lv.put(lv.root, i, scale * total)
        square = scale * scale
        for k in range(6):
            put(lv.coef, k * lv.z + i * lv.ch, square * faces[k])

    lv.loop(body)


def own_pairs(ref, i, base=0):
    v = slots(ref, base + 4 + 32 * i, 32)[:, :8].reshape(16, 2, 8, 128)
    return v[:, 0], v[:, 1]


def coarse_faces(first, second, group, ky, kx):
    g = (iota(2) // group) % 4
    v = jnp.where(g == 2, second, first + second)
    v = jnp.where(g == 1, pick(v, ky, 1), both(v, ky, 1))
    if kx is not None:
        v = jnp.where(g == 0, pick(v, kx, 2), both(v, kx, 2))
    return v


def own_step(lv, w_ref, alpha=None, beta=None):
    def body(i):
        first = 4 + 8 * i
        here = slots(w_ref, first + 1, 8)
        w = here[:, :8]
        near = [roll(w, 1, 2), roll(w, -1, 2), roll(here, 1, 1)[:, :8], roll(here, -1, 1)[:, :8],
                slots(w_ref, first, 8)[:, :8], slots(w_ref, first + 2, 8)[:, :8]]
        total = None
        for k, value in enumerate(near):
            term = slots(lv.coef, k * lv.z + first, 8)[:, :8] * value
            total = term if total is None else total + term
        r = slots(lv.r, first, 8)[:, :8] - ((1.0 + SHIFT) * w - total)
        if beta is not None:
            x = slots(lv.x, first, 8)[:, :8] + w + (alpha * w + beta * r)
            r = x * slots(lv.root, first, 8)[:, :8]
        target = lv.r_next if beta is None else lv.x_next
        for n in range(8):
            target[pl.ds(pl.multiple_of((first + n) * 16, 16), 8), :] = r[n]

    def turn(i, carry):
        for part in range(4):
            body(4 * i + part)
        return carry

    lax.fori_loop(0, 2, turn, 0)
    if beta is None:
        lv.r, lv.r_next = lv.r_next, lv.r
    else:
        lv.x, lv.x_next = lv.x_next, lv.x


def compact(v):
    v = v.reshape(8, 4, 8, 128)
    v = [v[n] for n in range(8)]
    for bit in (iota(2) % 2, (iota(2) // 4) % 2, iota(1) % 2):
        v = [jnp.where(bit == 0, v[n], v[n + 1]) for n in range(0, len(v), 2)]
    return v[0]


def expand(ref, v):
    out = [v]
    for k, axis in ((1, 1), (4, 2), (1, 2)):
        bit = (iota(axis) // k) % 2
        out = [jnp.where(bit == m, w, roll(w, k if m == 0 else -k, axis)) for w in out for m in range(2)]
    for n in range(8):
        put(ref, 4 * n, out[n])


def fourth_neighbours(w):
    low0, low2, t = iota(2) % 2, (iota(2) // 4) % 2, (iota(2) // 2) % 2
    last, first = w[3:], w[:1]
    up = jnp.where(low0 == 0, roll(first, -1, 2),
                   jnp.where(low2 == 0, roll(first, -3, 2), roll(roll(first, 5, 2), -1, 1)))
    down = jnp.where(low0 == 1, roll(last, 1, 2),
                     jnp.where(low2 == 1, roll(last, 3, 2), roll(roll(last, -5, 2), 1, 1)))
    after, before = jnp.concatenate([w[1:], up], axis=0), jnp.concatenate([down, w[:3]], axis=0)
    return [roll(w, 8, 2), roll(w, -8, 2), roll(w, 2, 1), roll(w, -2, 1),
            jnp.where(t == 1, roll(w, 2, 2), roll(before, -2, 2)),
            jnp.where(t == 0, roll(w, -2, 2), roll(after, 2, 2))]


def fourth_coefs(lv, up):
    x_low, _, y_low, _, z_low, _ = fourth_neighbours(up)
    lows = [jnp.where(iota(2) % 32 < 8, 0.0, x_low), y_low, z_low]
    g = iota(2) // 32
    faces = []
    for k in range(3):
        for value in (lows[k], up):
            out = value
            for to in range(4):
                if to != k:
                    out = jnp.where(g == to, roll(value, 32 * (to - k), 2), out)
            faces.append(out)
    total = faces[0] + faces[1] + faces[2] + faces[3] + faces[4] + faces[5]
    scale = lax.rsqrt(total)
    put(lv.scale, 0, scale)
    put(lv.root, 0, scale * total)
    for k in range(6):
        put(lv.coef, 4 * k, scale * scale * faces[k])


def fourth_solve(lv, f):
    over_theta, steps = SOLVE
    coefs = [slots(lv.coef, 4 * k, 4, 8) for k in range(6)]
    r = slots(lv.scale, 0, 4, 8) * f
    w = x = r * over_theta
    for alpha, beta in steps:
        total = None
        for coef, value in zip(coefs, fourth_neighbours(w)):
            total = coef * value if total is None else total + coef * value
        r = r - ((1.0 + SHIFT) * w - total)
        w = alpha * w + beta * r
        x = x + w
    return x * slots(lv.root, 0, 4, 8)


def kernel(nx, ny, nz, f_hbm, a_hbm, out_ref, *scratch):
    refs = list(scratch)

    def take(count):
        got = refs[:count]
        del refs[:count]
        return got

    levels = [Level(*shape, take(12)) for shape in LEVELS]
    (fext, aext, ys, yr, zs, zr, tb, tmp, xg1, xgf, rxs, rxr, q1, qf, yg1, ygf, zh1, zhf, eb2, eb1, eb0) = take(21)
    (local_sem, strip_send, strip_recv, ex_send, ex_recv, xg_send, xg_recv, rx_send, rx_recv,
     h_send, h_recv, yg_send, yg_recv, yc_send, yc_recv, zg_send, zg_recv) = take(17)
    l0, l1, l2, l3, l4 = levels

    b, j, k = lax.axis_index("gx"), lax.axis_index("gy"), lax.axis_index("gz")
    sub, lane, lane16 = iota(1), iota(2), iota(2, (1, 16, 128))
    lane2 = lax.broadcasted_iota(jnp.int32, (1, 128), 1)

    def remote(src, dst, send, recv, **to):
        return pltpu.make_async_remote_copy(
            src_ref=src, dst_ref=dst, send_sem=send, recv_sem=recv, device_id=to, device_id_type=MESH)

    own_f = pltpu.make_async_copy(f_hbm, fext.at[:, pl.ds(4, 8)], local_sem.at[0])
    own_a = pltpu.make_async_copy(a_hbm, aext.at[pl.ds(0, 3), pl.ds(4, 8)], local_sem.at[1])
    own_a.start()
    own_f.start()
    zr[...] = jnp.zeros_like(zr)

    barrier = pltpu.get_barrier_semaphore()
    partners = [{"gx": lax.rem(b + t, 8)} for t in (1, 2, 4, 6, 7)]
    partners += [{"gy": lax.rem(j + t, 8)} for t in range(1, 8)]
    partners += [{"gz": lax.rem(k + t, 8)} for t in range(1, 8)]
    partners += [{"gy": lax.rem(j + t, 8), "gz": lax.rem(k + u, 8)} for t in (1, 7) for u in (1, 7)]
    partners += [{"gx": lax.rem(b + t, 8), "gz": lax.rem(k + u, 8)} for t in (2, 4, 6) for u in (1, 7)]
    for to in partners:
        pl.semaphore_signal(barrier, inc=1, device_id=to, device_id_type=MESH)

    fext[:, 0] = jnp.zeros((4, 8, 128), F32)
    fext[:, 15] = jnp.zeros((4, 8, 128), F32)
    aext[3] = jnp.zeros((16, 8, 128), F32)
    for n in (1, 2):
        aext[n, 0] = jnp.zeros((8, 128), F32)
        aext[n, 15] = jnp.zeros((8, 128), F32)
    for ref in (l0.f, l0.wa, l1.f, l1.up, eb1):
        ref[...] = jnp.zeros_like(ref)
    for lv in levels:
        for w in (lv.wa, lv.wb, lv.up):
            w[pl.ds(0, lv.rows), :] = jnp.zeros((lv.rows, 128), F32)
            w[pl.ds((lv.z + 1) * lv.rows, lv.rows), :] = jnp.zeros((lv.rows, 128), F32)
    pl.semaphore_wait(barrier, len(partners))

    b_up, b_down = lax.rem(b + 1, 8), lax.rem(b + 7, 8)
    strips = [
        remote(a_hbm.at[:, pl.ds(5, 3)], aext.at[pl.ds(0, 3), pl.ds(1, 3)],
               strip_send.at[0], strip_recv.at[0], gx=b_up),
        remote(a_hbm.at[:, pl.ds(0, 3)], aext.at[pl.ds(0, 3), pl.ds(12, 3)],
               strip_send.at[1], strip_recv.at[1], gx=b_down),
        remote(a_hbm.at[0, 4], aext.at[0, 0], strip_send.at[4], strip_recv.at[4], gx=b_up),
        remote(a_hbm.at[0, 3], aext.at[0, 15], strip_send.at[5], strip_recv.at[5], gx=b_down),
        remote(f_hbm.at[:, pl.ds(5, 3)], fext.at[:, pl.ds(1, 3)],
               strip_send.at[2], strip_recv.at[2], gx=b_up),
        remote(f_hbm.at[:, pl.ds(0, 3)], fext.at[:, pl.ds(12, 3)],
               strip_send.at[3], strip_recv.at[3], gx=b_down),
    ]
    for copy in strips[:4]:
        copy.start()
    for copy in strips[:4]:
        copy.wait_send()
    for copy in strips[4:]:
        copy.start()

    class Wide:
        def __init__(self, n, block, ref, base, h):
            self.n, self.block, self.ref, self.base, self.h = n, block, ref, base, h
            rows, part = pl.ds(0, h), pl.ds(0, h * 8)
            j_up, j_down = jnp.minimum(j + 1, 7), jnp.maximum(j - 1, 0)
            k_to = (lax.rem(k + 1, 8), lax.rem(k + 7, 8))

            def make(src, dst, index, **to):
                return remote(src, dst, ex_send.at[n, index], ex_recv.at[n, index], **to)

            self.up = [make(ys.at[n, 0, rows], yr.at[n, 0, rows], 0, gy=j_up)]
            self.down = [make(ys.at[n, 1, rows], yr.at[n, 1, rows], 1, gy=j_down)]
            self.flat = []
            for dz in range(2):
                self.flat.append(make(zs.at[n, dz, part], zr.at[n, dz, 0, part], 2 + dz, gz=k_to[dz]))
                self.up.append(make(zs.at[n, dz, part], zr.at[n, dz, 1, part], 4 + dz, gy=j_up, gz=k_to[dz]))
                self.down.append(make(zs.at[n, dz, part], zr.at[n, dz, 2, part], 6 + dz, gy=j_down, gz=k_to[dz]))

        def start(self):
            n, block, ref, base, h = self.n, self.block, self.ref, self.base, self.h
            for i in range(h):
                ys[n, 0, i] = ref[pl.ds((base + 4) * 16 + block - h + i, 64, stride=16), :]
                ys[n, 1, i] = ref[pl.ds((base + 4) * 16 + i, 64, stride=16), :]
                zs[n, 0, pl.ds(i * 8, 8), :] = ref[pl.ds((base + 68 - h + i) * 16, 8), :]
                zs[n, 1, pl.ds(i * 8, 8), :] = ref[pl.ds((base + 4 + i) * 16, 8), :]

            @pl.when(j < 7)
            def _():
                for copy in self.up:
                    copy.start()

            @pl.when(j > 0)
            def _():
                for copy in self.down:
                    copy.start()

            for copy in self.flat:
                copy.start()

        def finish(self):
            n, block, ref, base, h = self.n, self.block, self.ref, self.base, self.h

            @pl.when(j > 0)
            def _():
                for copy in self.up:
                    copy.wait_recv()
                for i in range(h):
                    ref[pl.ds((base + 4) * 16 + 16 - h + i, 64, stride=16), :] = yr[n, 0, i]

            @pl.when(j < 7)
            def _():
                for copy in self.down:
                    copy.wait_recv()
                for i in range(h):
                    ref[pl.ds((base + 4) * 16 + block + i, 64, stride=16), :] = yr[n, 1, i]

            for copy in self.flat:
                copy.wait_recv()
            for dz in range(2):
                here, low, high = (zr[n, dz, m, pl.ds(0, h * 8), :].reshape(h, 8, 128) for m in range(3))
                if block == 8:
                    pair = [here, jnp.where(sub < 4, high, low)]
                else:
                    pair = [jnp.where(sub < 4, here, roll(high, 4, 1)), roll(low, 4, 1)]
                v = jnp.concatenate(pair, axis=1)
                if block == 8:
                    if dz == 0:
                        v = roll(jnp.where(lane16 < 64, slots(ref, base + 68 - h, h), v), 64, 2)
                    else:
                        v = roll(jnp.where(lane16 < 64, v, slots(ref, base + 4, h)), 64, 2)
                put(ref, base + (4 - h if dz == 0 else 68), v)

            @pl.when(j < 7)
            def _():
                for copy in self.up:
                    copy.wait_send()

            @pl.when(j > 0)
            def _():
                for copy in self.down:
                    copy.wait_send()

            for copy in self.flat:
                copy.wait_send()

    half_lane = lax.broadcasted_iota(jnp.int32, (64, 128), 1) < 64

    def to_tiles(src, dst, base):
        for y in range(0, 8, 2):
            rows = [src[pl.ds(y + d, 64, stride=8), :] for d in range(2)]
            turned = jnp.concatenate(rows, axis=0).T
            low, high = turned[:64], turned[64:]
            first = (base + 4) * 16 + y
            dst[pl.ds(first, 64, stride=16), :] = jnp.where(half_lane, low, pltpu.roll(high, 64, 1))
            dst[pl.ds(first + 1, 64, stride=16), :] = jnp.where(half_lane, pltpu.roll(low, 64, 1), high)

    fext_rows, aext_rows = fext.reshape(512, 128), aext.reshape(512, 128)

    def x_gather(xg, n):
        other = b + 1 - 2 * lax.rem(b, 2)
        first = remote(xg.at[b], xg.at[b], xg_send.at[n, 0], xg_recv.at[n, 0], gx=other)
        early = [remote(xg.at[b], xg.at[b], xg_send.at[n, t], xg_recv.at[n, t], gx=lax.rem(b + 2 * t, 8))
                 for t in range(1, 4)]
        second = [remote(xg.at[other], xg.at[other], xg_send.at[n, 3 + t], xg_recv.at[n, 3 + t],
                         gx=lax.rem(b + 2 * t, 8)) for t in range(1, 4)]
        for copy in [first] + early:
            copy.start()
        return first, early, second

    def x_pack(weight, xg, faces=False):
        source = lax.broadcasted_iota(jnp.int32, (128, 256), 0)
        target = lax.broadcasted_iota(jnp.int32, (128, 256), 1)
        slot, inner = source % 16, (target % 128) % 32
        hit = (source // 64 == target // 128) & ((source % 64) // 16 == (target % 128) // 32) & (inner < 4)
        pair = (slot // 2 == inner + 2) & hit
        if faces:
            pair = pair & (((source % 64) // 16 != 0) | (slot % 2 == 1))
        matrix = jnp.where(pair, weight, 0.0).astype(F32)
        moved = jnp.dot(tb[...], matrix, precision=HIGHEST, preferred_element_type=F32)
        parts = [moved[:, :128].reshape(32, 8, 128), moved[:, 128:].reshape(32, 8, 128)]
        total = None
        for g in range(8):
            part = roll(parts[g // 4][(g % 4) * 8:(g % 4) * 8 + 8], 4 * g, 2)
            total = part if total is None else total + part
        packed = jnp.where(sub % 2 == 0, total[:4], total[4:])
        xg[b] = packed.reshape(32, 128)

    def x_unpack(xg, dst, base):
        g = (lane // 4) % 8
        for q in range(4):
            for odd in range(2):
                v = []
                for n in range(8):
                    tile = xg[n, pl.ds(q * 8, 8), :].reshape(1, 8, 128)
                    v.append(jnp.where(sub % 2 == 1, tile, roll(tile, -1, 1)) if odd
                             else jnp.where(sub % 2 == 0, tile, roll(tile, 1, 1)))
                for s in (1, 2, 4):
                    high = (g // s) % 2 == 1
                    for n in range(8):
                        if n & s == 0:
                            lo, hi = v[n], v[n + s]
                            v[n] = jnp.where(high, roll(hi, 4 * s, 2), lo)
                            v[n + s] = jnp.where(high, hi, roll(lo, -4 * s, 2))
                for n in range(8):
                    put(tmp, n * 8 + 4 * odd + q, v[n])
        for i in range(4):
            dst[pl.ds((base + 4) * 16 + i, 64, stride=16), :] = tmp[pl.ds(2 * i, 64, stride=8), :]

    own_a.wait()
    for copy in strips[:4]:
        copy.wait_recv()
    to_tiles(aext_rows, l0.wa, 1)
    edges = Wide(0, 8, l0.wa, 1, 4)
    edges.start()
    edges.finish()
    group0 = (lane16 // 16) % 4
    row16 = iota(1, (1, 16, 128))
    x_at = 8 * b + lane16 % 16 - 4
    y_at = 8 * j + jnp.where(row16 < 12, row16, row16 - 16)

    def face_body(i):
        a, xd, xu, yd, yu, zd, zu = neighbours(l0, l0.wa, i)
        z_at = 128 * k + 64 * (iota(2, a.shape) // 64) + i * l0.ch - 4 + iota(0, a.shape)
        side_up = jnp.where(group0 == 0, xu, jnp.where(group0 == 1, yu, zu))
        side_low = jnp.where(group0 == 0, xd, jnp.where(group0 == 1, yd, zd))
        where = jnp.where(group0 == 0, x_at, jnp.where(group0 == 1, y_at, z_at))
        end = jnp.where(group0 == 0, nx - 1, jnp.where(group0 == 1, ny - 1, nz - 1))
        l0.put(l0.up, i, jnp.where(where == end, 0.0, 0.5 * (a + side_up)))
        l0.put(l0.low, i, jnp.where(where == 0, 0.0, 0.5 * (a + side_low)))

    l0.loop(face_body)

    own_f.wait()
    for copy in strips[4:]:
        copy.wait_recv()
    to_tiles(fext_rows, l0.f, 0)
    edges = Wide(1, 8, l0.f, 0, 3)
    edges.start()

    def body(i):
        put(tb, i * 16, coarse_faces(*own_pairs(l0.up, i), 16, 1, None))

    loop(2, body)
    x_pack(0.25, xgf, True)
    faces_first, faces_early, faces_second = x_gather(xgf, 1)
    make_coefs(l0, 16)

    edges.finish()

    over_theta, ((a1, b1), (a2, b2)) = SMOOTH

    def downward(lv):
        init_down(lv, over_theta)
        step(lv, lv.wa, lv.wb, a1, b1, add="w")
        step(lv, lv.wb, lv.wa, a2, b2, add="x")
        if lv in (l0, l1):
            own_step(lv, lv.wa)
        else:
            step(lv, lv.wa, None)

    def upward(lv, coarse_at):
        init_up(lv, coarse_at)
        step(lv, lv.wa, lv.wb, None, over_theta, add="xw")
        step(lv, lv.wb, lv.wa, a1, b1)
        if lv in (l0, l1):
            own_step(lv, lv.wa, a2, b2)
        else:
            step(lv, lv.wa, None, a2, b2, add="xw", last=True)

    def own_sums(lv, i):
        pairs, roots = own_pairs(lv.r, i), own_pairs(lv.root, i)
        return pairs[0] * roots[0] + pairs[1] * roots[1]

    downward(l0)

    def body(i):
        put(tb, i * 16, both(own_sums(l0, i), 1, 1))

    loop(2, body)
    x_pack(0.125, xg1)
    right_first, right_early, right_second = x_gather(xg1, 0)
    faces_first.wait_recv()
    for copy in faces_second:
        copy.start()

    slot = lane % 16
    for side, first in ((0, 10), (1, 4)):
        packed = jnp.zeros((8, 8, 128), F32)
        for g in range(8):
            v = slots(l0.r, 4 + 8 * g, 8)[:, :8]
            packed = jnp.where(slot // 2 == g, roll(v, 2 * g - first, 2), packed)
        rxs[side] = packed.reshape(64, 128)
    rx = [remote(rxs.at[0], rxr.at[0], rx_send.at[0], rx_recv.at[0], gx=b_up),
          remote(rxs.at[1], rxr.at[1], rx_send.at[1], rx_recv.at[1], gx=b_down)]

    for copy in faces_early + faces_second:
        copy.wait_recv()
    x_unpack(xgf, l1.up, 1)
    edges = Wide(2, 4, l1.up, 1, 4)
    edges.start()

    c = b // 2

    def second_pack(q):
        start = pl.multiple_of(c * 64, 64)
        q[...] = jnp.where(lane2 % 2 == 0, tb[pl.ds(start, 8, stride=8), :], tb[pl.ds(start + 2, 8, stride=8), :])

    class Second:
        def __init__(self, q, yg, zh, n):
            yg[c, j] = q[...]
            self.along = [remote(q, yg.at[c, j], yg_send.at[n, t], yg_recv.at[n, t], gy=lax.rem(j + t, 8))
                          for t in range(1, 8)]
            self.quarters = [remote(yg.at[c], yg.at[c], yc_send.at[n, t], yc_recv.at[n, t], gx=lax.rem(b + 2 * t, 8))
                             for t in range(1, 4)]
            self.above = [remote(yg.at[3], zh.at[0], h_send.at[n, 0, t], h_recv.at[n, 0],
                                 gx=lax.rem(b + 2 * t, 8), gz=lax.rem(k + 1, 8)) for t in range(4)]
            self.below = [remote(yg.at[0], zh.at[1], h_send.at[n, 1, t], h_recv.at[n, 1],
                                 gx=lax.rem(b + 2 * t, 8), gz=lax.rem(k + 7, 8)) for t in range(4)]
            self.yg, self.zh = yg, zh
            for copy in self.along:
                copy.start()

        def spread(self):
            for copy in self.along:
                copy.wait_recv()
            for copy in self.quarters:
                copy.start()

            @pl.when(c == 3)
            def _():
                for copy in self.above:
                    copy.start()

            @pl.when(c == 0)
            def _():
                for copy in self.below:
                    copy.start()

        def finish(self, dst, base):
            for copy in self.quarters + [self.above[0], self.below[0]]:
                copy.wait_recv()
            yg, zh = self.yg, self.zh
            for n in range(8):
                v = jnp.concatenate([zh[0, n]] + [yg[m, n] for m in range(4)] + [zh[1, n]], axis=0)
                dst[pl.ds(base * 16 + 2 * n, 48, stride=16), :] = jnp.where(lane2 % 2 == 0, v, roll(v, 1, 1))
                dst[pl.ds(base * 16 + 2 * n + 1, 48, stride=16), :] = jnp.where(lane2 % 2 == 1, v, roll(v, -1, 1))

        def wait_send(self):
            for copy in self.along + self.quarters:
                copy.wait_send()

            @pl.when(c == 3)
            def _():
                for copy in self.above:
                    copy.wait_send()

            @pl.when(c == 0)
            def _():
                for copy in self.below:
                    copy.wait_send()

    def body(i):
        put(tb, i * 16, 0.25 * coarse_faces(*own_pairs(l1.up, i, 1), 32, 1, 1))

    loop(2, body)
    second_pack(qf)
    faces_second_level = Second(qf, ygf, zhf, 0)
    edges.finish()
    right_first.wait_recv()
    for copy in right_second:
        copy.start()
    make_coefs(l1, 32)

    for copy in right_early + right_second:
        copy.wait_recv()
    x_unpack(xg1, l1.f, 0)
    edges = Wide(3, 4, l1.f, 0, 3)
    edges.start()
    edges.finish()
    faces_second_level.spread()
    downward(l1)

    def body(i):
        put(tb, i * 16, 0.125 * both(both(own_sums(l1, i), 1, 1), 1, 2))

    loop(2, body)
    second_pack(q1)
    right_second_level = Second(q1, yg1, zh1, 1)
    faces_second_level.finish(l2.up, 1)

    t = lane % 4

    def third(ref, faces=False):
        first_row = 144 if faces else 128
        even, odd = (ref[pl.ds(first_row + d, 256, stride=2), :].reshape(16, 2, 8, 128) for d in range(2))
        if faces:
            g = lane // 32
            first, second = (jnp.where(g == 1, odd[:, d], even[:, d] + odd[:, d]) for d in range(2))
            v = jnp.where(g == 2, second, first + second)
            v = 0.25 * jnp.where(g == 0, pick(v, 2, 2), both(v, 2, 2))
        else:
            roots = [l2.root[pl.ds(128 + d, 256, stride=2), :].reshape(16, 2, 8, 128) for d in range(2)]
            v = even * roots[0] + odd * roots[1]
            v = 0.125 * both(v[:, 0] + v[:, 1], 2, 2)
        v = v.reshape(4, 4, 8, 128)
        out = v[:, 0]
        for u in range(1, 4):
            out = jnp.where(t == u, v[:, u], out)
        return out

    def z_gather(g, n, base):
        rows = pl.ds(pl.multiple_of((4 * k + base) * 8, 8), 32)
        return [remote(g.at[rows], g.at[rows], zg_send.at[n, u], zg_recv.at[n, u], gz=lax.rem(k + u, 8))
                for u in range(1, 8)]

    put(l3.up, 4 * k + 1, third(l2.up, True))
    third_faces = z_gather(l3.up, 0, 1)

    for copy in third_faces:
        copy.start()
    make_coefs(l2, 32)
    right_second_level.spread()
    for copy in rx:
        copy.start()
    for copy in third_faces:
        copy.wait_recv()
    make_coefs(l3, 32)

    group = lane // 32
    v = slots(l3.up, 1, 32, 8)
    v = jnp.where(group == 2, pick(v, 1, 2), both(v, 1, 2))
    v = jnp.where(group == 1, pick(v, 1, 1), both(v, 1, 1))
    fourth_coefs(l4, 0.25 * compact(jnp.where(group == 0, pick(v, 4, 2), both(v, 4, 2))))
    right_second_level.finish(l2.f, 0)
    edges1 = Wide(4, 4, l1.r, 0, 2)
    edges1.start()
    downward(l2)
    put(l3.f, 4 * k, third(l2.r))
    third_right = z_gather(l3.f, 1, 0)
    for copy in third_right:
        copy.start()

    edges1.finish()
    for copy in third_right:
        copy.wait_recv()

    downward(l3)

    v = slots(l3.r, 0, 32, 8) * slots(l3.root, 0, 32, 8)
    expand(l4.x, fourth_solve(l4, 0.125 * compact(both(both(both(v, 1, 2), 1, 1), 4, 2))))
    upward(l3, lambda i: l4.get(l4.x, i))

    for q in range(6):
        v = l3.x[pl.ds(pl.multiple_of(lax.rem(4 * k + q + 31, 32) * 8, 8), 8), :].reshape(1, 8, 128)
        for z in range(4):
            moved = v
            for u in range(4):
                if u != z:
                    moved = jnp.where(t == u, roll(v, u - z, 2), moved)
            first = (4 * q + z) * 16
            eb2[pl.ds(first, 8, stride=2), :] = moved.reshape(8, 128)
            eb2[pl.ds(first + 1, 8, stride=2), :] = moved.reshape(8, 128)

    def twice(ref, offset):
        def chunk(i):
            v = slots(ref, i * 4 + offset, 4)
            return jnp.broadcast_to(v[:, None], (4, 2, 16, 128)).reshape(8, 16, 128)

        return chunk

    upward(l2, twice(eb2, 0))

    for copy in rx:
        copy.wait_recv()
    for g in range(8):
        v = slots(l0.r, 4 + 8 * g, 8)
        own = v[:, :8]
        own = jnp.where(slot // 2 == 1, roll(rxr[0].reshape(8, 8, 128), 2 - 2 * g, 2), own)
        own = jnp.where(slot // 2 == 6, roll(rxr[1].reshape(8, 8, 128), 12 - 2 * g, 2), own)
        put(l0.r, 4 + 8 * g, jnp.concatenate([own, v[:, 8:]], axis=1))
    edges0 = Wide(5, 8, l0.r, 0, 2)
    edges0.start()

    for i, from_y in ((0, 0), (1, 1), (2, 2), (3, 3), (6, 14), (7, 15)):
        v = l2.x[pl.ds(lax.rem(2 * j + from_y, 16), 48, stride=16), :]
        eb1[pl.ds(2 * i, 48, stride=16), :] = v
        eb1[pl.ds(2 * i + 1, 48, stride=16), :] = v
    upward(l1, twice(eb1, 6))
    edges = Wide(6, 4, l1.x, 0, 2)
    edges.start()
    edges0.finish()
    edges.finish()

    source = lax.broadcasted_iota(jnp.int32, (128, 128), 0)
    target = lax.broadcasted_iota(jnp.int32, (128, 128), 1)
    hit = (source // 32 == (target % 64) // 16) & (source % 32 == 4 * b - 2 + (target % 16) // 2)
    v = slots(l1.x, 0, 72)
    v = jnp.where(sub < 6, v[:, :8], v[:, 8:]).reshape(576, 128)
    v = jnp.dot(v, jnp.where(hit, 1.0, 0.0).astype(F32), precision=HIGHEST, preferred_element_type=F32)
    eb0[pl.ds(0, 576, stride=2), :] = v
    eb0[pl.ds(1, 576, stride=2), :] = v

    def top_chunk(i):
        v = jnp.where(lane16 < 64, slots(eb0, i * 4 + 2, 4), slots(eb0, i * 4 + 34, 4))
        return jnp.broadcast_to(v[:, None], (4, 2, 16, 128)).reshape(8, 16, 128)

    upward(l0, top_chunk)

    for y in range(0, 8, 2):
        first = l0.x[pl.ds(64 + y, 64, stride=16), :]
        second = l0.x[pl.ds(65 + y, 64, stride=16), :]
        low = jnp.where(half_lane, first, pltpu.roll(second, 64, 1))
        high = jnp.where(half_lane, pltpu.roll(first, 64, 1), second)
        turned = pltpu.roll(jnp.concatenate([low, high], axis=0), 124, 1).T
        for d in range(2):
            for v in range(4):
                start = d * 64 + v * 16
                out_ref[pl.ds(v * 64 + y + d, 8, stride=8), :] = turned[start:start + 8]

    for copy in (strips[4:] + [faces_first, right_first] + faces_early + right_early + faces_second + right_second + rx
                 + third_faces + third_right):
        copy.wait_send()
    faces_second_level.wait_send()
    right_second_level.wait_send()


def solution(mesh):
    def per_device(right_side, affinity):
        nx = affinity.shape[1] * mesh.shape["gx"]
        ny = affinity.shape[2] * mesh.shape["gy"]
        nz = affinity.shape[3] * mesh.shape["gz"]
        scratch = []
        for z, rows, *_ in LEVELS:
            scratch += level_shapes(z, rows)
        scratch += [pltpu.VMEM(shape, F32) for shape in (
            (4, 16, 8, 128), (4, 16, 8, 128),
            (7, 2, 4, 64, 128), (7, 2, 4, 64, 128), (7, 2, 32, 128), (7, 2, 3, 32, 128),
            (256, 128), (512, 128), (8, 32, 128), (8, 32, 128), (2, 64, 128), (2, 64, 128),
            (8, 128), (8, 128), (4, 8, 8, 128), (4, 8, 8, 128), (2, 8, 8, 128), (2, 8, 8, 128), (384, 128), (768, 128), (1152, 128))]
        dma = pltpu.SemaphoreType.DMA
        scratch += [dma(shape) for shape in (
            (2,), (6,), (6,), (7, 8), (7, 8), (2, 7), (2, 7), (2,), (2,), (2, 2, 4), (2, 2), (2, 8), (2, 8), (2, 4), (2, 4), (2, 8), (2, 8))]
        out = pl.pallas_call(
            functools.partial(kernel, nx, ny, nz),
            out_shape=jax.ShapeDtypeStruct((256, 128), F32),
            in_specs=[pl.BlockSpec(memory_space=pl.ANY)] * 2,
            out_specs=pl.BlockSpec(memory_space=pltpu.VMEM),
            scratch_shapes=scratch,
            compiler_params=pltpu.CompilerParams(
                collective_id=0, has_side_effects=True, vmem_limit_bytes=60 * 1024 * 1024),
        )(right_side, affinity)
        return out.reshape(right_side.shape)

    spec = P(None, "gx", "gy", "gz")
    return jax.shard_map(per_device, mesh=mesh, in_specs=(spec, spec), out_specs=spec, check_vma=False)
```

```python
import functools

import jax
import jax.numpy as jnp
from jax import lax
from jax.experimental import pallas as pl
from jax.experimental.pallas import tpu as pltpu
from jax.sharding import PartitionSpec as P

MESH = pl.DeviceIdType.MESH
HIGHEST = lax.Precision.HIGHEST
F32 = jnp.float32

DEGREE = 3
COARSE_DEGREE = 8
SHIFT = 0.02
SMOOTH_LOWER = 0.5
UPPER = 2.0 + SHIFT


def cheb_coefs(a, b, m):
    theta, delta = 0.5 * (b + a), 0.5 * (b - a)
    sigma = theta / delta
    rho = 1.0 / sigma
    steps = []
    for _ in range(m - 1):
        nxt = 1.0 / (2.0 * sigma - rho)
        steps.append((nxt * rho, 2.0 * nxt / delta))
        rho = nxt
    return 1.0 / theta, steps


SMOOTH = cheb_coefs(SMOOTH_LOWER, UPPER, DEGREE)
SOLVE = cheb_coefs(SHIFT, UPPER, COARSE_DEGREE)


def iota(dim, shape=(1, 8, 128)):
    return lax.broadcasted_iota(jnp.int32, shape, dim)


def roll(x, shift, axis):
    shift = shift % x.shape[axis]
    return x if shift == 0 else pltpu.roll(x, shift, axis)


def both(x, k, axis):
    bit = (iota(axis, (1,) + x.shape[1:]) // k) % 2
    return x + jnp.where(bit == 0, roll(x, -k, axis), roll(x, k, axis))


def pick(x, k, axis):
    bit = (iota(axis, (1,) + x.shape[1:]) // k) % 2
    return jnp.where(bit == 1, x, roll(x, -k, axis))


def slots(ref, start, count, rows=16):
    if not isinstance(start, int):
        start = pl.multiple_of(start * rows, rows)
    else:
        start = start * rows
    return ref[pl.ds(start, count * rows), :].reshape(count, rows, 128)


def put(ref, start, value):
    count, rows = value.shape[:2]
    if not isinstance(start, int):
        start = pl.multiple_of(start * rows, rows)
    else:
        start = start * rows
    ref[pl.ds(start, count * rows), :] = value.reshape(count * rows, 128)


def loop(count, body):
    def run(i, carry):
        body(i)
        return carry

    lax.fori_loop(0, count, run, 0)


class Level:
    def __init__(self, z, rows, sy, sx, mode, refs):
        self.z, self.rows, self.sy, self.sx, self.mode = z, rows, sy, sx, mode
        self.ch = 128 // rows
        self.parts = z // self.ch if rows == 8 else 3
        (self.coef, self.scale, self.root, self.f, self.r, self.x, self.wa, self.wb, self.up, self.low,
         self.r_next, self.x_next) = refs

    def loop(self, body):
        def turn(i, carry):
            for part in range(self.parts):
                body(i * self.parts + part)
            return carry

        turns = self.z // (self.ch * self.parts)
        if turns == 1:
            turn(0, 0)
        else:
            lax.fori_loop(0, turns, turn, 0)

    def get(self, ref, i, offset=0):
        return slots(ref, i * self.ch + offset, self.ch, self.rows)

    def put(self, ref, i, value, offset=0):
        put(ref, i * self.ch + offset, value)


LEVELS = ((72, 16, 1, 1, 0), (72, 16, 1, 1, 0), (24, 16, 1, 2, 0), (32, 8, 1, 4, 1), (32, 8, 2, 8, 2))


def level_shapes(z, rows):
    n = z * rows
    pad = (z + 2) * rows
    return [pltpu.VMEM((6 * n, 128), F32)] + [pltpu.VMEM((n, 128), F32)] * 5 + [pltpu.VMEM((pad, 128), F32)] * 4 + [
        pltpu.VMEM((n, 128), F32)] * 2


def join_halves(ref):
    odd = iota(2, (1, 16, 128)) % 2 == 1
    put(ref, 0, jnp.where(odd, roll(slots(ref, 24, 1), 1, 2), 0.0))
    put(ref, 25, jnp.where(odd, 0.0, roll(slots(ref, 1, 1), -1, 2)))


def neighbours(lv, w_ref, i):
    w, before, after = lv.get(w_ref, i, 1), lv.get(w_ref, i, 0), lv.get(w_ref, i, 2)
    xd, xu = roll(w, lv.sx, 2), roll(w, -lv.sx, 2)
    yd, yu = roll(w, lv.sy, 1), roll(w, -lv.sy, 1)
    if lv.mode == 0:
        zd, zu = before, after
    else:
        s = lv.mode
        t = iota(2) % 4
        zu = jnp.where(t < 4 - s, roll(w, -s, 2), roll(after, 4 - s, 2))
        zd = jnp.where(t >= s, roll(w, s, 2), roll(before, s - 4, 2))
    return w, xd, xu, yd, yu, zd, zu


def init_down(lv, over_theta):
    def body(i):
        r = lv.get(lv.scale, i) * lv.get(lv.f, i)
        lv.put(lv.r, i, r)
        lv.put(lv.wa, i, r * over_theta, 1)

    lv.loop(body)


def init_up(lv, coarse_at):
    def body(i):
        lv.put(lv.wa, i, lv.get(lv.scale, i) * coarse_at(i), 1)

    lv.loop(body)


def step(lv, w_ref, w_next, alpha=None, beta=None, add="", last=False):
    if lv.z == 24:
        join_halves(w_ref)

    def body(i):
        w, *near = neighbours(lv, w_ref, i)
        total = None
        for k, value in enumerate(near):
            term = slots(lv.coef, k * lv.z + i * lv.ch, lv.ch, lv.rows) * value
            total = term if total is None else total + term
        r = lv.get(lv.r, i) - ((1.0 + SHIFT) * w - total)
        if not last:
            lv.put(lv.r_next, i, r)
        if beta is None:
            return
        new = beta * r if alpha is None else alpha * w + beta * r
        if add:
            x = new + w if "w" in add else new
            if "x" in add:
                x = x + lv.get(lv.x, i)
            lv.put(lv.x_next, i, x * lv.get(lv.root, i) if last else x)
        if not last:
            lv.put(w_next, i, new, 1)

    lv.loop(body)
    if not last:
        lv.r, lv.r_next = lv.r_next, lv.r
    if add:
        lv.x, lv.x_next = lv.x_next, lv.x


def make_coefs(lv, group):
    g = (iota(2, (1, lv.rows, 128)) // group) % 4

    def spread(value, k):
        out = value
        for to in range(4):
            if to != k:
                out = jnp.where(g == to, roll(value, group * (to - k), 2), out)
        return out

    if lv.z == 24:
        join_halves(lv.up)

    def body(i):
        if group == 16:
            up = lv.get(lv.up, i)
            lows = [lv.get(lv.low, i)] * 3
        else:
            up, x_low, _, y_low, _, z_low, _ = neighbours(lv, lv.up, i)
            lows = [jnp.where(iota(2, (1, lv.rows, 128)) % 32 < lv.sx, 0.0, x_low), y_low, z_low]
        faces = []
        for k in range(3):
            faces += [spread(lows[k], k), spread(up, k)]
        total = faces[0] + faces[1] + faces[2] + faces[3] + faces[4] + faces[5]
        scale = jnp.where(total > 0.0, lax.rsqrt(total), 0.0)
        lv.put(lv.scale, i, scale)
        lv.put(lv.root, i, scale * total)
        square = scale * scale
        for k in range(6):
            put(lv.coef, k * lv.z + i * lv.ch, square * faces[k])

    lv.loop(body)


def own_pairs(ref, i, base=0):
    v = slots(ref, base + 4 + 32 * i, 32)[:, :8].reshape(16, 2, 8, 128)
    return v[:, 0], v[:, 1]


def coarse_faces(first, second, group, ky, kx):
    g = (iota(2) // group) % 4
    v = jnp.where(g == 2, second, first + second)
    v = jnp.where(g == 1, pick(v, ky, 1), both(v, ky, 1))
    if kx is not None:
        v = jnp.where(g == 0, pick(v, kx, 2), both(v, kx, 2))
    return v


def own_step(lv, w_ref, alpha=None, beta=None):
    def body(i):
        first = 4 + 8 * i
        here = slots(w_ref, first + 1, 8)
        w = here[:, :8]
        near = [roll(w, 1, 2), roll(w, -1, 2), roll(here, 1, 1)[:, :8], roll(here, -1, 1)[:, :8],
                slots(w_ref, first, 8)[:, :8], slots(w_ref, first + 2, 8)[:, :8]]
        total = None
        for k, value in enumerate(near):
            term = slots(lv.coef, k * lv.z + first, 8)[:, :8] * value
            total = term if total is None else total + term
        r = slots(lv.r, first, 8)[:, :8] - ((1.0 + SHIFT) * w - total)
        if beta is not None:
            x = slots(lv.x, first, 8)[:, :8] + w + (alpha * w + beta * r)
            r = x * slots(lv.root, first, 8)[:, :8]
        target = lv.r_next if beta is None else lv.x_next
        for n in range(8):
            target[pl.ds(pl.multiple_of((first + n) * 16, 16), 8), :] = r[n]

    def turn(i, carry):
        for part in range(4):
            body(4 * i + part)
        return carry

    lax.fori_loop(0, 2, turn, 0)
    if beta is None:
        lv.r, lv.r_next = lv.r_next, lv.r
    else:
        lv.x, lv.x_next = lv.x_next, lv.x


def compact(v):
    v = v.reshape(8, 4, 8, 128)
    v = [v[n] for n in range(8)]
    for bit in (iota(2) % 2, (iota(2) // 4) % 2, iota(1) % 2):
        v = [jnp.where(bit == 0, v[n], v[n + 1]) for n in range(0, len(v), 2)]
    return v[0]


def expand(ref, v):
    out = [v]
    for k, axis in ((1, 1), (4, 2), (1, 2)):
        bit = (iota(axis) // k) % 2
        out = [jnp.where(bit == m, w, roll(w, k if m == 0 else -k, axis)) for w in out for m in range(2)]
    for n in range(8):
        put(ref, 4 * n, out[n])


def fourth_neighbours(w):
    low0, low2, t = iota(2) % 2, (iota(2) // 4) % 2, (iota(2) // 2) % 2
    last, first = w[3:], w[:1]
    up = jnp.where(low0 == 0, roll(first, -1, 2),
                   jnp.where(low2 == 0, roll(first, -3, 2), roll(roll(first, 5, 2), -1, 1)))
    down = jnp.where(low0 == 1, roll(last, 1, 2),
                     jnp.where(low2 == 1, roll(last, 3, 2), roll(roll(last, -5, 2), 1, 1)))
    after, before = jnp.concatenate([w[1:], up], axis=0), jnp.concatenate([down, w[:3]], axis=0)
    return [roll(w, 8, 2), roll(w, -8, 2), roll(w, 2, 1), roll(w, -2, 1),
            jnp.where(t == 1, roll(w, 2, 2), roll(before, -2, 2)),
            jnp.where(t == 0, roll(w, -2, 2), roll(after, 2, 2))]


def fourth_coefs(lv, up):
    x_low, _, y_low, _, z_low, _ = fourth_neighbours(up)
    lows = [jnp.where(iota(2) % 32 < 8, 0.0, x_low), y_low, z_low]
    g = iota(2) // 32
    faces = []
    for k in range(3):
        for value in (lows[k], up):
            out = value
            for to in range(4):
                if to != k:
                    out = jnp.where(g == to, roll(value, 32 * (to - k), 2), out)
            faces.append(out)
    total = faces[0] + faces[1] + faces[2] + faces[3] + faces[4] + faces[5]
    scale = lax.rsqrt(total)
    put(lv.scale, 0, scale)
    put(lv.root, 0, scale * total)
    for k in range(6):
        put(lv.coef, 4 * k, scale * scale * faces[k])


def fourth_solve(lv, f):
    over_theta, steps = SOLVE
    coefs = [slots(lv.coef, 4 * k, 4, 8) for k in range(6)]
    r = slots(lv.scale, 0, 4, 8) * f
    w = x = r * over_theta
    for alpha, beta in steps:
        total = None
        for coef, value in zip(coefs, fourth_neighbours(w)):
            total = coef * value if total is None else total + coef * value
        r = r - ((1.0 + SHIFT) * w - total)
        w = alpha * w + beta * r
        x = x + w
    return x * slots(lv.root, 0, 4, 8)


def kernel(nx, ny, nz, f_hbm, a_hbm, out_ref, *scratch):
    refs = list(scratch)

    def take(count):
        got = refs[:count]
        del refs[:count]
        return got

    levels = [Level(*shape, take(12)) for shape in LEVELS]
    (fext, aext, ys, yr, zs, zr, tb, tmp, xg1, xgf, rxs, rxr, q1, qf, yg1, ygf, zh1, zhf, eb2, eb1, eb0) = take(21)
    (local_sem, strip_send, strip_recv, ex_send, ex_recv, xg_send, xg_recv, rx_send, rx_recv,
     h_send, h_recv, yg_send, yg_recv, yc_send, yc_recv, zg_send, zg_recv) = take(17)
    l0, l1, l2, l3, l4 = levels

    b, j, k = lax.axis_index("gx"), lax.axis_index("gy"), lax.axis_index("gz")
    sub, lane, lane16 = iota(1), iota(2), iota(2, (1, 16, 128))
    lane2 = lax.broadcasted_iota(jnp.int32, (1, 128), 1)

    def remote(src, dst, send, recv, **to):
        return pltpu.make_async_remote_copy(
            src_ref=src, dst_ref=dst, send_sem=send, recv_sem=recv, device_id=to, device_id_type=MESH)

    own_f = pltpu.make_async_copy(f_hbm, fext.at[:, pl.ds(4, 8)], local_sem.at[0])
    own_a = pltpu.make_async_copy(a_hbm, aext.at[pl.ds(0, 3), pl.ds(4, 8)], local_sem.at[1])
    own_a.start()
    own_f.start()
    zr[...] = jnp.zeros_like(zr)

    barrier = pltpu.get_barrier_semaphore()
    partners = [{"gx": lax.rem(b + t, 8)} for t in (1, 2, 4, 6, 7)]
    partners += [{"gy": lax.rem(j + t, 8)} for t in range(1, 8)]
    partners += [{"gz": lax.rem(k + t, 8)} for t in range(1, 8)]
    partners += [{"gy": lax.rem(j + t, 8), "gz": lax.rem(k + u, 8)} for t in (1, 7) for u in (1, 7)]
    partners += [{"gx": lax.rem(b + t, 8), "gz": lax.rem(k + u, 8)} for t in (2, 4, 6) for u in (1, 7)]
    for to in partners:
        pl.semaphore_signal(barrier, inc=1, device_id=to, device_id_type=MESH)

    fext[:, 0] = jnp.zeros((4, 8, 128), F32)
    fext[:, 15] = jnp.zeros((4, 8, 128), F32)
    aext[3] = jnp.zeros((16, 8, 128), F32)
    for n in (1, 2):
        aext[n, 0] = jnp.zeros((8, 128), F32)
        aext[n, 15] = jnp.zeros((8, 128), F32)
    for ref in (l0.f, l0.wa, l1.f, l1.up, eb1):
        ref[...] = jnp.zeros_like(ref)
    for lv in levels:
        for w in (lv.wa, lv.wb, lv.up):
            w[pl.ds(0, lv.rows), :] = jnp.zeros((lv.rows, 128), F32)
            w[pl.ds((lv.z + 1) * lv.rows, lv.rows), :] = jnp.zeros((lv.rows, 128), F32)
    pl.semaphore_wait(barrier, len(partners))

    b_up, b_down = lax.rem(b + 1, 8), lax.rem(b + 7, 8)
    strips = [
        remote(a_hbm.at[:, pl.ds(5, 3)], aext.at[pl.ds(0, 3), pl.ds(1, 3)],
               strip_send.at[0], strip_recv.at[0], gx=b_up),
        remote(a_hbm.at[:, pl.ds(0, 3)], aext.at[pl.ds(0, 3), pl.ds(12, 3)],
               strip_send.at[1], strip_recv.at[1], gx=b_down),
        remote(a_hbm.at[0, 4], aext.at[0, 0], strip_send.at[4], strip_recv.at[4], gx=b_up),
        remote(a_hbm.at[0, 3], aext.at[0, 15], strip_send.at[5], strip_recv.at[5], gx=b_down),
        remote(f_hbm.at[:, pl.ds(5, 3)], fext.at[:, pl.ds(1, 3)],
               strip_send.at[2], strip_recv.at[2], gx=b_up),
        remote(f_hbm.at[:, pl.ds(0, 3)], fext.at[:, pl.ds(12, 3)],
               strip_send.at[3], strip_recv.at[3], gx=b_down),
    ]
    for copy in strips[:4]:
        copy.start()
    for copy in strips[:4]:
        copy.wait_send()
    for copy in strips[4:]:
        copy.start()

    class Wide:
        def __init__(self, n, block, ref, base, h):
            self.n, self.block, self.ref, self.base, self.h = n, block, ref, base, h
            rows, part = pl.ds(0, h), pl.ds(0, h * 8)
            j_up, j_down = jnp.minimum(j + 1, 7), jnp.maximum(j - 1, 0)
            k_to = (lax.rem(k + 1, 8), lax.rem(k + 7, 8))

            def make(src, dst, index, **to):
                return remote(src, dst, ex_send.at[n, index], ex_recv.at[n, index], **to)

            self.up = [make(ys.at[n, 0, rows], yr.at[n, 0, rows], 0, gy=j_up)]
            self.down = [make(ys.at[n, 1, rows], yr.at[n, 1, rows], 1, gy=j_down)]
            self.flat = []
            for dz in range(2):
                self.flat.append(make(zs.at[n, dz, part], zr.at[n, dz, 0, part], 2 + dz, gz=k_to[dz]))
                self.up.append(make(zs.at[n, dz, part], zr.at[n, dz, 1, part], 4 + dz, gy=j_up, gz=k_to[dz]))
                self.down.append(make(zs.at[n, dz, part], zr.at[n, dz, 2, part], 6 + dz, gy=j_down, gz=k_to[dz]))

        def start(self):
            n, block, ref, base, h = self.n, self.block, self.ref, self.base, self.h
            for i in range(h):
                ys[n, 0, i] = ref[pl.ds((base + 4) * 16 + block - h + i, 64, stride=16), :]
                ys[n, 1, i] = ref[pl.ds((base + 4) * 16 + i, 64, stride=16), :]
                zs[n, 0, pl.ds(i * 8, 8), :] = ref[pl.ds((base + 68 - h + i) * 16, 8), :]
                zs[n, 1, pl.ds(i * 8, 8), :] = ref[pl.ds((base + 4 + i) * 16, 8), :]

            @pl.when(j < 7)
            def _():
                for copy in self.up:
                    copy.start()

            @pl.when(j > 0)
            def _():
                for copy in self.down:
                    copy.start()

            for copy in self.flat:
                copy.start()

        def finish(self):
            n, block, ref, base, h = self.n, self.block, self.ref, self.base, self.h

            @pl.when(j > 0)
            def _():
                for copy in self.up:
                    copy.wait_recv()
                for i in range(h):
                    ref[pl.ds((base + 4) * 16 + 16 - h + i, 64, stride=16), :] = yr[n, 0, i]

            @pl.when(j < 7)
            def _():
                for copy in self.down:
                    copy.wait_recv()
                for i in range(h):
                    ref[pl.ds((base + 4) * 16 + block + i, 64, stride=16), :] = yr[n, 1, i]

            for copy in self.flat:
                copy.wait_recv()
            for dz in range(2):
                here, low, high = (zr[n, dz, m, pl.ds(0, h * 8), :].reshape(h, 8, 128) for m in range(3))
                if block == 8:
                    pair = [here, jnp.where(sub < 4, high, low)]
                else:
                    pair = [jnp.where(sub < 4, here, roll(high, 4, 1)), roll(low, 4, 1)]
                v = jnp.concatenate(pair, axis=1)
                if block == 8:
                    if dz == 0:
                        v = roll(jnp.where(lane16 < 64, slots(ref, base + 68 - h, h), v), 64, 2)
                    else:
                        v = roll(jnp.where(lane16 < 64, v, slots(ref, base + 4, h)), 64, 2)
                put(ref, base + (4 - h if dz == 0 else 68), v)

            @pl.when(j < 7)
            def _():
                for copy in self.up:
                    copy.wait_send()

            @pl.when(j > 0)
            def _():
                for copy in self.down:
                    copy.wait_send()

            for copy in self.flat:
                copy.wait_send()

    half_lane = lax.broadcasted_iota(jnp.int32, (64, 128), 1) < 64

    def to_tiles(src, dst, base):
        for y in range(0, 8, 2):
            rows = [src[pl.ds(y + d, 64, stride=8), :] for d in range(2)]
            turned = jnp.concatenate(rows, axis=0).T
            low, high = turned[:64], turned[64:]
            first = (base + 4) * 16 + y
            dst[pl.ds(first, 64, stride=16), :] = jnp.where(half_lane, low, pltpu.roll(high, 64, 1))
            dst[pl.ds(first + 1, 64, stride=16), :] = jnp.where(half_lane, pltpu.roll(low, 64, 1), high)

    fext_rows, aext_rows = fext.reshape(512, 128), aext.reshape(512, 128)

    def x_gather(xg, n):
        other = b + 1 - 2 * lax.rem(b, 2)
        first = remote(xg.at[b], xg.at[b], xg_send.at[n, 0], xg_recv.at[n, 0], gx=other)
        early = [remote(xg.at[b], xg.at[b], xg_send.at[n, t], xg_recv.at[n, t], gx=lax.rem(b + 2 * t, 8))
                 for t in range(1, 4)]
        second = [remote(xg.at[other], xg.at[other], xg_send.at[n, 3 + t], xg_recv.at[n, 3 + t],
                         gx=lax.rem(b + 2 * t, 8)) for t in range(1, 4)]
        for copy in [first] + early:
            copy.start()
        return first, early, second

    def x_pack(weight, xg, faces=False):
        source = lax.broadcasted_iota(jnp.int32, (128, 256), 0)
        target = lax.broadcasted_iota(jnp.int32, (128, 256), 1)
        slot, inner = source % 16, (target % 128) % 32
        hit = (source // 64 == target // 128) & ((source % 64) // 16 == (target % 128) // 32) & (inner < 4)
        pair = (slot // 2 == inner + 2) & hit
        if faces:
            pair = pair & (((source % 64) // 16 != 0) | (slot % 2 == 1))
        matrix = jnp.where(pair, weight, 0.0).astype(F32)
        moved = jnp.dot(tb[...], matrix, precision=HIGHEST, preferred_element_type=F32)
        parts = [moved[:, :128].reshape(32, 8, 128), moved[:, 128:].reshape(32, 8, 128)]
        total = None
        for g in range(8):
            part = roll(parts[g // 4][(g % 4) * 8:(g % 4) * 8 + 8], 4 * g, 2)
            total = part if total is None else total + part
        packed = jnp.where(sub % 2 == 0, total[:4], total[4:])
        xg[b] = packed.reshape(32, 128)

    def x_unpack(xg, dst, base):
        g = (lane // 4) % 8
        for q in range(4):
            for odd in range(2):
                v = []
                for n in range(8):
                    tile = xg[n, pl.ds(q * 8, 8), :].reshape(1, 8, 128)
                    v.append(jnp.where(sub % 2 == 1, tile, roll(tile, -1, 1)) if odd
                             else jnp.where(sub % 2 == 0, tile, roll(tile, 1, 1)))
                for s in (1, 2, 4):
                    high = (g // s) % 2 == 1
                    for n in range(8):
                        if n & s == 0:
                            lo, hi = v[n], v[n + s]
                            v[n] = jnp.where(high, roll(hi, 4 * s, 2), lo)
                            v[n + s] = jnp.where(high, hi, roll(lo, -4 * s, 2))
                for n in range(8):
                    put(tmp, n * 8 + 4 * odd + q, v[n])
        for i in range(4):
            dst[pl.ds((base + 4) * 16 + i, 64, stride=16), :] = tmp[pl.ds(2 * i, 64, stride=8), :]

    own_a.wait()
    for copy in strips[:4]:
        copy.wait_recv()
    to_tiles(aext_rows, l0.wa, 1)
    edges = Wide(0, 8, l0.wa, 1, 4)
    edges.start()
    edges.finish()
    group0 = (lane16 // 16) % 4
    row16 = iota(1, (1, 16, 128))
    x_at = 8 * b + lane16 % 16 - 4
    y_at = 8 * j + jnp.where(row16 < 12, row16, row16 - 16)

    def face_body(i):
        a, xd, xu, yd, yu, zd, zu = neighbours(l0, l0.wa, i)
        z_at = 128 * k + 64 * (iota(2, a.shape) // 64) + i * l0.ch - 4 + iota(0, a.shape)
        side_up = jnp.where(group0 == 0, xu, jnp.where(group0 == 1, yu, zu))
        side_low = jnp.where(group0 == 0, xd, jnp.where(group0 == 1, yd, zd))
        where = jnp.where(group0 == 0, x_at, jnp.where(group0 == 1, y_at, z_at))
        end = jnp.where(group0 == 0, nx - 1, jnp.where(group0 == 1, ny - 1, nz - 1))
        l0.put(l0.up, i, jnp.where(where == end, 0.0, 0.5 * (a + side_up)))
        l0.put(l0.low, i, jnp.where(where == 0, 0.0, 0.5 * (a + side_low)))

    l0.loop(face_body)

    own_f.wait()
    for copy in strips[4:]:
        copy.wait_recv()
    to_tiles(fext_rows, l0.f, 0)
    edges = Wide(1, 8, l0.f, 0, 3)
    edges.start()

    def body(i):
        put(tb, i * 16, coarse_faces(*own_pairs(l0.up, i), 16, 1, None))

    loop(2, body)
    x_pack(0.25, xgf, True)
    faces_first, faces_early, faces_second = x_gather(xgf, 1)
    make_coefs(l0, 16)

    edges.finish()

    over_theta, ((a1, b1), (a2, b2)) = SMOOTH

    def downward(lv):
        init_down(lv, over_theta)
        step(lv, lv.wa, lv.wb, a1, b1, add="w")
        step(lv, lv.wb, lv.wa, a2, b2, add="x")
        if lv in (l0, l1):
            own_step(lv, lv.wa)
        else:
            step(lv, lv.wa, None)

    def upward(lv, coarse_at):
        init_up(lv, coarse_at)
        step(lv, lv.wa, lv.wb, None, over_theta, add="xw")
        step(lv, lv.wb, lv.wa, a1, b1)
        if lv in (l0, l1):
            own_step(lv, lv.wa, a2, b2)
        else:
            step(lv, lv.wa, None, a2, b2, add="xw", last=True)

    def own_sums(lv, i):
        pairs, roots = own_pairs(lv.r, i), own_pairs(lv.root, i)
        return pairs[0] * roots[0] + pairs[1] * roots[1]

    downward(l0)

    def body(i):
        put(tb, i * 16, both(own_sums(l0, i), 1, 1))

    loop(2, body)
    x_pack(0.125, xg1)
    right_first, right_early, right_second = x_gather(xg1, 0)
    faces_first.wait_recv()
    for copy in faces_second:
        copy.start()

    slot = lane % 16
    for side, first in ((0, 10), (1, 4)):
        packed = jnp.zeros((8, 8, 128), F32)
        for g in range(8):
            v = slots(l0.r, 4 + 8 * g, 8)[:, :8]
            packed = jnp.where(slot // 2 == g, roll(v, 2 * g - first, 2), packed)
        rxs[side] = packed.reshape(64, 128)
    rx = [remote(rxs.at[0], rxr.at[0], rx_send.at[0], rx_recv.at[0], gx=b_up),
          remote(rxs.at[1], rxr.at[1], rx_send.at[1], rx_recv.at[1], gx=b_down)]

    for copy in faces_early + faces_second:
        copy.wait_recv()
    x_unpack(xgf, l1.up, 1)
    edges = Wide(2, 4, l1.up, 1, 4)
    edges.start()

    c = b // 2

    def second_pack(q):
        start = pl.multiple_of(c * 64, 64)
        q[...] = jnp.where(lane2 % 2 == 0, tb[pl.ds(start, 8, stride=8), :], tb[pl.ds(start + 2, 8, stride=8), :])

    class Second:
        def __init__(self, q, yg, zh, n):
            yg[c, j] = q[...]
            self.along = [remote(q, yg.at[c, j], yg_send.at[n, t], yg_recv.at[n, t], gy=lax.rem(j + t, 8))
                          for t in range(1, 8)]
            self.quarters = [remote(yg.at[c], yg.at[c], yc_send.at[n, t], yc_recv.at[n, t], gx=lax.rem(b + 2 * t, 8))
                             for t in range(1, 4)]
            self.above = [remote(yg.at[3], zh.at[0], h_send.at[n, 0, t], h_recv.at[n, 0],
                                 gx=lax.rem(b + 2 * t, 8), gz=lax.rem(k + 1, 8)) for t in range(4)]
            self.below = [remote(yg.at[0], zh.at[1], h_send.at[n, 1, t], h_recv.at[n, 1],
                                 gx=lax.rem(b + 2 * t, 8), gz=lax.rem(k + 7, 8)) for t in range(4)]
            self.yg, self.zh = yg, zh
            for copy in self.along:
                copy.start()

        def spread(self):
            for copy in self.along:
                copy.wait_recv()
            for copy in self.quarters:
                copy.start()

            @pl.when(c == 3)
            def _():
                for copy in self.above:
                    copy.start()

            @pl.when(c == 0)
            def _():
                for copy in self.below:
                    copy.start()

        def finish(self, dst, base):
            for copy in self.quarters + [self.above[0], self.below[0]]:
                copy.wait_recv()
            yg, zh = self.yg, self.zh
            for n in range(8):
                v = jnp.concatenate([zh[0, n]] + [yg[m, n] for m in range(4)] + [zh[1, n]], axis=0)
                low, high = v[:24], v[24:]
                dst[pl.ds(base * 16 + 2 * n, 24, stride=16), :] = jnp.where(lane2 % 2 == 0, low, roll(high, 1, 1))
                dst[pl.ds(base * 16 + 2 * n + 1, 24, stride=16), :] = jnp.where(lane2 % 2 == 0, roll(low, -1, 1), high)

        def wait_send(self):
            for copy in self.along + self.quarters:
                copy.wait_send()

            @pl.when(c == 3)
            def _():
                for copy in self.above:
                    copy.wait_send()

            @pl.when(c == 0)
            def _():
                for copy in self.below:
                    copy.wait_send()

    def body(i):
        put(tb, i * 16, 0.25 * coarse_faces(*own_pairs(l1.up, i, 1), 32, 1, 1))

    loop(2, body)
    second_pack(qf)
    faces_second_level = Second(qf, ygf, zhf, 0)
    edges.finish()
    right_first.wait_recv()
    for copy in right_second:
        copy.start()
    make_coefs(l1, 32)

    for copy in right_early + right_second:
        copy.wait_recv()
    x_unpack(xg1, l1.f, 0)
    edges = Wide(3, 4, l1.f, 0, 3)
    edges.start()
    edges.finish()
    faces_second_level.spread()
    downward(l1)

    def body(i):
        put(tb, i * 16, 0.125 * both(both(own_sums(l1, i), 1, 1), 1, 2))

    loop(2, body)
    second_pack(q1)
    right_second_level = Second(q1, yg1, zh1, 1)
    faces_second_level.finish(l2.up, 1)

    t = lane % 4

    def third(ref, faces=False):
        g, odd_lane = lane // 32, lane % 2 == 1

        def rows(values, d):
            return values[pl.ds((16 if faces else 0) + d, 192, stride=2), :].reshape(24, 8, 128)

        if faces:
            v = jnp.where(g == 1, rows(ref, 1), rows(ref, 0) + rows(ref, 1))
        else:
            v = rows(ref, 0) * rows(l2.root, 0) + rows(ref, 1) * rows(l2.root, 1)
        halves = []
        for part in (v[8:], v[:16]):
            part = part.reshape(8, 2, 8, 128)
            both_z = part[:, 0] + part[:, 1]
            halves.append(jnp.where(g == 2, part[:, 1], both_z) if faces else both_z)
        v = jnp.concatenate([jnp.where(odd_lane, roll(halves[0], 1, 2), halves[0]),
                             jnp.where(odd_lane, halves[1], roll(halves[1], -1, 2))], axis=0)
        if faces:
            v = 0.25 * jnp.where(g == 0, pick(v, 2, 2), both(v, 2, 2))
        else:
            v = 0.125 * both(v, 2, 2)
        v = v.reshape(4, 4, 8, 128)
        out = v[:, 0]
        for u in range(1, 4):
            out = jnp.where(t == u, v[:, u], out)
        return out

    def z_gather(g, n, base):
        rows = pl.ds(pl.multiple_of((4 * k + base) * 8, 8), 32)
        return [remote(g.at[rows], g.at[rows], zg_send.at[n, u], zg_recv.at[n, u], gz=lax.rem(k + u, 8))
                for u in range(1, 8)]

    put(l3.up, 4 * k + 1, third(l2.up, True))
    third_faces = z_gather(l3.up, 0, 1)

    for copy in third_faces:
        copy.start()
    make_coefs(l2, 32)
    right_second_level.spread()
    for copy in rx:
        copy.start()
    for copy in third_faces:
        copy.wait_recv()
    make_coefs(l3, 32)

    group = lane // 32
    v = slots(l3.up, 1, 32, 8)
    v = jnp.where(group == 2, pick(v, 1, 2), both(v, 1, 2))
    v = jnp.where(group == 1, pick(v, 1, 1), both(v, 1, 1))
    fourth_coefs(l4, 0.25 * compact(jnp.where(group == 0, pick(v, 4, 2), both(v, 4, 2))))
    right_second_level.finish(l2.f, 0)
    edges1 = Wide(4, 4, l1.r, 0, 2)
    edges1.start()
    downward(l2)
    put(l3.f, 4 * k, third(l2.r))
    third_right = z_gather(l3.f, 1, 0)
    for copy in third_right:
        copy.start()

    edges1.finish()
    for copy in third_right:
        copy.wait_recv()

    downward(l3)

    v = slots(l3.r, 0, 32, 8) * slots(l3.root, 0, 32, 8)
    expand(l4.x, fourth_solve(l4, 0.125 * compact(both(both(both(v, 1, 2), 1, 1), 4, 2))))
    upward(l3, lambda i: l4.get(l4.x, i))

    for q in range(6):
        v = l3.x[pl.ds(pl.multiple_of(lax.rem(4 * k + q + 31, 32) * 8, 8), 8), :].reshape(1, 8, 128)
        for z in range(4):
            moved = v
            for u in range(4):
                if u != z:
                    moved = jnp.where(t == u, roll(v, u - z, 2), moved)
            first = (4 * q + z) * 16
            eb2[pl.ds(first, 8, stride=2), :] = moved.reshape(8, 128)
            eb2[pl.ds(first + 1, 8, stride=2), :] = moved.reshape(8, 128)

    def twice(ref, offset):
        def chunk(i):
            v = slots(ref, i * 4 + offset, 4)
            return jnp.broadcast_to(v[:, None], (4, 2, 16, 128)).reshape(8, 16, 128)

        return chunk

    def second_chunk(i):
        v = jnp.where(lane16 % 2 == 0, slots(eb2, i * 4, 4), slots(eb2, i * 4 + 12, 4))
        return jnp.broadcast_to(v[:, None], (4, 2, 16, 128)).reshape(8, 16, 128)

    upward(l2, second_chunk)

    for copy in rx:
        copy.wait_recv()
    for g in range(8):
        v = slots(l0.r, 4 + 8 * g, 8)
        own = v[:, :8]
        own = jnp.where(slot // 2 == 1, roll(rxr[0].reshape(8, 8, 128), 2 - 2 * g, 2), own)
        own = jnp.where(slot // 2 == 6, roll(rxr[1].reshape(8, 8, 128), 12 - 2 * g, 2), own)
        put(l0.r, 4 + 8 * g, jnp.concatenate([own, v[:, 8:]], axis=1))
    edges0 = Wide(5, 8, l0.r, 0, 2)
    edges0.start()

    for i, from_y in ((0, 0), (1, 1), (2, 2), (3, 3), (6, 14), (7, 15)):
        v = l2.x[pl.ds(lax.rem(2 * j + from_y, 16), 24, stride=16), :]
        low, high = jnp.where(lane2 % 2 == 0, v, roll(v, 1, 1)), jnp.where(lane2 % 2 == 1, v, roll(v, -1, 1))
        for d in range(2):
            eb1[pl.ds(2 * i + d, 24, stride=16), :] = low
            eb1[pl.ds(2 * i + d + 384, 24, stride=16), :] = high
    upward(l1, twice(eb1, 6))
    edges = Wide(6, 4, l1.x, 0, 2)
    edges.start()
    edges0.finish()
    edges.finish()

    source = lax.broadcasted_iota(jnp.int32, (128, 128), 0)
    target = lax.broadcasted_iota(jnp.int32, (128, 128), 1)
    hit = (source // 32 == (target % 64) // 16) & (source % 32 == 4 * b - 2 + (target % 16) // 2)
    v = slots(l1.x, 0, 72)
    v = jnp.where(sub < 6, v[:, :8], v[:, 8:]).reshape(576, 128)
    v = jnp.dot(v, jnp.where(hit, 1.0, 0.0).astype(F32), precision=HIGHEST, preferred_element_type=F32)
    eb0[pl.ds(0, 576, stride=2), :] = v
    eb0[pl.ds(1, 576, stride=2), :] = v

    def top_chunk(i):
        v = jnp.where(lane16 < 64, slots(eb0, i * 4 + 2, 4), slots(eb0, i * 4 + 34, 4))
        return jnp.broadcast_to(v[:, None], (4, 2, 16, 128)).reshape(8, 16, 128)

    upward(l0, top_chunk)

    for y in range(0, 8, 2):
        first = l0.x[pl.ds(64 + y, 64, stride=16), :]
        second = l0.x[pl.ds(65 + y, 64, stride=16), :]
        low = jnp.where(half_lane, first, pltpu.roll(second, 64, 1))
        high = jnp.where(half_lane, pltpu.roll(first, 64, 1), second)
        turned = pltpu.roll(jnp.concatenate([low, high], axis=0), 124, 1).T
        for d in range(2):
            for v in range(4):
                start = d * 64 + v * 16
                out_ref[pl.ds(v * 64 + y + d, 8, stride=8), :] = turned[start:start + 8]

    for copy in (strips[4:] + [faces_first, right_first] + faces_early + right_early + faces_second + right_second + rx
                 + third_faces + third_right):
        copy.wait_send()
    faces_second_level.wait_send()
    right_second_level.wait_send()


def solution(mesh):
    def per_device(right_side, affinity):
        nx = affinity.shape[1] * mesh.shape["gx"]
        ny = affinity.shape[2] * mesh.shape["gy"]
        nz = affinity.shape[3] * mesh.shape["gz"]
        scratch = []
        for z, rows, *_ in LEVELS:
            scratch += level_shapes(z, rows)
        scratch += [pltpu.VMEM(shape, F32) for shape in (
            (4, 16, 8, 128), (4, 16, 8, 128),
            (7, 2, 4, 64, 128), (7, 2, 4, 64, 128), (7, 2, 32, 128), (7, 2, 3, 32, 128),
            (256, 128), (512, 128), (8, 32, 128), (8, 32, 128), (2, 64, 128), (2, 64, 128),
            (8, 128), (8, 128), (4, 8, 8, 128), (4, 8, 8, 128), (2, 8, 8, 128), (2, 8, 8, 128), (384, 128), (768, 128), (1152, 128))]
        dma = pltpu.SemaphoreType.DMA
        scratch += [dma(shape) for shape in (
            (2,), (6,), (6,), (7, 8), (7, 8), (2, 7), (2, 7), (2,), (2,), (2, 2, 4), (2, 2), (2, 8), (2, 8), (2, 4), (2, 4), (2, 8), (2, 8))]
        out = pl.pallas_call(
            functools.partial(kernel, nx, ny, nz),
            out_shape=jax.ShapeDtypeStruct((256, 128), F32),
            in_specs=[pl.BlockSpec(memory_space=pl.ANY)] * 2,
            out_specs=pl.BlockSpec(memory_space=pltpu.VMEM),
            scratch_shapes=scratch,
            compiler_params=pltpu.CompilerParams(
                collective_id=0, has_side_effects=True, vmem_limit_bytes=60 * 1024 * 1024),
        )(right_side, affinity)
        return out.reshape(right_side.shape)

    spec = P(None, "gx", "gy", "gz")
    return jax.shard_map(per_device, mesh=mesh, in_specs=(spec, spec), out_specs=spec, check_vma=False)
```

```python
import functools

import jax
import jax.numpy as jnp
from jax import lax
from jax.experimental import pallas as pl
from jax.experimental.pallas import tpu as pltpu
from jax.sharding import PartitionSpec as P

MESH = pl.DeviceIdType.MESH
HIGHEST = lax.Precision.HIGHEST
F32 = jnp.float32

DEGREE = 3
COARSE_DEGREE = 8
SHIFT = 0.02
SMOOTH_LOWER = 0.5
UPPER = 2.0 + SHIFT


def cheb_coefs(a, b, m):
    theta, delta = 0.5 * (b + a), 0.5 * (b - a)
    sigma = theta / delta
    rho = 1.0 / sigma
    steps = []
    for _ in range(m - 1):
        nxt = 1.0 / (2.0 * sigma - rho)
        steps.append((nxt * rho, 2.0 * nxt / delta))
        rho = nxt
    return 1.0 / theta, steps


SMOOTH = cheb_coefs(SMOOTH_LOWER, UPPER, DEGREE)
SOLVE = cheb_coefs(SHIFT, UPPER, COARSE_DEGREE)


def iota(dim, shape=(1, 8, 128)):
    return lax.broadcasted_iota(jnp.int32, shape, dim)


def roll(x, shift, axis):
    shift = shift % x.shape[axis]
    return x if shift == 0 else pltpu.roll(x, shift, axis)


def both(x, k, axis):
    bit = (iota(axis, (1,) + x.shape[1:]) // k) % 2
    return x + jnp.where(bit == 0, roll(x, -k, axis), roll(x, k, axis))


def pick(x, k, axis):
    bit = (iota(axis, (1,) + x.shape[1:]) // k) % 2
    return jnp.where(bit == 1, x, roll(x, -k, axis))


def slots(ref, start, count, rows=16):
    if not isinstance(start, int):
        start = pl.multiple_of(start * rows, rows)
    else:
        start = start * rows
    return ref[pl.ds(start, count * rows), :].reshape(count, rows, 128)


def put(ref, start, value):
    count, rows = value.shape[:2]
    if not isinstance(start, int):
        start = pl.multiple_of(start * rows, rows)
    else:
        start = start * rows
    ref[pl.ds(start, count * rows), :] = value.reshape(count * rows, 128)


def loop(count, body):
    def run(i, carry):
        body(i)
        return carry

    lax.fori_loop(0, count, run, 0)


class Level:
    def __init__(self, z, rows, sy, sx, mode, refs):
        self.z, self.rows, self.sy, self.sx, self.mode = z, rows, sy, sx, mode
        self.ch = 128 // rows
        self.parts = z // self.ch if rows == 8 else 3
        (self.coef, self.scale, self.root, self.f, self.r, self.x, self.wa, self.wb, self.up, self.low,
         self.r_next, self.x_next) = refs

    def loop(self, body):
        def turn(i, carry):
            for part in range(self.parts):
                body(i * self.parts + part)
            return carry

        turns = self.z // (self.ch * self.parts)
        if turns == 1:
            turn(0, 0)
        else:
            lax.fori_loop(0, turns, turn, 0)

    def get(self, ref, i, offset=0):
        return slots(ref, i * self.ch + offset, self.ch, self.rows)

    def put(self, ref, i, value, offset=0):
        put(ref, i * self.ch + offset, value)


LEVELS = ((72, 16, 1, 1, 0), (72, 16, 1, 1, 0), (24, 16, 1, 2, 0), (32, 8, 1, 4, 1), (32, 8, 2, 8, 2))


def level_shapes(z, rows):
    n = z * rows
    pad = (z + 2) * rows
    return [pltpu.VMEM((6 * n, 128), F32)] + [pltpu.VMEM((n, 128), F32)] * 5 + [pltpu.VMEM((pad, 128), F32)] * 4 + [
        pltpu.VMEM((n, 128), F32)] * 2


def join_halves(ref):
    odd = iota(2, (1, 16, 128)) % 2 == 1
    put(ref, 0, jnp.where(odd, roll(slots(ref, 24, 1), 1, 2), 0.0))
    put(ref, 25, jnp.where(odd, 0.0, roll(slots(ref, 1, 1), -1, 2)))


def neighbours(lv, w_ref, i):
    w, before, after = lv.get(w_ref, i, 1), lv.get(w_ref, i, 0), lv.get(w_ref, i, 2)
    xd, xu = roll(w, lv.sx, 2), roll(w, -lv.sx, 2)
    yd, yu = roll(w, lv.sy, 1), roll(w, -lv.sy, 1)
    if lv.mode == 0:
        zd, zu = before, after
    else:
        s = lv.mode
        t = iota(2) % 4
        zu = jnp.where(t < 4 - s, roll(w, -s, 2), roll(after, 4 - s, 2))
        zd = jnp.where(t >= s, roll(w, s, 2), roll(before, s - 4, 2))
    return w, xd, xu, yd, yu, zd, zu


def init_down(lv, over_theta):
    def body(i):
        r = lv.get(lv.scale, i) * lv.get(lv.f, i)
        lv.put(lv.r, i, r)
        lv.put(lv.wa, i, r * over_theta, 1)

    lv.loop(body)


def init_up(lv, coarse_at):
    def body(i):
        lv.put(lv.wa, i, lv.get(lv.scale, i) * coarse_at(i), 1)

    lv.loop(body)


def step(lv, w_ref, w_next, alpha=None, beta=None, add="", last=False):
    if lv.z == 24:
        join_halves(w_ref)

    def body(i):
        w, *near = neighbours(lv, w_ref, i)
        total = None
        for k, value in enumerate(near):
            term = slots(lv.coef, k * lv.z + i * lv.ch, lv.ch, lv.rows) * value
            total = term if total is None else total + term
        r = lv.get(lv.r, i) - ((1.0 + SHIFT) * w - total)
        if not last:
            lv.put(lv.r_next, i, r)
        if beta is None:
            return
        new = beta * r if alpha is None else alpha * w + beta * r
        if add:
            x = new + w if "w" in add else new
            if "x" in add:
                x = x + lv.get(lv.x, i)
            lv.put(lv.x_next, i, x * lv.get(lv.root, i) if last else x)
        if not last:
            lv.put(w_next, i, new, 1)

    lv.loop(body)
    if not last:
        lv.r, lv.r_next = lv.r_next, lv.r
    if add:
        lv.x, lv.x_next = lv.x_next, lv.x


def make_coefs(lv, group):
    g = (iota(2, (1, lv.rows, 128)) // group) % 4

    def spread(value, k):
        out = value
        for to in range(4):
            if to != k:
                out = jnp.where(g == to, roll(value, group * (to - k), 2), out)
        return out

    if lv.z == 24:
        join_halves(lv.up)

    def body(i):
        if group == 16:
            up = lv.get(lv.up, i)
            lows = [lv.get(lv.low, i)] * 3
        else:
            up, x_low, _, y_low, _, z_low, _ = neighbours(lv, lv.up, i)
            lows = [jnp.where(iota(2, (1, lv.rows, 128)) % 32 < lv.sx, 0.0, x_low), y_low, z_low]
        faces = []
        for k in range(3):
            faces += [spread(lows[k], k), spread(up, k)]
        total = faces[0] + faces[1] + faces[2] + faces[3] + faces[4] + faces[5]
        scale = jnp.where(total > 0.0, lax.rsqrt(total), 0.0)
        lv.put(lv.scale, i, scale)
        lv.put(lv.root, i, scale * total)
        square = scale * scale
        for k in range(6):
            put(lv.coef, k * lv.z + i * lv.ch, square * faces[k])

    lv.loop(body)


def own_pairs(ref, i, base=0):
    v = slots(ref, base + 4 + 32 * i, 32)[:, :8].reshape(16, 2, 8, 128)
    return v[:, 0], v[:, 1]


def coarse_faces(first, second, group, ky, kx):
    g = (iota(2) // group) % 4
    v = jnp.where(g == 2, second, first + second)
    v = jnp.where(g == 1, pick(v, ky, 1), both(v, ky, 1))
    if kx is not None:
        v = jnp.where(g == 0, pick(v, kx, 2), both(v, kx, 2))
    return v


def own_step(lv, w_ref, alpha=None, beta=None):
    def body(i):
        first = 4 + 8 * i
        here = slots(w_ref, first + 1, 8)
        w = here[:, :8]
        near = [roll(w, 1, 2), roll(w, -1, 2), roll(here, 1, 1)[:, :8], roll(here, -1, 1)[:, :8],
                slots(w_ref, first, 8)[:, :8], slots(w_ref, first + 2, 8)[:, :8]]
        total = None
        for k, value in enumerate(near):
            term = slots(lv.coef, k * lv.z + first, 8)[:, :8] * value
            total = term if total is None else total + term
        r = slots(lv.r, first, 8)[:, :8] - ((1.0 + SHIFT) * w - total)
        if beta is not None:
            x = slots(lv.x, first, 8)[:, :8] + w + (alpha * w + beta * r)
            r = x * slots(lv.root, first, 8)[:, :8]
        target = lv.r_next if beta is None else lv.x_next
        for n in range(8):
            target[pl.ds(pl.multiple_of((first + n) * 16, 16), 8), :] = r[n]

    def turn(i, carry):
        for part in range(4):
            body(4 * i + part)
        return carry

    lax.fori_loop(0, 2, turn, 0)
    if beta is None:
        lv.r, lv.r_next = lv.r_next, lv.r
    else:
        lv.x, lv.x_next = lv.x_next, lv.x


def compact(v):
    v = v.reshape(8, 4, 8, 128)
    v = [v[n] for n in range(8)]
    for bit in (iota(2) % 2, (iota(2) // 4) % 2, iota(1) % 2):
        v = [jnp.where(bit == 0, v[n], v[n + 1]) for n in range(0, len(v), 2)]
    return v[0]


def expand(ref, v):
    out = [v]
    for k, axis in ((1, 1), (4, 2), (1, 2)):
        bit = (iota(axis) // k) % 2
        out = [jnp.where(bit == m, w, roll(w, k if m == 0 else -k, axis)) for w in out for m in range(2)]
    for n in range(8):
        put(ref, 4 * n, out[n])


def fourth_neighbours(w):
    low0, low2, t = iota(2) % 2, (iota(2) // 4) % 2, (iota(2) // 2) % 2
    last, first = w[3:], w[:1]
    up = jnp.where(low0 == 0, roll(first, -1, 2),
                   jnp.where(low2 == 0, roll(first, -3, 2), roll(roll(first, 5, 2), -1, 1)))
    down = jnp.where(low0 == 1, roll(last, 1, 2),
                     jnp.where(low2 == 1, roll(last, 3, 2), roll(roll(last, -5, 2), 1, 1)))
    after, before = jnp.concatenate([w[1:], up], axis=0), jnp.concatenate([down, w[:3]], axis=0)
    return [roll(w, 8, 2), roll(w, -8, 2), roll(w, 2, 1), roll(w, -2, 1),
            jnp.where(t == 1, roll(w, 2, 2), roll(before, -2, 2)),
            jnp.where(t == 0, roll(w, -2, 2), roll(after, 2, 2))]


def fourth_coefs(lv, up):
    x_low, _, y_low, _, z_low, _ = fourth_neighbours(up)
    lows = [jnp.where(iota(2) % 32 < 8, 0.0, x_low), y_low, z_low]
    g = iota(2) // 32
    faces = []
    for k in range(3):
        for value in (lows[k], up):
            out = value
            for to in range(4):
                if to != k:
                    out = jnp.where(g == to, roll(value, 32 * (to - k), 2), out)
            faces.append(out)
    total = faces[0] + faces[1] + faces[2] + faces[3] + faces[4] + faces[5]
    scale = lax.rsqrt(total)
    put(lv.scale, 0, scale)
    put(lv.root, 0, scale * total)
    for k in range(6):
        put(lv.coef, 4 * k, scale * scale * faces[k])


def fourth_solve(lv, f):
    over_theta, steps = SOLVE
    coefs = [slots(lv.coef, 4 * k, 4, 8) for k in range(6)]
    r = slots(lv.scale, 0, 4, 8) * f
    w = x = r * over_theta
    for alpha, beta in steps:
        total = None
        for coef, value in zip(coefs, fourth_neighbours(w)):
            total = coef * value if total is None else total + coef * value
        r = r - ((1.0 + SHIFT) * w - total)
        w = alpha * w + beta * r
        x = x + w
    return x * slots(lv.root, 0, 4, 8)


def kernel(nx, ny, nz, f_hbm, a_hbm, out_ref, *scratch):
    refs = list(scratch)

    def take(count):
        got = refs[:count]
        del refs[:count]
        return got

    levels = [Level(*shape, take(12)) for shape in LEVELS]
    (fext, aext, ys, yr, zs, zr, tb, tmp, xg1, xgf, rxs, rxr, q1, qf, yg1, ygf, zh1, zhf, eb2, eb1, eb0) = take(21)
    (local_sem, strip_send, strip_recv, ex_send, ex_recv, xg_send, xg_recv, rx_send, rx_recv,
     h_send, h_recv, yg_send, yg_recv, yc_send, yc_recv, zg_send, zg_recv) = take(17)
    l0, l1, l2, l3, l4 = levels

    b, j, k = lax.axis_index("gx"), lax.axis_index("gy"), lax.axis_index("gz")
    sub, lane, lane16 = iota(1), iota(2), iota(2, (1, 16, 128))
    lane2 = lax.broadcasted_iota(jnp.int32, (1, 128), 1)

    def remote(src, dst, send, recv, **to):
        return pltpu.make_async_remote_copy(
            src_ref=src, dst_ref=dst, send_sem=send, recv_sem=recv, device_id=to, device_id_type=MESH)

    own_f = pltpu.make_async_copy(f_hbm, fext.at[:, pl.ds(4, 8)], local_sem.at[0])
    own_a = pltpu.make_async_copy(a_hbm, aext.at[pl.ds(0, 3), pl.ds(4, 8)], local_sem.at[1])
    own_a.start()
    own_f.start()
    zr[...] = jnp.zeros_like(zr)

    barrier = pltpu.get_barrier_semaphore()
    partners = [{"gx": lax.rem(b + t, 8)} for t in (1, 2, 4, 6, 7)]
    partners += [{"gy": lax.rem(j + t, 8)} for t in range(1, 8)]
    partners += [{"gz": lax.rem(k + t, 8)} for t in range(1, 8)]
    partners += [{"gy": lax.rem(j + t, 8), "gz": lax.rem(k + u, 8)} for t in (1, 7) for u in (1, 7)]
    partners += [{"gx": lax.rem(b + t, 8), "gz": lax.rem(k + u, 8)} for t in (2, 4, 6) for u in (1, 7)]
    for to in partners:
        pl.semaphore_signal(barrier, inc=1, device_id=to, device_id_type=MESH)

    fext[:, 0] = jnp.zeros((4, 8, 128), F32)
    fext[:, 15] = jnp.zeros((4, 8, 128), F32)
    aext[3] = jnp.zeros((16, 8, 128), F32)
    for n in (1, 2):
        aext[n, 0] = jnp.zeros((8, 128), F32)
        aext[n, 15] = jnp.zeros((8, 128), F32)
    for ref in (l0.f, l0.wa, l1.f, l1.up, eb1):
        ref[...] = jnp.zeros_like(ref)
    for lv in levels:
        for w in (lv.wa, lv.wb, lv.up):
            w[pl.ds(0, lv.rows), :] = jnp.zeros((lv.rows, 128), F32)
            w[pl.ds((lv.z + 1) * lv.rows, lv.rows), :] = jnp.zeros((lv.rows, 128), F32)
    pl.semaphore_wait(barrier, len(partners))

    b_up, b_down = lax.rem(b + 1, 8), lax.rem(b + 7, 8)
    strips = [
        remote(a_hbm.at[:, pl.ds(5, 3)], aext.at[pl.ds(0, 3), pl.ds(1, 3)],
               strip_send.at[0], strip_recv.at[0], gx=b_up),
        remote(a_hbm.at[:, pl.ds(0, 3)], aext.at[pl.ds(0, 3), pl.ds(12, 3)],
               strip_send.at[1], strip_recv.at[1], gx=b_down),
        remote(a_hbm.at[0, 4], aext.at[0, 0], strip_send.at[4], strip_recv.at[4], gx=b_up),
        remote(a_hbm.at[0, 3], aext.at[0, 15], strip_send.at[5], strip_recv.at[5], gx=b_down),
        remote(f_hbm.at[:, pl.ds(5, 3)], fext.at[:, pl.ds(1, 3)],
               strip_send.at[2], strip_recv.at[2], gx=b_up),
        remote(f_hbm.at[:, pl.ds(0, 3)], fext.at[:, pl.ds(12, 3)],
               strip_send.at[3], strip_recv.at[3], gx=b_down),
    ]
    for copy in strips:
        copy.start()

    class Wide:
        def __init__(self, n, block, ref, base, h):
            self.n, self.block, self.ref, self.base, self.h = n, block, ref, base, h
            rows, part = pl.ds(0, h), pl.ds(0, h * 8)
            j_up, j_down = jnp.minimum(j + 1, 7), jnp.maximum(j - 1, 0)
            k_to = (lax.rem(k + 1, 8), lax.rem(k + 7, 8))

            def make(src, dst, index, **to):
                return remote(src, dst, ex_send.at[n, index], ex_recv.at[n, index], **to)

            self.up = [make(ys.at[n, 0, rows], yr.at[n, 0, rows], 0, gy=j_up)]
            self.down = [make(ys.at[n, 1, rows], yr.at[n, 1, rows], 1, gy=j_down)]
            self.flat = []
            for dz in range(2):
                self.flat.append(make(zs.at[n, dz, part], zr.at[n, dz, 0, part], 2 + dz, gz=k_to[dz]))
                self.up.append(make(zs.at[n, dz, part], zr.at[n, dz, 1, part], 4 + dz, gy=j_up, gz=k_to[dz]))
                self.down.append(make(zs.at[n, dz, part], zr.at[n, dz, 2, part], 6 + dz, gy=j_down, gz=k_to[dz]))

        def start(self):
            n, block, ref, base, h = self.n, self.block, self.ref, self.base, self.h
            for i in range(h):
                ys[n, 0, i] = ref[pl.ds((base + 4) * 16 + block - h + i, 64, stride=16), :]
                ys[n, 1, i] = ref[pl.ds((base + 4) * 16 + i, 64, stride=16), :]
                zs[n, 0, pl.ds(i * 8, 8), :] = ref[pl.ds((base + 68 - h + i) * 16, 8), :]
                zs[n, 1, pl.ds(i * 8, 8), :] = ref[pl.ds((base + 4 + i) * 16, 8), :]

            @pl.when(j < 7)
            def _():
                for copy in self.up:
                    copy.start()

            @pl.when(j > 0)
            def _():
                for copy in self.down:
                    copy.start()

            for copy in self.flat:
                copy.start()

        def finish(self):
            n, block, ref, base, h = self.n, self.block, self.ref, self.base, self.h

            @pl.when(j > 0)
            def _():
                for copy in self.up:
                    copy.wait_recv()
                for i in range(h):
                    ref[pl.ds((base + 4) * 16 + 16 - h + i, 64, stride=16), :] = yr[n, 0, i]

            @pl.when(j < 7)
            def _():
                for copy in self.down:
                    copy.wait_recv()
                for i in range(h):
                    ref[pl.ds((base + 4) * 16 + block + i, 64, stride=16), :] = yr[n, 1, i]

            for copy in self.flat:
                copy.wait_recv()
            for dz in range(2):
                here, low, high = (zr[n, dz, m, pl.ds(0, h * 8), :].reshape(h, 8, 128) for m in range(3))
                if block == 8:
                    pair = [here, jnp.where(sub < 4, high, low)]
                else:
                    pair = [jnp.where(sub < 4, here, roll(high, 4, 1)), roll(low, 4, 1)]
                v = jnp.concatenate(pair, axis=1)
                if block == 8:
                    if dz == 0:
                        v = roll(jnp.where(lane16 < 64, slots(ref, base + 68 - h, h), v), 64, 2)
                    else:
                        v = roll(jnp.where(lane16 < 64, v, slots(ref, base + 4, h)), 64, 2)
                put(ref, base + (4 - h if dz == 0 else 68), v)

            @pl.when(j < 7)
            def _():
                for copy in self.up:
                    copy.wait_send()

            @pl.when(j > 0)
            def _():
                for copy in self.down:
                    copy.wait_send()

            for copy in self.flat:
                copy.wait_send()

    half_lane = lax.broadcasted_iota(jnp.int32, (64, 128), 1) < 64

    def to_tiles(src, dst, base):
        for y in range(0, 8, 2):
            rows = [src[pl.ds(y + d, 64, stride=8), :] for d in range(2)]
            turned = jnp.concatenate(rows, axis=0).T
            low, high = turned[:64], turned[64:]
            first = (base + 4) * 16 + y
            dst[pl.ds(first, 64, stride=16), :] = jnp.where(half_lane, low, pltpu.roll(high, 64, 1))
            dst[pl.ds(first + 1, 64, stride=16), :] = jnp.where(half_lane, pltpu.roll(low, 64, 1), high)

    fext_rows, aext_rows = fext.reshape(512, 128), aext.reshape(512, 128)

    def x_gather(xg, n):
        other = b + 1 - 2 * lax.rem(b, 2)
        first = remote(xg.at[b], xg.at[b], xg_send.at[n, 0], xg_recv.at[n, 0], gx=other)
        early = [remote(xg.at[b], xg.at[b], xg_send.at[n, t], xg_recv.at[n, t], gx=lax.rem(b + 2 * t, 8))
                 for t in range(1, 4)]
        second = [remote(xg.at[other], xg.at[other], xg_send.at[n, 3 + t], xg_recv.at[n, 3 + t],
                         gx=lax.rem(b + 2 * t, 8)) for t in range(1, 4)]
        for copy in [first] + early:
            copy.start()
        return first, early, second

    def x_pack(weight, xg, faces=False):
        source = lax.broadcasted_iota(jnp.int32, (128, 256), 0)
        target = lax.broadcasted_iota(jnp.int32, (128, 256), 1)
        slot, inner = source % 16, (target % 128) % 32
        hit = (source // 64 == target // 128) & ((source % 64) // 16 == (target % 128) // 32) & (inner < 4)
        pair = (slot // 2 == inner + 2) & hit
        if faces:
            pair = pair & (((source % 64) // 16 != 0) | (slot % 2 == 1))
        matrix = jnp.where(pair, weight, 0.0).astype(F32)
        moved = jnp.dot(tb[...], matrix, precision=HIGHEST, preferred_element_type=F32)
        parts = [moved[:, :128].reshape(32, 8, 128), moved[:, 128:].reshape(32, 8, 128)]
        total = None
        for g in range(8):
            part = roll(parts[g // 4][(g % 4) * 8:(g % 4) * 8 + 8], 4 * g, 2)
            total = part if total is None else total + part
        packed = jnp.where(sub % 2 == 0, total[:4], total[4:])
        xg[b] = packed.reshape(32, 128)

    def x_unpack(xg, dst, base):
        g = (lane // 4) % 8
        for q in range(4):
            for odd in range(2):
                v = []
                for n in range(8):
                    tile = xg[n, pl.ds(q * 8, 8), :].reshape(1, 8, 128)
                    v.append(jnp.where(sub % 2 == 1, tile, roll(tile, -1, 1)) if odd
                             else jnp.where(sub % 2 == 0, tile, roll(tile, 1, 1)))
                for s in (1, 2, 4):
                    high = (g // s) % 2 == 1
                    for n in range(8):
                        if n & s == 0:
                            lo, hi = v[n], v[n + s]
                            v[n] = jnp.where(high, roll(hi, 4 * s, 2), lo)
                            v[n + s] = jnp.where(high, hi, roll(lo, -4 * s, 2))
                for n in range(8):
                    put(tmp, n * 8 + 4 * odd + q, v[n])
        for i in range(4):
            dst[pl.ds((base + 4) * 16 + i, 64, stride=16), :] = tmp[pl.ds(2 * i, 64, stride=8), :]

    own_a.wait()
    for copy in strips[:4]:
        copy.wait_recv()
    to_tiles(aext_rows, l0.wa, 1)
    edges = Wide(0, 8, l0.wa, 1, 4)
    edges.start()
    edges.finish()
    group0 = (lane16 // 16) % 4
    row16 = iota(1, (1, 16, 128))
    x_at = 8 * b + lane16 % 16 - 4
    y_at = 8 * j + jnp.where(row16 < 12, row16, row16 - 16)

    def face_body(i):
        a, xd, xu, yd, yu, zd, zu = neighbours(l0, l0.wa, i)
        z_at = 128 * k + 64 * (iota(2, a.shape) // 64) + i * l0.ch - 4 + iota(0, a.shape)
        side_up = jnp.where(group0 == 0, xu, jnp.where(group0 == 1, yu, zu))
        side_low = jnp.where(group0 == 0, xd, jnp.where(group0 == 1, yd, zd))
        where = jnp.where(group0 == 0, x_at, jnp.where(group0 == 1, y_at, z_at))
        end = jnp.where(group0 == 0, nx - 1, jnp.where(group0 == 1, ny - 1, nz - 1))
        l0.put(l0.up, i, jnp.where(where == end, 0.0, 0.5 * (a + side_up)))
        l0.put(l0.low, i, jnp.where(where == 0, 0.0, 0.5 * (a + side_low)))

    l0.loop(face_body)

    own_f.wait()
    for copy in strips[4:]:
        copy.wait_recv()
    to_tiles(fext_rows, l0.f, 0)
    edges = Wide(1, 8, l0.f, 0, 3)
    edges.start()

    def body(i):
        put(tb, i * 16, coarse_faces(*own_pairs(l0.up, i), 16, 1, None))

    loop(2, body)
    x_pack(0.25, xgf, True)
    faces_first, faces_early, faces_second = x_gather(xgf, 1)
    make_coefs(l0, 16)

    edges.finish()

    over_theta, ((a1, b1), (a2, b2)) = SMOOTH

    def downward(lv):
        init_down(lv, over_theta)
        step(lv, lv.wa, lv.wb, a1, b1, add="w")
        step(lv, lv.wb, lv.wa, a2, b2, add="x")
        if lv in (l0, l1):
            own_step(lv, lv.wa)
        else:
            step(lv, lv.wa, None)

    def upward(lv, coarse_at):
        init_up(lv, coarse_at)
        step(lv, lv.wa, lv.wb, None, over_theta, add="xw")
        step(lv, lv.wb, lv.wa, a1, b1)
        if lv in (l0, l1):
            own_step(lv, lv.wa, a2, b2)
        else:
            step(lv, lv.wa, None, a2, b2, add="xw", last=True)

    def own_sums(lv, i):
        pairs, roots = own_pairs(lv.r, i), own_pairs(lv.root, i)
        return pairs[0] * roots[0] + pairs[1] * roots[1]

    downward(l0)

    def body(i):
        put(tb, i * 16, both(own_sums(l0, i), 1, 1))

    loop(2, body)
    x_pack(0.125, xg1)
    right_first, right_early, right_second = x_gather(xg1, 0)
    faces_first.wait_recv()
    for copy in faces_second:
        copy.start()

    slot = lane % 16
    for side, first in ((0, 10), (1, 4)):
        packed = jnp.zeros((8, 8, 128), F32)
        for g in range(8):
            v = slots(l0.r, 4 + 8 * g, 8)[:, :8]
            packed = jnp.where(slot // 2 == g, roll(v, 2 * g - first, 2), packed)
        rxs[side] = packed.reshape(64, 128)
    rx = [remote(rxs.at[0], rxr.at[0], rx_send.at[0], rx_recv.at[0], gx=b_up),
          remote(rxs.at[1], rxr.at[1], rx_send.at[1], rx_recv.at[1], gx=b_down)]

    for copy in faces_early + faces_second:
        copy.wait_recv()
    x_unpack(xgf, l1.up, 1)
    edges = Wide(2, 4, l1.up, 1, 4)
    edges.start()

    c = b // 2

    def second_pack(q):
        start = pl.multiple_of(c * 64, 64)
        q[...] = jnp.where(lane2 % 2 == 0, tb[pl.ds(start, 8, stride=8), :], tb[pl.ds(start + 2, 8, stride=8), :])

    class Second:
        def __init__(self, q, yg, zh, n):
            yg[c, j] = q[...]
            self.along = [remote(q, yg.at[c, j], yg_send.at[n, t], yg_recv.at[n, t], gy=lax.rem(j + t, 8))
                          for t in range(1, 8)]
            self.quarters = [remote(yg.at[c], yg.at[c], yc_send.at[n, t], yc_recv.at[n, t], gx=lax.rem(b + 2 * t, 8))
                             for t in range(1, 4)]
            self.above = [remote(yg.at[3], zh.at[0], h_send.at[n, 0, t], h_recv.at[n, 0],
                                 gx=lax.rem(b + 2 * t, 8), gz=lax.rem(k + 1, 8)) for t in range(4)]
            self.below = [remote(yg.at[0], zh.at[1], h_send.at[n, 1, t], h_recv.at[n, 1],
                                 gx=lax.rem(b + 2 * t, 8), gz=lax.rem(k + 7, 8)) for t in range(4)]
            self.yg, self.zh = yg, zh
            for copy in self.along:
                copy.start()

        def spread(self):
            for copy in self.along:
                copy.wait_recv()
            for copy in self.quarters:
                copy.start()

            @pl.when(c == 3)
            def _():
                for copy in self.above:
                    copy.start()

            @pl.when(c == 0)
            def _():
                for copy in self.below:
                    copy.start()

        def finish(self, dst, base):
            for copy in self.quarters + [self.above[0], self.below[0]]:
                copy.wait_recv()
            yg, zh = self.yg, self.zh
            for n in range(8):
                v = jnp.concatenate([zh[0, n]] + [yg[m, n] for m in range(4)] + [zh[1, n]], axis=0)
                low, high = v[:24], v[24:]
                dst[pl.ds(base * 16 + 2 * n, 24, stride=16), :] = jnp.where(lane2 % 2 == 0, low, roll(high, 1, 1))
                dst[pl.ds(base * 16 + 2 * n + 1, 24, stride=16), :] = jnp.where(lane2 % 2 == 0, roll(low, -1, 1), high)

        def wait_send(self):
            for copy in self.along + self.quarters:
                copy.wait_send()

            @pl.when(c == 3)
            def _():
                for copy in self.above:
                    copy.wait_send()

            @pl.when(c == 0)
            def _():
                for copy in self.below:
                    copy.wait_send()

    def body(i):
        put(tb, i * 16, 0.25 * coarse_faces(*own_pairs(l1.up, i, 1), 32, 1, 1))

    loop(2, body)
    second_pack(qf)
    faces_second_level = Second(qf, ygf, zhf, 0)
    edges.finish()
    right_first.wait_recv()
    for copy in right_second:
        copy.start()
    make_coefs(l1, 32)

    for copy in right_early + right_second:
        copy.wait_recv()
    x_unpack(xg1, l1.f, 0)
    edges = Wide(3, 4, l1.f, 0, 3)
    edges.start()
    edges.finish()
    faces_second_level.spread()
    downward(l1)

    def body(i):
        put(tb, i * 16, 0.125 * both(both(own_sums(l1, i), 1, 1), 1, 2))

    loop(2, body)
    second_pack(q1)
    right_second_level = Second(q1, yg1, zh1, 1)
    faces_second_level.finish(l2.up, 1)

    t = lane % 4

    def third(ref, faces=False):
        g, odd_lane = lane // 32, lane % 2 == 1

        def rows(values, d):
            return values[pl.ds((16 if faces else 0) + d, 192, stride=2), :].reshape(24, 8, 128)

        if faces:
            v = jnp.where(g == 1, rows(ref, 1), rows(ref, 0) + rows(ref, 1))
        else:
            v = rows(ref, 0) * rows(l2.root, 0) + rows(ref, 1) * rows(l2.root, 1)
        halves = []
        for part in (v[8:], v[:16]):
            part = part.reshape(8, 2, 8, 128)
            both_z = part[:, 0] + part[:, 1]
            halves.append(jnp.where(g == 2, part[:, 1], both_z) if faces else both_z)
        v = jnp.concatenate([jnp.where(odd_lane, roll(halves[0], 1, 2), halves[0]),
                             jnp.where(odd_lane, halves[1], roll(halves[1], -1, 2))], axis=0)
        if faces:
            v = 0.25 * jnp.where(g == 0, pick(v, 2, 2), both(v, 2, 2))
        else:
            v = 0.125 * both(v, 2, 2)
        v = v.reshape(4, 4, 8, 128)
        out = v[:, 0]
        for u in range(1, 4):
            out = jnp.where(t == u, v[:, u], out)
        return out

    def z_gather(g, n, base):
        rows = pl.ds(pl.multiple_of((4 * k + base) * 8, 8), 32)
        return [remote(g.at[rows], g.at[rows], zg_send.at[n, u], zg_recv.at[n, u], gz=lax.rem(k + u, 8))
                for u in range(1, 8)]

    put(l3.up, 4 * k + 1, third(l2.up, True))
    third_faces = z_gather(l3.up, 0, 1)

    for copy in third_faces:
        copy.start()
    make_coefs(l2, 32)
    right_second_level.spread()
    for copy in rx:
        copy.start()
    for copy in third_faces:
        copy.wait_recv()
    make_coefs(l3, 32)

    group = lane // 32
    v = slots(l3.up, 1, 32, 8)
    v = jnp.where(group == 2, pick(v, 1, 2), both(v, 1, 2))
    v = jnp.where(group == 1, pick(v, 1, 1), both(v, 1, 1))
    fourth_coefs(l4, 0.25 * compact(jnp.where(group == 0, pick(v, 4, 2), both(v, 4, 2))))
    right_second_level.finish(l2.f, 0)
    edges1 = Wide(4, 4, l1.r, 0, 2)
    edges1.start()
    downward(l2)
    put(l3.f, 4 * k, third(l2.r))
    third_right = z_gather(l3.f, 1, 0)
    for copy in third_right:
        copy.start()

    edges1.finish()
    for copy in third_right:
        copy.wait_recv()

    downward(l3)

    v = slots(l3.r, 0, 32, 8) * slots(l3.root, 0, 32, 8)
    expand(l4.x, fourth_solve(l4, 0.125 * compact(both(both(both(v, 1, 2), 1, 1), 4, 2))))
    upward(l3, lambda i: l4.get(l4.x, i))

    for q in range(6):
        v = l3.x[pl.ds(pl.multiple_of(lax.rem(4 * k + q + 31, 32) * 8, 8), 8), :].reshape(1, 8, 128)
        for z in range(4):
            moved = v
            for u in range(4):
                if u != z:
                    moved = jnp.where(t == u, roll(v, u - z, 2), moved)
            first = (4 * q + z) * 16
            eb2[pl.ds(first, 8, stride=2), :] = moved.reshape(8, 128)
            eb2[pl.ds(first + 1, 8, stride=2), :] = moved.reshape(8, 128)

    def twice(ref, offset):
        def chunk(i):
            v = slots(ref, i * 4 + offset, 4)
            return jnp.broadcast_to(v[:, None], (4, 2, 16, 128)).reshape(8, 16, 128)

        return chunk

    def second_chunk(i):
        v = jnp.where(lane16 % 2 == 0, slots(eb2, i * 4, 4), slots(eb2, i * 4 + 12, 4))
        return jnp.broadcast_to(v[:, None], (4, 2, 16, 128)).reshape(8, 16, 128)

    upward(l2, second_chunk)

    for copy in rx:
        copy.wait_recv()
    for g in range(8):
        v = slots(l0.r, 4 + 8 * g, 8)
        own = v[:, :8]
        own = jnp.where(slot // 2 == 1, roll(rxr[0].reshape(8, 8, 128), 2 - 2 * g, 2), own)
        own = jnp.where(slot // 2 == 6, roll(rxr[1].reshape(8, 8, 128), 12 - 2 * g, 2), own)
        put(l0.r, 4 + 8 * g, jnp.concatenate([own, v[:, 8:]], axis=1))
    edges0 = Wide(5, 8, l0.r, 0, 2)
    edges0.start()

    for i, from_y in ((0, 0), (1, 1), (2, 2), (3, 3), (6, 14), (7, 15)):
        v = l2.x[pl.ds(lax.rem(2 * j + from_y, 16), 24, stride=16), :]
        low, high = jnp.where(lane2 % 2 == 0, v, roll(v, 1, 1)), jnp.where(lane2 % 2 == 1, v, roll(v, -1, 1))
        for d in range(2):
            eb1[pl.ds(2 * i + d, 24, stride=16), :] = low
            eb1[pl.ds(2 * i + d + 384, 24, stride=16), :] = high
    upward(l1, twice(eb1, 6))
    edges = Wide(6, 4, l1.x, 0, 2)
    edges.start()
    edges0.finish()
    edges.finish()

    source = lax.broadcasted_iota(jnp.int32, (128, 128), 0)
    target = lax.broadcasted_iota(jnp.int32, (128, 128), 1)
    hit = (source // 32 == (target % 64) // 16) & (source % 32 == 4 * b - 2 + (target % 16) // 2)
    v = slots(l1.x, 0, 72)
    v = jnp.where(sub < 6, v[:, :8], v[:, 8:]).reshape(576, 128)
    v = jnp.dot(v, jnp.where(hit, 1.0, 0.0).astype(F32), precision=HIGHEST, preferred_element_type=F32)
    eb0[pl.ds(0, 576, stride=2), :] = v
    eb0[pl.ds(1, 576, stride=2), :] = v

    def top_chunk(i):
        v = jnp.where(lane16 < 64, slots(eb0, i * 4 + 2, 4), slots(eb0, i * 4 + 34, 4))
        return jnp.broadcast_to(v[:, None], (4, 2, 16, 128)).reshape(8, 16, 128)

    upward(l0, top_chunk)

    for y in range(0, 8, 2):
        first = l0.x[pl.ds(64 + y, 64, stride=16), :]
        second = l0.x[pl.ds(65 + y, 64, stride=16), :]
        low = jnp.where(half_lane, first, pltpu.roll(second, 64, 1))
        high = jnp.where(half_lane, pltpu.roll(first, 64, 1), second)
        turned = pltpu.roll(jnp.concatenate([low, high], axis=0), 124, 1).T
        for d in range(2):
            for v in range(4):
                start = d * 64 + v * 16
                out_ref[pl.ds(v * 64 + y + d, 8, stride=8), :] = turned[start:start + 8]

    for copy in (strips + [faces_first, right_first] + faces_early + right_early + faces_second + right_second + rx
                 + third_faces + third_right):
        copy.wait_send()
    faces_second_level.wait_send()
    right_second_level.wait_send()


def solution(mesh):
    def per_device(right_side, affinity):
        nx = affinity.shape[1] * mesh.shape["gx"]
        ny = affinity.shape[2] * mesh.shape["gy"]
        nz = affinity.shape[3] * mesh.shape["gz"]
        scratch = []
        for z, rows, *_ in LEVELS:
            scratch += level_shapes(z, rows)
        scratch += [pltpu.VMEM(shape, F32) for shape in (
            (4, 16, 8, 128), (4, 16, 8, 128),
            (7, 2, 4, 64, 128), (7, 2, 4, 64, 128), (7, 2, 32, 128), (7, 2, 3, 32, 128),
            (256, 128), (512, 128), (8, 32, 128), (8, 32, 128), (2, 64, 128), (2, 64, 128),
            (8, 128), (8, 128), (4, 8, 8, 128), (4, 8, 8, 128), (2, 8, 8, 128), (2, 8, 8, 128), (384, 128), (768, 128), (1152, 128))]
        dma = pltpu.SemaphoreType.DMA
        scratch += [dma(shape) for shape in (
            (2,), (6,), (6,), (7, 8), (7, 8), (2, 7), (2, 7), (2,), (2,), (2, 2, 4), (2, 2), (2, 8), (2, 8), (2, 4), (2, 4), (2, 8), (2, 8))]
        out = pl.pallas_call(
            functools.partial(kernel, nx, ny, nz),
            out_shape=jax.ShapeDtypeStruct((256, 128), F32),
            in_specs=[pl.BlockSpec(memory_space=pl.ANY)] * 2,
            out_specs=pl.BlockSpec(memory_space=pltpu.VMEM),
            scratch_shapes=scratch,
            compiler_params=pltpu.CompilerParams(
                collective_id=0, has_side_effects=True, vmem_limit_bytes=60 * 1024 * 1024),
        )(right_side, affinity)
        return out.reshape(right_side.shape)

    spec = P(None, "gx", "gy", "gz")
    return jax.shard_map(per_device, mesh=mesh, in_specs=(spec, spec), out_specs=spec, check_vma=False)
```

```python
import functools

import jax
import jax.numpy as jnp
from jax import lax
from jax.experimental import pallas as pl
from jax.experimental.pallas import tpu as pltpu
from jax.sharding import PartitionSpec as P

MESH = pl.DeviceIdType.MESH
HIGHEST = lax.Precision.HIGHEST
F32 = jnp.float32

DEGREE = 3
COARSE_DEGREE = 8
SHIFT = 0.02
SMOOTH_LOWER = 0.5
UPPER = 2.0 + SHIFT


def cheb_coefs(a, b, m):
    theta, delta = 0.5 * (b + a), 0.5 * (b - a)
    sigma = theta / delta
    rho = 1.0 / sigma
    steps = []
    for _ in range(m - 1):
        nxt = 1.0 / (2.0 * sigma - rho)
        steps.append((nxt * rho, 2.0 * nxt / delta))
        rho = nxt
    return 1.0 / theta, steps


SMOOTH = cheb_coefs(SMOOTH_LOWER, UPPER, DEGREE)
SOLVE = cheb_coefs(SHIFT, UPPER, COARSE_DEGREE)


def iota(dim, shape=(1, 8, 128)):
    return lax.broadcasted_iota(jnp.int32, shape, dim)


def roll(x, shift, axis):
    shift = shift % x.shape[axis]
    return x if shift == 0 else pltpu.roll(x, shift, axis)


def both(x, k, axis):
    bit = (iota(axis, (1,) + x.shape[1:]) // k) % 2
    return x + jnp.where(bit == 0, roll(x, -k, axis), roll(x, k, axis))


def pick(x, k, axis):
    bit = (iota(axis, (1,) + x.shape[1:]) // k) % 2
    return jnp.where(bit == 1, x, roll(x, -k, axis))


def slots(ref, start, count, rows=16):
    if not isinstance(start, int):
        start = pl.multiple_of(start * rows, rows)
    else:
        start = start * rows
    return ref[pl.ds(start, count * rows), :].reshape(count, rows, 128)


def put(ref, start, value):
    count, rows = value.shape[:2]
    if not isinstance(start, int):
        start = pl.multiple_of(start * rows, rows)
    else:
        start = start * rows
    ref[pl.ds(start, count * rows), :] = value.reshape(count * rows, 128)


def loop(count, body):
    def run(i, carry):
        body(i)
        return carry

    lax.fori_loop(0, count, run, 0)


class Level:
    def __init__(self, z, rows, sy, sx, mode, refs):
        self.z, self.rows, self.sy, self.sx, self.mode = z, rows, sy, sx, mode
        self.ch = 128 // rows
        self.parts = z // self.ch
        (self.coef, self.scale, self.root, self.f, self.r, self.x, self.wa, self.wb, self.up, self.low,
         self.r_next, self.x_next) = refs

    def loop(self, body):
        def turn(i, carry):
            for part in range(self.parts):
                body(i * self.parts + part)
            return carry

        turns = self.z // (self.ch * self.parts)
        if turns == 1:
            turn(0, 0)
        else:
            lax.fori_loop(0, turns, turn, 0)

    def get(self, ref, i, offset=0):
        return slots(ref, i * self.ch + offset, self.ch, self.rows)

    def put(self, ref, i, value, offset=0):
        put(ref, i * self.ch + offset, value)


LEVELS = ((72, 16, 1, 1, 0), (72, 16, 1, 1, 0), (24, 16, 1, 2, 0), (32, 8, 1, 4, 1), (32, 8, 2, 8, 2))


def level_shapes(z, rows):
    n = z * rows
    pad = (z + 2) * rows
    return [pltpu.VMEM((6 * n, 128), F32)] + [pltpu.VMEM((n, 128), F32)] * 5 + [pltpu.VMEM((pad, 128), F32)] * 4 + [
        pltpu.VMEM((n, 128), F32)] * 2


def join_halves(ref):
    odd = iota(2, (1, 16, 128)) % 2 == 1
    put(ref, 0, jnp.where(odd, roll(slots(ref, 24, 1), 1, 2), 0.0))
    put(ref, 25, jnp.where(odd, 0.0, roll(slots(ref, 1, 1), -1, 2)))


def neighbours(lv, w_ref, i):
    w, before, after = lv.get(w_ref, i, 1), lv.get(w_ref, i, 0), lv.get(w_ref, i, 2)
    xd, xu = roll(w, lv.sx, 2), roll(w, -lv.sx, 2)
    yd, yu = roll(w, lv.sy, 1), roll(w, -lv.sy, 1)
    if lv.mode == 0:
        zd, zu = before, after
    else:
        s = lv.mode
        t = iota(2) % 4
        zu = jnp.where(t < 4 - s, roll(w, -s, 2), roll(after, 4 - s, 2))
        zd = jnp.where(t >= s, roll(w, s, 2), roll(before, s - 4, 2))
    return w, xd, xu, yd, yu, zd, zu


def init_down(lv, over_theta):
    def body(i):
        r = lv.get(lv.scale, i) * lv.get(lv.f, i)
        lv.put(lv.r, i, r)
        lv.put(lv.wa, i, r * over_theta, 1)

    lv.loop(body)


def init_up(lv, coarse_at):
    def body(i):
        lv.put(lv.wa, i, lv.get(lv.scale, i) * coarse_at(i), 1)

    lv.loop(body)


def step(lv, w_ref, w_next, alpha=None, beta=None, add="", last=False):
    if lv.z == 24:
        join_halves(w_ref)

    def body(i):
        w, *near = neighbours(lv, w_ref, i)
        total = None
        for k, value in enumerate(near):
            term = slots(lv.coef, k * lv.z + i * lv.ch, lv.ch, lv.rows) * value
            total = term if total is None else total + term
        r = lv.get(lv.r, i) - ((1.0 + SHIFT) * w - total)
        if not last:
            lv.put(lv.r_next, i, r)
        if beta is None:
            return
        new = beta * r if alpha is None else alpha * w + beta * r
        if add:
            x = new + w if "w" in add else new
            if "x" in add:
                x = x + lv.get(lv.x, i)
            lv.put(lv.x_next, i, x * lv.get(lv.root, i) if last else x)
        if not last:
            lv.put(w_next, i, new, 1)

    lv.loop(body)
    if not last:
        lv.r, lv.r_next = lv.r_next, lv.r
    if add:
        lv.x, lv.x_next = lv.x_next, lv.x


def make_coefs(lv, group):
    g = (iota(2, (1, lv.rows, 128)) // group) % 4

    def spread(value, k):
        out = value
        for to in range(4):
            if to != k:
                out = jnp.where(g == to, roll(value, group * (to - k), 2), out)
        return out

    if lv.z == 24:
        join_halves(lv.up)

    def body(i):
        if group == 16:
            up = lv.get(lv.up, i)
            lows = [lv.get(lv.low, i)] * 3
        else:
            up, x_low, _, y_low, _, z_low, _ = neighbours(lv, lv.up, i)
            lows = [jnp.where(iota(2, (1, lv.rows, 128)) % 32 < lv.sx, 0.0, x_low), y_low, z_low]
        faces = []
        for k in range(3):
            faces += [spread(lows[k], k), spread(up, k)]
        total = faces[0] + faces[1] + faces[2] + faces[3] + faces[4] + faces[5]
        scale = jnp.where(total > 0.0, lax.rsqrt(total), 0.0)
        lv.put(lv.scale, i, scale)
        lv.put(lv.root, i, scale * total)
        square = scale * scale
        for k in range(6):
            put(lv.coef, k * lv.z + i * lv.ch, square * faces[k])

    lv.loop(body)


def own_pairs(ref, i, base=0):
    v = slots(ref, base + 4 + 32 * i, 32)[:, :8].reshape(16, 2, 8, 128)
    return v[:, 0], v[:, 1]


def coarse_faces(first, second, group, ky, kx):
    g = (iota(2) // group) % 4
    v = jnp.where(g == 2, second, first + second)
    v = jnp.where(g == 1, pick(v, ky, 1), both(v, ky, 1))
    if kx is not None:
        v = jnp.where(g == 0, pick(v, kx, 2), both(v, kx, 2))
    return v


def own_step(lv, w_ref, alpha=None, beta=None):
    def body(i):
        first = 4 + 8 * i
        here = slots(w_ref, first + 1, 8)
        w = here[:, :8]
        near = [roll(w, 1, 2), roll(w, -1, 2), roll(here, 1, 1)[:, :8], roll(here, -1, 1)[:, :8],
                slots(w_ref, first, 8)[:, :8], slots(w_ref, first + 2, 8)[:, :8]]
        total = None
        for k, value in enumerate(near):
            term = slots(lv.coef, k * lv.z + first, 8)[:, :8] * value
            total = term if total is None else total + term
        r = slots(lv.r, first, 8)[:, :8] - ((1.0 + SHIFT) * w - total)
        if beta is not None:
            x = slots(lv.x, first, 8)[:, :8] + w + (alpha * w + beta * r)
            r = x * slots(lv.root, first, 8)[:, :8]
        target = lv.r_next if beta is None else lv.x_next
        for n in range(8):
            target[pl.ds(pl.multiple_of((first + n) * 16, 16), 8), :] = r[n]

    def turn(i, carry):
        for part in range(4):
            body(4 * i + part)
        return carry

    lax.fori_loop(0, 2, turn, 0)
    if beta is None:
        lv.r, lv.r_next = lv.r_next, lv.r
    else:
        lv.x, lv.x_next = lv.x_next, lv.x


def compact(v):
    v = v.reshape(8, 4, 8, 128)
    v = [v[n] for n in range(8)]
    for bit in (iota(2) % 2, (iota(2) // 4) % 2, iota(1) % 2):
        v = [jnp.where(bit == 0, v[n], v[n + 1]) for n in range(0, len(v), 2)]
    return v[0]


def expand(ref, v):
    out = [v]
    for k, axis in ((1, 1), (4, 2), (1, 2)):
        bit = (iota(axis) // k) % 2
        out = [jnp.where(bit == m, w, roll(w, k if m == 0 else -k, axis)) for w in out for m in range(2)]
    for n in range(8):
        put(ref, 4 * n, out[n])


def fourth_neighbours(w):
    low0, low2, t = iota(2) % 2, (iota(2) // 4) % 2, (iota(2) // 2) % 2
    last, first = w[3:], w[:1]
    up = jnp.where(low0 == 0, roll(first, -1, 2),
                   jnp.where(low2 == 0, roll(first, -3, 2), roll(roll(first, 5, 2), -1, 1)))
    down = jnp.where(low0 == 1, roll(last, 1, 2),
                     jnp.where(low2 == 1, roll(last, 3, 2), roll(roll(last, -5, 2), 1, 1)))
    after, before = jnp.concatenate([w[1:], up], axis=0), jnp.concatenate([down, w[:3]], axis=0)
    return [roll(w, 8, 2), roll(w, -8, 2), roll(w, 2, 1), roll(w, -2, 1),
            jnp.where(t == 1, roll(w, 2, 2), roll(before, -2, 2)),
            jnp.where(t == 0, roll(w, -2, 2), roll(after, 2, 2))]


def fourth_coefs(lv, up):
    x_low, _, y_low, _, z_low, _ = fourth_neighbours(up)
    lows = [jnp.where(iota(2) % 32 < 8, 0.0, x_low), y_low, z_low]
    g = iota(2) // 32
    faces = []
    for k in range(3):
        for value in (lows[k], up):
            out = value
            for to in range(4):
                if to != k:
                    out = jnp.where(g == to, roll(value, 32 * (to - k), 2), out)
            faces.append(out)
    total = faces[0] + faces[1] + faces[2] + faces[3] + faces[4] + faces[5]
    scale = lax.rsqrt(total)
    put(lv.scale, 0, scale)
    put(lv.root, 0, scale * total)
    for k in range(6):
        put(lv.coef, 4 * k, scale * scale * faces[k])


def fourth_solve(lv, f):
    over_theta, steps = SOLVE
    coefs = [slots(lv.coef, 4 * k, 4, 8) for k in range(6)]
    r = slots(lv.scale, 0, 4, 8) * f
    w = x = r * over_theta
    for alpha, beta in steps:
        total = None
        for coef, value in zip(coefs, fourth_neighbours(w)):
            total = coef * value if total is None else total + coef * value
        r = r - ((1.0 + SHIFT) * w - total)
        w = alpha * w + beta * r
        x = x + w
    return x * slots(lv.root, 0, 4, 8)


def kernel(nx, ny, nz, f_hbm, a_hbm, out_ref, *scratch):
    refs = list(scratch)

    def take(count):
        got = refs[:count]
        del refs[:count]
        return got

    levels = [Level(*shape, take(12)) for shape in LEVELS]
    (fext, aext, ys, yr, zs, zr, tb, tmp, xg1, xgf, rxs, rxr, q1, qf, yg1, ygf, zh1, zhf, eb2, eb1, eb0) = take(21)
    (local_sem, strip_send, strip_recv, ex_send, ex_recv, xg_send, xg_recv, rx_send, rx_recv,
     h_send, h_recv, yg_send, yg_recv, yc_send, yc_recv, zg_send, zg_recv) = take(17)
    l0, l1, l2, l3, l4 = levels

    b, j, k = lax.axis_index("gx"), lax.axis_index("gy"), lax.axis_index("gz")
    sub, lane, lane16 = iota(1), iota(2), iota(2, (1, 16, 128))
    lane2 = lax.broadcasted_iota(jnp.int32, (1, 128), 1)

    def remote(src, dst, send, recv, **to):
        return pltpu.make_async_remote_copy(
            src_ref=src, dst_ref=dst, send_sem=send, recv_sem=recv, device_id=to, device_id_type=MESH)

    own_f = pltpu.make_async_copy(f_hbm, fext.at[:, pl.ds(4, 8)], local_sem.at[0])
    own_a = pltpu.make_async_copy(a_hbm, aext.at[pl.ds(0, 3), pl.ds(4, 8)], local_sem.at[1])
    own_a.start()
    own_f.start()
    zr[...] = jnp.zeros_like(zr)

    barrier = pltpu.get_barrier_semaphore()
    partners = [{"gx": lax.rem(b + t, 8)} for t in (1, 2, 4, 6, 7)]
    partners += [{"gy": lax.rem(j + t, 8)} for t in range(1, 8)]
    partners += [{"gz": lax.rem(k + t, 8)} for t in range(1, 8)]
    partners += [{"gy": lax.rem(j + t, 8), "gz": lax.rem(k + u, 8)} for t in (1, 7) for u in (1, 7)]
    partners += [{"gx": lax.rem(b + t, 8), "gz": lax.rem(k + u, 8)} for t in (2, 4, 6) for u in (1, 7)]
    for to in partners:
        pl.semaphore_signal(barrier, inc=1, device_id=to, device_id_type=MESH)

    fext[:, 0] = jnp.zeros((4, 8, 128), F32)
    fext[:, 15] = jnp.zeros((4, 8, 128), F32)
    aext[3] = jnp.zeros((16, 8, 128), F32)
    for n in (1, 2):
        aext[n, 0] = jnp.zeros((8, 128), F32)
        aext[n, 15] = jnp.zeros((8, 128), F32)
    for ref in (l0.f, l0.wa, l1.f, l1.up, eb1):
        ref[...] = jnp.zeros_like(ref)
    for lv in levels:
        for w in (lv.wa, lv.wb, lv.up):
            w[pl.ds(0, lv.rows), :] = jnp.zeros((lv.rows, 128), F32)
            w[pl.ds((lv.z + 1) * lv.rows, lv.rows), :] = jnp.zeros((lv.rows, 128), F32)
    pl.semaphore_wait(barrier, len(partners))

    b_up, b_down = lax.rem(b + 1, 8), lax.rem(b + 7, 8)
    strips = [
        remote(a_hbm.at[:, pl.ds(5, 3)], aext.at[pl.ds(0, 3), pl.ds(1, 3)],
               strip_send.at[0], strip_recv.at[0], gx=b_up),
        remote(a_hbm.at[:, pl.ds(0, 3)], aext.at[pl.ds(0, 3), pl.ds(12, 3)],
               strip_send.at[1], strip_recv.at[1], gx=b_down),
        remote(a_hbm.at[0, 4], aext.at[0, 0], strip_send.at[4], strip_recv.at[4], gx=b_up),
        remote(a_hbm.at[0, 3], aext.at[0, 15], strip_send.at[5], strip_recv.at[5], gx=b_down),
        remote(f_hbm.at[:, pl.ds(5, 3)], fext.at[:, pl.ds(1, 3)],
               strip_send.at[2], strip_recv.at[2], gx=b_up),
        remote(f_hbm.at[:, pl.ds(0, 3)], fext.at[:, pl.ds(12, 3)],
               strip_send.at[3], strip_recv.at[3], gx=b_down),
    ]
    for copy in strips[:4]:
        copy.start()
    for copy in strips[:4]:
        copy.wait_send()
    for copy in strips[4:]:
        copy.start()

    class Wide:
        def __init__(self, n, block, ref, base, h):
            self.n, self.block, self.ref, self.base, self.h = n, block, ref, base, h
            rows, part = pl.ds(0, h), pl.ds(0, h * 8)
            j_up, j_down = jnp.minimum(j + 1, 7), jnp.maximum(j - 1, 0)
            k_to = (lax.rem(k + 1, 8), lax.rem(k + 7, 8))

            def make(src, dst, index, **to):
                return remote(src, dst, ex_send.at[n, index], ex_recv.at[n, index], **to)

            self.up = [make(ys.at[n, 0, rows], yr.at[n, 0, rows], 0, gy=j_up)]
            self.down = [make(ys.at[n, 1, rows], yr.at[n, 1, rows], 1, gy=j_down)]
            self.flat = []
            for dz in range(2):
                self.flat.append(make(zs.at[n, dz, part], zr.at[n, dz, 0, part], 2 + dz, gz=k_to[dz]))
                self.up.append(make(zs.at[n, dz, part], zr.at[n, dz, 1, part], 4 + dz, gy=j_up, gz=k_to[dz]))
                self.down.append(make(zs.at[n, dz, part], zr.at[n, dz, 2, part], 6 + dz, gy=j_down, gz=k_to[dz]))

        def start(self):
            n, block, ref, base, h = self.n, self.block, self.ref, self.base, self.h
            for i in range(h):
                ys[n, 0, i] = ref[pl.ds((base + 4) * 16 + block - h + i, 64, stride=16), :]
                ys[n, 1, i] = ref[pl.ds((base + 4) * 16 + i, 64, stride=16), :]
                zs[n, 0, pl.ds(i * 8, 8), :] = ref[pl.ds((base + 68 - h + i) * 16, 8), :]
                zs[n, 1, pl.ds(i * 8, 8), :] = ref[pl.ds((base + 4 + i) * 16, 8), :]

            @pl.when(j < 7)
            def _():
                for copy in self.up:
                    copy.start()

            @pl.when(j > 0)
            def _():
                for copy in self.down:
                    copy.start()

            for copy in self.flat:
                copy.start()

        def finish(self):
            n, block, ref, base, h = self.n, self.block, self.ref, self.base, self.h

            @pl.when(j > 0)
            def _():
                for copy in self.up:
                    copy.wait_recv()
                for i in range(h):
                    ref[pl.ds((base + 4) * 16 + 16 - h + i, 64, stride=16), :] = yr[n, 0, i]

            @pl.when(j < 7)
            def _():
                for copy in self.down:
                    copy.wait_recv()
                for i in range(h):
                    ref[pl.ds((base + 4) * 16 + block + i, 64, stride=16), :] = yr[n, 1, i]

            for copy in self.flat:
                copy.wait_recv()
            for dz in range(2):
                here, low, high = (zr[n, dz, m, pl.ds(0, h * 8), :].reshape(h, 8, 128) for m in range(3))
                if block == 8:
                    pair = [here, jnp.where(sub < 4, high, low)]
                else:
                    pair = [jnp.where(sub < 4, here, roll(high, 4, 1)), roll(low, 4, 1)]
                v = jnp.concatenate(pair, axis=1)
                if block == 8:
                    if dz == 0:
                        v = roll(jnp.where(lane16 < 64, slots(ref, base + 68 - h, h), v), 64, 2)
                    else:
                        v = roll(jnp.where(lane16 < 64, v, slots(ref, base + 4, h)), 64, 2)
                put(ref, base + (4 - h if dz == 0 else 68), v)

            @pl.when(j < 7)
            def _():
                for copy in self.up:
                    copy.wait_send()

            @pl.when(j > 0)
            def _():
                for copy in self.down:
                    copy.wait_send()

            for copy in self.flat:
                copy.wait_send()

    half_lane = lax.broadcasted_iota(jnp.int32, (64, 128), 1) < 64

    def to_tiles(src, dst, base):
        for y in range(0, 8, 2):
            rows = [src[pl.ds(y + d, 64, stride=8), :] for d in range(2)]
            turned = jnp.concatenate(rows, axis=0).T
            low, high = turned[:64], turned[64:]
            first = (base + 4) * 16 + y
            dst[pl.ds(first, 64, stride=16), :] = jnp.where(half_lane, low, pltpu.roll(high, 64, 1))
            dst[pl.ds(first + 1, 64, stride=16), :] = jnp.where(half_lane, pltpu.roll(low, 64, 1), high)

    fext_rows, aext_rows = fext.reshape(512, 128), aext.reshape(512, 128)

    def x_gather(xg, n):
        other = b + 1 - 2 * lax.rem(b, 2)
        first = remote(xg.at[b], xg.at[b], xg_send.at[n, 0], xg_recv.at[n, 0], gx=other)
        early = [remote(xg.at[b], xg.at[b], xg_send.at[n, t], xg_recv.at[n, t], gx=lax.rem(b + 2 * t, 8))
                 for t in range(1, 4)]
        second = [remote(xg.at[other], xg.at[other], xg_send.at[n, 3 + t], xg_recv.at[n, 3 + t],
                         gx=lax.rem(b + 2 * t, 8)) for t in range(1, 4)]
        for copy in [first] + early:
            copy.start()
        return first, early, second

    def x_pack(weight, xg, faces=False):
        source = lax.broadcasted_iota(jnp.int32, (128, 256), 0)
        target = lax.broadcasted_iota(jnp.int32, (128, 256), 1)
        slot, inner = source % 16, (target % 128) % 32
        hit = (source // 64 == target // 128) & ((source % 64) // 16 == (target % 128) // 32) & (inner < 4)
        pair = (slot // 2 == inner + 2) & hit
        if faces:
            pair = pair & (((source % 64) // 16 != 0) | (slot % 2 == 1))
        matrix = jnp.where(pair, weight, 0.0).astype(F32)
        moved = jnp.dot(tb[...], matrix, precision=HIGHEST, preferred_element_type=F32)
        parts = [moved[:, :128].reshape(32, 8, 128), moved[:, 128:].reshape(32, 8, 128)]
        total = None
        for g in range(8):
            part = roll(parts[g // 4][(g % 4) * 8:(g % 4) * 8 + 8], 4 * g, 2)
            total = part if total is None else total + part
        packed = jnp.where(sub % 2 == 0, total[:4], total[4:])
        xg[b] = packed.reshape(32, 128)

    def x_unpack(xg, dst, base):
        g = (lane // 4) % 8
        for q in range(4):
            for odd in range(2):
                v = []
                for n in range(8):
                    tile = xg[n, pl.ds(q * 8, 8), :].reshape(1, 8, 128)
                    v.append(jnp.where(sub % 2 == 1, tile, roll(tile, -1, 1)) if odd
                             else jnp.where(sub % 2 == 0, tile, roll(tile, 1, 1)))
                for s in (1, 2, 4):
                    high = (g // s) % 2 == 1
                    for n in range(8):
                        if n & s == 0:
                            lo, hi = v[n], v[n + s]
                            v[n] = jnp.where(high, roll(hi, 4 * s, 2), lo)
                            v[n + s] = jnp.where(high, hi, roll(lo, -4 * s, 2))
                for n in range(8):
                    put(tmp, n * 8 + 4 * odd + q, v[n])
        for i in range(4):
            dst[pl.ds((base + 4) * 16 + i, 64, stride=16), :] = tmp[pl.ds(2 * i, 64, stride=8), :]

    own_a.wait()
    for copy in strips[:4]:
        copy.wait_recv()
    to_tiles(aext_rows, l0.wa, 1)
    edges = Wide(0, 8, l0.wa, 1, 4)
    edges.start()
    edges.finish()
    group0 = (lane16 // 16) % 4
    row16 = iota(1, (1, 16, 128))
    x_at = 8 * b + lane16 % 16 - 4
    y_at = 8 * j + jnp.where(row16 < 12, row16, row16 - 16)

    def face_body(i):
        a, xd, xu, yd, yu, zd, zu = neighbours(l0, l0.wa, i)
        z_at = 128 * k + 64 * (iota(2, a.shape) // 64) + i * l0.ch - 4 + iota(0, a.shape)
        side_up = jnp.where(group0 == 0, xu, jnp.where(group0 == 1, yu, zu))
        side_low = jnp.where(group0 == 0, xd, jnp.where(group0 == 1, yd, zd))
        where = jnp.where(group0 == 0, x_at, jnp.where(group0 == 1, y_at, z_at))
        end = jnp.where(group0 == 0, nx - 1, jnp.where(group0 == 1, ny - 1, nz - 1))
        l0.put(l0.up, i, jnp.where(where == end, 0.0, 0.5 * (a + side_up)))
        l0.put(l0.low, i, jnp.where(where == 0, 0.0, 0.5 * (a + side_low)))

    l0.loop(face_body)

    own_f.wait()
    for copy in strips[4:]:
        copy.wait_recv()
    to_tiles(fext_rows, l0.f, 0)
    edges = Wide(1, 8, l0.f, 0, 3)
    edges.start()

    def body(i):
        put(tb, i * 16, coarse_faces(*own_pairs(l0.up, i), 16, 1, None))

    loop(2, body)
    x_pack(0.25, xgf, True)
    faces_first, faces_early, faces_second = x_gather(xgf, 1)
    make_coefs(l0, 16)

    edges.finish()

    over_theta, ((a1, b1), (a2, b2)) = SMOOTH

    def downward(lv):
        init_down(lv, over_theta)
        step(lv, lv.wa, lv.wb, a1, b1, add="w")
        step(lv, lv.wb, lv.wa, a2, b2, add="x")
        if lv in (l0, l1):
            own_step(lv, lv.wa)
        else:
            step(lv, lv.wa, None)

    def upward(lv, coarse_at):
        init_up(lv, coarse_at)
        step(lv, lv.wa, lv.wb, None, over_theta, add="xw")
        step(lv, lv.wb, lv.wa, a1, b1)
        if lv in (l0, l1):
            own_step(lv, lv.wa, a2, b2)
        else:
            step(lv, lv.wa, None, a2, b2, add="xw", last=True)

    def own_sums(lv, i):
        pairs, roots = own_pairs(lv.r, i), own_pairs(lv.root, i)
        return pairs[0] * roots[0] + pairs[1] * roots[1]

    downward(l0)

    def body(i):
        put(tb, i * 16, both(own_sums(l0, i), 1, 1))

    loop(2, body)
    x_pack(0.125, xg1)
    right_first, right_early, right_second = x_gather(xg1, 0)
    faces_first.wait_recv()
    for copy in faces_second:
        copy.start()

    slot = lane % 16
    for side, first in ((0, 10), (1, 4)):
        packed = jnp.zeros((8, 8, 128), F32)
        for g in range(8):
            v = slots(l0.r, 4 + 8 * g, 8)[:, :8]
            packed = jnp.where(slot // 2 == g, roll(v, 2 * g - first, 2), packed)
        rxs[side] = packed.reshape(64, 128)
    rx = [remote(rxs.at[0], rxr.at[0], rx_send.at[0], rx_recv.at[0], gx=b_up),
          remote(rxs.at[1], rxr.at[1], rx_send.at[1], rx_recv.at[1], gx=b_down)]

    for copy in faces_early + faces_second:
        copy.wait_recv()
    x_unpack(xgf, l1.up, 1)
    edges = Wide(2, 4, l1.up, 1, 4)
    edges.start()

    c = b // 2

    def second_pack(q):
        start = pl.multiple_of(c * 64, 64)
        q[...] = jnp.where(lane2 % 2 == 0, tb[pl.ds(start, 8, stride=8), :], tb[pl.ds(start + 2, 8, stride=8), :])

    class Second:
        def __init__(self, q, yg, zh, n):
            yg[c, j] = q[...]
            self.along = [remote(q, yg.at[c, j], yg_send.at[n, t], yg_recv.at[n, t], gy=lax.rem(j + t, 8))
                          for t in range(1, 8)]
            self.quarters = [remote(yg.at[c], yg.at[c], yc_send.at[n, t], yc_recv.at[n, t], gx=lax.rem(b + 2 * t, 8))
                             for t in range(1, 4)]
            self.above = [remote(yg.at[3], zh.at[0], h_send.at[n, 0, t], h_recv.at[n, 0],
                                 gx=lax.rem(b + 2 * t, 8), gz=lax.rem(k + 1, 8)) for t in range(4)]
            self.below = [remote(yg.at[0], zh.at[1], h_send.at[n, 1, t], h_recv.at[n, 1],
                                 gx=lax.rem(b + 2 * t, 8), gz=lax.rem(k + 7, 8)) for t in range(4)]
            self.yg, self.zh = yg, zh
            for copy in self.along:
                copy.start()

        def spread(self):
            for copy in self.along:
                copy.wait_recv()
            for copy in self.quarters:
                copy.start()

            @pl.when(c == 3)
            def _():
                for copy in self.above:
                    copy.start()

            @pl.when(c == 0)
            def _():
                for copy in self.below:
                    copy.start()

        def finish(self, dst, base):
            for copy in self.quarters + [self.above[0], self.below[0]]:
                copy.wait_recv()
            yg, zh = self.yg, self.zh
            for n in range(8):
                v = jnp.concatenate([zh[0, n]] + [yg[m, n] for m in range(4)] + [zh[1, n]], axis=0)
                low, high = v[:24], v[24:]
                dst[pl.ds(base * 16 + 2 * n, 24, stride=16), :] = jnp.where(lane2 % 2 == 0, low, roll(high, 1, 1))
                dst[pl.ds(base * 16 + 2 * n + 1, 24, stride=16), :] = jnp.where(lane2 % 2 == 0, roll(low, -1, 1), high)

        def wait_send(self):
            for copy in self.along + self.quarters:
                copy.wait_send()

            @pl.when(c == 3)
            def _():
                for copy in self.above:
                    copy.wait_send()

            @pl.when(c == 0)
            def _():
                for copy in self.below:
                    copy.wait_send()

    def body(i):
        put(tb, i * 16, 0.25 * coarse_faces(*own_pairs(l1.up, i, 1), 32, 1, 1))

    loop(2, body)
    second_pack(qf)
    faces_second_level = Second(qf, ygf, zhf, 0)
    edges.finish()
    right_first.wait_recv()
    for copy in right_second:
        copy.start()
    make_coefs(l1, 32)

    for copy in right_early + right_second:
        copy.wait_recv()
    x_unpack(xg1, l1.f, 0)
    edges = Wide(3, 4, l1.f, 0, 3)
    edges.start()
    edges.finish()
    faces_second_level.spread()
    downward(l1)

    def body(i):
        put(tb, i * 16, 0.125 * both(both(own_sums(l1, i), 1, 1), 1, 2))

    loop(2, body)
    second_pack(q1)
    right_second_level = Second(q1, yg1, zh1, 1)
    faces_second_level.finish(l2.up, 1)

    t = lane % 4

    def third(ref, faces=False):
        g, odd_lane = lane // 32, lane % 2 == 1

        def rows(values, d):
            return values[pl.ds((16 if faces else 0) + d, 192, stride=2), :].reshape(24, 8, 128)

        if faces:
            v = jnp.where(g == 1, rows(ref, 1), rows(ref, 0) + rows(ref, 1))
        else:
            v = rows(ref, 0) * rows(l2.root, 0) + rows(ref, 1) * rows(l2.root, 1)
        halves = []
        for part in (v[8:], v[:16]):
            part = part.reshape(8, 2, 8, 128)
            both_z = part[:, 0] + part[:, 1]
            halves.append(jnp.where(g == 2, part[:, 1], both_z) if faces else both_z)
        v = jnp.concatenate([jnp.where(odd_lane, roll(halves[0], 1, 2), halves[0]),
                             jnp.where(odd_lane, halves[1], roll(halves[1], -1, 2))], axis=0)
        if faces:
            v = 0.25 * jnp.where(g == 0, pick(v, 2, 2), both(v, 2, 2))
        else:
            v = 0.125 * both(v, 2, 2)
        v = v.reshape(4, 4, 8, 128)
        out = v[:, 0]
        for u in range(1, 4):
            out = jnp.where(t == u, v[:, u], out)
        return out

    def z_gather(g, n, base):
        rows = pl.ds(pl.multiple_of((4 * k + base) * 8, 8), 32)
        return [remote(g.at[rows], g.at[rows], zg_send.at[n, u], zg_recv.at[n, u], gz=lax.rem(k + u, 8))
                for u in range(1, 8)]

    put(l3.up, 4 * k + 1, third(l2.up, True))
    third_faces = z_gather(l3.up, 0, 1)

    for copy in third_faces:
        copy.start()
    make_coefs(l2, 32)
    right_second_level.spread()
    for copy in rx:
        copy.start()
    for copy in third_faces:
        copy.wait_recv()
    make_coefs(l3, 32)

    group = lane // 32
    v = slots(l3.up, 1, 32, 8)
    v = jnp.where(group == 2, pick(v, 1, 2), both(v, 1, 2))
    v = jnp.where(group == 1, pick(v, 1, 1), both(v, 1, 1))
    fourth_coefs(l4, 0.25 * compact(jnp.where(group == 0, pick(v, 4, 2), both(v, 4, 2))))
    right_second_level.finish(l2.f, 0)
    edges1 = Wide(4, 4, l1.r, 0, 2)
    edges1.start()
    downward(l2)
    put(l3.f, 4 * k, third(l2.r))
    third_right = z_gather(l3.f, 1, 0)
    for copy in third_right:
        copy.start()

    edges1.finish()
    for copy in third_right:
        copy.wait_recv()

    downward(l3)

    v = slots(l3.r, 0, 32, 8) * slots(l3.root, 0, 32, 8)
    expand(l4.x, fourth_solve(l4, 0.125 * compact(both(both(both(v, 1, 2), 1, 1), 4, 2))))
    upward(l3, lambda i: l4.get(l4.x, i))

    for q in range(6):
        v = l3.x[pl.ds(pl.multiple_of(lax.rem(4 * k + q + 31, 32) * 8, 8), 8), :].reshape(1, 8, 128)
        for z in range(4):
            moved = v
            for u in range(4):
                if u != z:
                    moved = jnp.where(t == u, roll(v, u - z, 2), moved)
            first = (4 * q + z) * 16
            eb2[pl.ds(first, 8, stride=2), :] = moved.reshape(8, 128)
            eb2[pl.ds(first + 1, 8, stride=2), :] = moved.reshape(8, 128)

    def twice(ref, offset):
        def chunk(i):
            v = slots(ref, i * 4 + offset, 4)
            return jnp.broadcast_to(v[:, None], (4, 2, 16, 128)).reshape(8, 16, 128)

        return chunk

    def second_chunk(i):
        v = jnp.where(lane16 % 2 == 0, slots(eb2, i * 4, 4), slots(eb2, i * 4 + 12, 4))
        return jnp.broadcast_to(v[:, None], (4, 2, 16, 128)).reshape(8, 16, 128)

    upward(l2, second_chunk)

    for copy in rx:
        copy.wait_recv()
    for g in range(8):
        v = slots(l0.r, 4 + 8 * g, 8)
        own = v[:, :8]
        own = jnp.where(slot // 2 == 1, roll(rxr[0].reshape(8, 8, 128), 2 - 2 * g, 2), own)
        own = jnp.where(slot // 2 == 6, roll(rxr[1].reshape(8, 8, 128), 12 - 2 * g, 2), own)
        put(l0.r, 4 + 8 * g, jnp.concatenate([own, v[:, 8:]], axis=1))
    edges0 = Wide(5, 8, l0.r, 0, 2)
    edges0.start()

    for i, from_y in ((0, 0), (1, 1), (2, 2), (3, 3), (6, 14), (7, 15)):
        v = l2.x[pl.ds(lax.rem(2 * j + from_y, 16), 24, stride=16), :]
        low, high = jnp.where(lane2 % 2 == 0, v, roll(v, 1, 1)), jnp.where(lane2 % 2 == 1, v, roll(v, -1, 1))
        for d in range(2):
            eb1[pl.ds(2 * i + d, 24, stride=16), :] = low
            eb1[pl.ds(2 * i + d + 384, 24, stride=16), :] = high
    upward(l1, twice(eb1, 6))
    edges = Wide(6, 4, l1.x, 0, 2)
    edges.start()
    edges0.finish()
    edges.finish()

    source = lax.broadcasted_iota(jnp.int32, (128, 128), 0)
    target = lax.broadcasted_iota(jnp.int32, (128, 128), 1)
    hit = (source // 32 == (target % 64) // 16) & (source % 32 == 4 * b - 2 + (target % 16) // 2)
    v = slots(l1.x, 0, 72)
    v = jnp.where(sub < 6, v[:, :8], v[:, 8:]).reshape(576, 128)
    v = jnp.dot(v, jnp.where(hit, 1.0, 0.0).astype(F32), precision=HIGHEST, preferred_element_type=F32)
    eb0[pl.ds(0, 576, stride=2), :] = v
    eb0[pl.ds(1, 576, stride=2), :] = v

    def top_chunk(i):
        v = jnp.where(lane16 < 64, slots(eb0, i * 4 + 2, 4), slots(eb0, i * 4 + 34, 4))
        return jnp.broadcast_to(v[:, None], (4, 2, 16, 128)).reshape(8, 16, 128)

    upward(l0, top_chunk)

    for y in range(0, 8, 2):
        first = l0.x[pl.ds(64 + y, 64, stride=16), :]
        second = l0.x[pl.ds(65 + y, 64, stride=16), :]
        low = jnp.where(half_lane, first, pltpu.roll(second, 64, 1))
        high = jnp.where(half_lane, pltpu.roll(first, 64, 1), second)
        turned = pltpu.roll(jnp.concatenate([low, high], axis=0), 124, 1).T
        for d in range(2):
            for v in range(4):
                start = d * 64 + v * 16
                out_ref[pl.ds(v * 64 + y + d, 8, stride=8), :] = turned[start:start + 8]

    for copy in (strips[4:] + [faces_first, right_first] + faces_early + right_early + faces_second + right_second + rx
                 + third_faces + third_right):
        copy.wait_send()
    faces_second_level.wait_send()
    right_second_level.wait_send()


def solution(mesh):
    def per_device(right_side, affinity):
        nx = affinity.shape[1] * mesh.shape["gx"]
        ny = affinity.shape[2] * mesh.shape["gy"]
        nz = affinity.shape[3] * mesh.shape["gz"]
        scratch = []
        for z, rows, *_ in LEVELS:
            scratch += level_shapes(z, rows)
        scratch += [pltpu.VMEM(shape, F32) for shape in (
            (4, 16, 8, 128), (4, 16, 8, 128),
            (7, 2, 4, 64, 128), (7, 2, 4, 64, 128), (7, 2, 32, 128), (7, 2, 3, 32, 128),
            (256, 128), (512, 128), (8, 32, 128), (8, 32, 128), (2, 64, 128), (2, 64, 128),
            (8, 128), (8, 128), (4, 8, 8, 128), (4, 8, 8, 128), (2, 8, 8, 128), (2, 8, 8, 128), (384, 128), (768, 128), (1152, 128))]
        dma = pltpu.SemaphoreType.DMA
        scratch += [dma(shape) for shape in (
            (2,), (6,), (6,), (7, 8), (7, 8), (2, 7), (2, 7), (2,), (2,), (2, 2, 4), (2, 2), (2, 8), (2, 8), (2, 4), (2, 4), (2, 8), (2, 8))]
        out = pl.pallas_call(
            functools.partial(kernel, nx, ny, nz),
            out_shape=jax.ShapeDtypeStruct((256, 128), F32),
            in_specs=[pl.BlockSpec(memory_space=pl.ANY)] * 2,
            out_specs=pl.BlockSpec(memory_space=pltpu.VMEM),
            scratch_shapes=scratch,
            compiler_params=pltpu.CompilerParams(
                collective_id=0, has_side_effects=True, vmem_limit_bytes=60 * 1024 * 1024),
        )(right_side, affinity)
        return out.reshape(right_side.shape)

    spec = P(None, "gx", "gy", "gz")
    return jax.shard_map(per_device, mesh=mesh, in_specs=(spec, spec), out_specs=spec, check_vma=False)
```
